128 devices in a mesh: lat: 8 (over x, y_lo), ord: 16 (over y_hi, z, core).
Axes of the slice: x: 4, y: 4 (y_hi: 2, y_lo: 2; y = y_hi * 2 + y_lo), z: 4, core: 2. Of those that a mesh axis runs over, the one named last changes fastest.
Arguments:
- heights: bfloat16 [2048, 43200], P(('lat', 'ord')), may hold values from -1.5 to 1.5
- panels: bfloat16 [2048, 5120, 128], P('lat', 'ord'), may hold values from -0.125 to 0.125
- ord_slot: int32 [5120], replicated, may hold values from 0 to 5119, each once
- cutoffs: int32 [5120], P('ord'), may hold values from 13360 to 21599
Outputs:
- gravity: float32 [2048, 43200], P(('lat', 'ord'))
The draws below stay inside these ranges and needn't reach their ends.
Inputs may be any that keep to these rules, and one draw needn't show every extreme that they name: `ord_slot`: a permutation of the order slots.
All inputs are finite; a program needn't handle non-finite values.
Results may differ from the reference program's by a relative error of at most 0.0039.
Values may be sent and summed in bfloat16 or wider, within the bound.
A program may use at most 192 MiB of HBM per device.

```python
import math
import jax
import jax.numpy as jnp
from jax import lax

ORDERS = 5120
DEG = 128
NMAX = 21600
LON = 43200
CYCLES = 2048


def with_ends(result, stream_key, low, largest):
    dims = result.shape
    place = [jax.random.randint(jax.random.fold_in(stream_key, axis), (), 0, dims[axis]) for axis in range(len(dims))]
    result = result.at[tuple(place)].set(low)
    longest = dims.index(max(dims))
    place[longest] = (place[longest] + 1) % dims[longest]
    return result.at[tuple(place)].set(largest)


def block_levels(key, shape, shards, low, top_value):
    def one(position, blocks):
        draws = jax.random.uniform(jax.random.fold_in(jax.random.fold_in(key, 6), position), (blocks,), jnp.float32, low / len(shards), top_value / len(shards))
        return jnp.repeat(jnp.exp(draws), shape[position] // blocks).reshape((-1,) + (1,) * (len(shape) - position - 1))

    loudness = one(*shards[0])
    for cut in shards[1:]:
        loudness = loudness * one(*cut)
    return loudness


def bell_draw(rng, dims, spread, most, shards=(), held_as=jnp.bfloat16):
    drawn = spread * jax.random.normal(rng, dims, jnp.float32)
    if shards:
        drawn = drawn * block_levels(rng, dims, shards, -0.22, 0.18)
    return jnp.clip(drawn, -most, most).astype(held_as)


def setup_inputs(seed: int = 0) -> dict:
    streams_of = jax.random.split(jax.random.key(seed), 5)
    return {
        "heights": jnp.clip(jax.random.uniform(streams_of[0], (CYCLES, LON), jnp.float32, -1.5, 1.5) * block_levels(streams_of[0], (CYCLES, LON), ((0, 128),), -0.4, 0.0), -1.5, 1.5).astype(jnp.bfloat16),
        "panels": bell_draw(streams_of[1], (CYCLES, ORDERS, DEG), CYCLES ** -0.5, 0.125, ((0, 8), (1, 16))),
        "ord_slot": jax.random.permutation(streams_of[2], ORDERS).astype(jnp.int32),
        "cutoffs": with_ends(jax.random.randint(streams_of[3], (ORDERS,), (NMAX + ORDERS) // 2, NMAX), jax.random.fold_in(streams_of[3], 1), (NMAX + ORDERS) // 2, NMAX - 1).astype(jnp.int32),
    }


def reference(heights, panels, ord_slot, cutoffs):
    level = heights.astype(jnp.float32)
    cycles = level.shape[0]
    scale_in = 1.0 / math.sqrt(LON)
    pieces = []
    value = level
    for power in range(3):
        if power > 0:
            value = value * level
        spectrum = jnp.fft.rfft(value, axis=1)[:, 1:ORDERS + 1] * scale_in
        pieces.append(jnp.real(spectrum)[:, ord_slot])
        pieces.append(jnp.imag(spectrum)[:, ord_slot])
    picked = jnp.stack(pieces).astype(jnp.bfloat16)
    picked = lax.optimization_barrier(picked)
    stride = (NMAX - ORDERS) // DEG
    degree_int = (ORDERS + jnp.arange(DEG, dtype=jnp.int32) * stride).astype(jnp.int32)
    degree = degree_int.astype(jnp.float32)
    factors = jnp.stack([jnp.ones_like(degree), (degree + 2.0) / (2.0 * NMAX), (degree + 2.0) * (degree + 1.0) / (6.0 * NMAX * NMAX)])
    block = math.gcd(ORDERS, 256)

    def one_block(index):
        start = (index * block).astype(jnp.int32)
        panel = lax.dynamic_slice_in_dim(panels, start, block, 1).astype(jnp.float32)
        spectra = lax.dynamic_slice_in_dim(picked, start, block, 2).astype(jnp.float32)
        limits = lax.dynamic_slice_in_dim(cutoffs, start, block, 0)
        sums = jnp.einsum('xrk,rkn->xkn', spectra, panel)
        folded = lax.optimization_barrier(jnp.sum(sums.reshape(3, 2, block, DEG) * factors[:, None, None, :], axis=0))
        keep = (degree_int[None, :] <= limits[:, None]).astype(jnp.float32)
        coeffs = (folded * keep).astype(jnp.bfloat16)
        coeffs = lax.optimization_barrier(coeffs).astype(jnp.float32)
        return jnp.einsum('rkn,ckn->crk', panel, coeffs)
    outputs = lax.map(one_block, jnp.arange(ORDERS // block, dtype=jnp.int32))
    synthesis = outputs.transpose(1, 2, 0, 3).reshape(2, cycles, ORDERS)
    half = LON // 2 + 1
    target = (ord_slot + 1).astype(jnp.int32)
    full_real = jnp.zeros((cycles, half), synthesis.dtype).at[:, target].set(synthesis[0])
    full_imag = jnp.zeros((cycles, half), synthesis.dtype).at[:, target].set(synthesis[1])
    field = jnp.fft.irfft(full_real + 1j * full_imag, n=LON, axis=1) * (LON / 2.0)
    return field * math.sqrt(CYCLES / (DEG * ORDERS))
```

```python
import functools
import math

import jax
import jax.numpy as jnp
import numpy as np
from jax import lax
from jax.experimental import pallas as pl
from jax.experimental.pallas import tpu as pltpu
from jax.sharding import PartitionSpec as P

LON = 43200
SLOW = 180
FAST = 240
HALF = 96
ORDERS = 5120
DEG = 128
NMAX = 21600
CYC = 16
TROWS = 6016
F32 = jnp.float32
BF16 = jnp.bfloat16
MIB = 1024 * 1024


def split16(table):
    high = table.astype(np.float32).astype(jnp.bfloat16)
    low = (table - high.astype(np.float64)).astype(np.float32).astype(jnp.bfloat16)
    return high, low


def angles(left, right, total):
    return 2.0 * np.pi / total * ((left[:, None] * right[None, :]) % total)


@functools.cache
def tables():
    k = np.arange(91)
    a = np.arange(SLOW)
    b = np.arange(FAST)
    q = np.arange(29)
    ka = angles(k, a, SLOW)
    first = np.zeros((2, HALF, 192))
    first[0, :91, :SLOW] = np.cos(ka)
    first[1, :91, :SLOW] = -np.sin(ka)
    first = first.reshape(2 * HALF, 192)
    kb = angles(k, b, LON)
    twist = np.zeros((2, HALF, 256), np.float32)
    twist[0, :91, :FAST] = np.cos(kb)
    twist[1, :91, :FAST] = np.sin(kb)
    bq = angles(b, q, FAST)
    bq1 = angles(b, q + 1, FAST)
    second = np.zeros((2, 256, 2, 128))
    second[0, :FAST, 0, 0:29] = np.cos(bq)
    second[1, :FAST, 0, 0:29] = np.sin(bq)
    second[0, :FAST, 1, 0:29] = -np.sin(bq)
    second[1, :FAST, 1, 0:29] = np.cos(bq)
    second[0, :FAST, 0, 32:61] = np.cos(bq1)
    second[1, :FAST, 0, 32:61] = -np.sin(bq1)
    second[0, :FAST, 1, 32:61] = -np.sin(bq1)
    second[1, :FAST, 1, 32:61] = -np.cos(bq1)
    second = second.reshape(512, 256) / math.sqrt(LON)
    back = np.zeros((2, 2, 32, 2, 256))
    back[0, 0, :29, 0, :FAST] = np.cos(bq).T
    back[0, 0, :29, 1, :FAST] = np.sin(bq).T
    back[1, 0, :29, 0, :FAST] = -np.sin(bq).T
    back[1, 0, :29, 1, :FAST] = np.cos(bq).T
    back[0, 1, :29, 0, :FAST] = np.cos(bq1).T
    back[0, 1, :29, 1, :FAST] = -np.sin(bq1).T
    back[1, 1, :29, 0, :FAST] = -np.sin(bq1).T
    back[1, 1, :29, 1, :FAST] = -np.cos(bq1).T
    back = np.concatenate(split16(back.reshape(128, 512)), 0)
    last = np.zeros((192, 2, HALF))
    last[:SLOW, 0, :91] = np.cos(ka).T
    last[:SLOW, 1, :91] = -np.sin(ka).T
    last = last.reshape(192, 2 * HALF) * math.sqrt(2048 / (DEG * ORDERS))
    rows = np.arange(128)
    lanes = np.arange(256)
    diag = (lanes[None, :] % 16 == rows[:, None] // 8).astype(jnp.bfloat16)
    pick = (lanes[None, :] % 16 == np.arange(32)[:, None] % 16).astype(np.float32)
    return dict(
        first=split16(first), twist=twist, second=split16(second), back=back,
        last=split16(last), diag=diag, pick=pick,
    )


def swap_chunks(rows):
    rows = list(rows)
    chunk = lax.broadcasted_iota(jnp.int32, (8, 128), 1) // 16
    for d in (4, 2, 1):
        low = (chunk & d) == 0
        new = list(rows)
        for r in range(8):
            if r & d:
                continue
            new[r] = jnp.where(low, rows[r], pltpu.roll(rows[r + d], d * 16, 1))
            new[r + d] = jnp.where(low, pltpu.roll(rows[r], 128 - d * 16, 1), rows[r + d])
        rows = new
    return rows


def dot(left, right):
    return jnp.dot(left, right, preferred_element_type=F32)


def halves(value):
    high = value.astype(BF16)
    return high, (value - high.astype(F32)).astype(BF16)


def forward_kernel(slot_ref, x_ref, fh_ref, fl_ref, twist_ref, sh_ref, sl_ref, out_ref,
                   xs, qs, ts, gs):
    keep = lax.broadcasted_iota(jnp.int32, (CYC, 256), 1) < FAST
    for r in range(CYC):
        for lane in range(2):
            xs[lane, r * 192 + 176 : r * 192 + 192, :] = jnp.zeros((16, 128), F32)
    for a in range(SLOW):
        start = FAST * a // 128 * 128
        off = FAST * a - start
        if start + 384 <= LON:
            v = x_ref[:, start : start + 384].astype(F32)
        else:
            v = jnp.concatenate(
                [x_ref[:, start:LON].astype(F32), jnp.zeros((CYC, start + 384 - LON), F32)], 1
            )
        if off:
            v = pltpu.roll(v, 384 - off, 1)
        v = jnp.where(keep, v[:, :256], 0.0)
        for lane in range(2):
            xs.at[lane][pl.ds(a, CYC, stride=192), :] = v[:, lane * 128 : lane * 128 + 128]

    def one_cycle(r, carry):
        rows = pl.ds(pl.multiple_of(r * 192, 192), 192)
        level = jnp.concatenate([xs[0, rows, :], xs[1, rows, :]], 1)
        value = level
        for p in range(3):
            if p:
                value = value * level
            if p == 0:
                high = value.astype(BF16)
                y = dot(fh_ref[...], high) + dot(fl_ref[...], high)
            else:
                high, low = halves(value)
                y = dot(fh_ref[...], high) + dot(fl_ref[...], high) + dot(fh_ref[...], low)
            re, im = y[:HALF], y[HALF:]
            c, s = twist_ref[0], twist_ref[1]
            z = jnp.concatenate([re * c + im * s, im * c - re * s], 1)
            zh, zl = halves(z)
            o = dot(zh, sh_ref[...]) + dot(zh, sl_ref[...]) + dot(zl, sh_ref[...])
            qs[pl.ds(r * 8 + p, HALF, stride=128), :] = o[:, :128]
            qs[pl.ds(r * 8 + 3 + p, HALF, stride=128), :] = o[:, 128:]
        for x in (6, 7):
            qs[pl.ds(r * 8 + x, HALF, stride=128), :] = jnp.zeros((HALF, 128), F32)
        return carry

    lax.fori_loop(0, CYC, one_cycle, 0)

    def one_k(k, carry):
        t = qs[pl.ds(pl.multiple_of(k * 128, 128), 128), :].T
        ts[pl.ds(k, 32, stride=SLOW), :] = t[0:32]
        ts[pl.ds(SLOW - k, 32, stride=SLOW), :] = t[32:64]
        return carry

    lax.fori_loop(0, 91, one_k, 0)

    def one_tile(tile, carry):
        for i in range(128):
            gs[i : i + 1, :] = ts[pl.ds(slot_ref[tile * 128 + i] + 1, 1), :]
        t = gs[...].T
        sides = []
        for h in range(2):
            sides.append(
                jnp.concatenate(swap_chunks([t[(h * 8 + r) * 8 : (h * 8 + r + 1) * 8] for r in range(8)]), 0)
            )
        out_ref[pl.ds(pl.multiple_of(tile * 64, 64), 64), :] = jnp.concatenate(sides, 1).astype(BF16)
        return carry

    lax.fori_loop(0, ORDERS // 128, one_tile, 0)


def vmem():
    return pl.BlockSpec(memory_space=pltpu.VMEM)


def forward(heights, slots):
    t = tables()
    return pl.pallas_call(
        forward_kernel,
        out_shape=jax.ShapeDtypeStruct((ORDERS // 2, 256), BF16),
        in_specs=[pl.BlockSpec(memory_space=pltpu.SMEM)] + [vmem()] * 6,
        out_specs=vmem(),
        scratch_shapes=[
            pltpu.VMEM((2, CYC * 192, 128), F32),
            pltpu.VMEM((HALF * 128, 128), F32),
            pltpu.VMEM((TROWS, 128), F32),
            pltpu.VMEM((128, 128), F32),
        ],
        compiler_params=pltpu.CompilerParams(vmem_limit_bytes=48 * MIB),
        name="forward",
    )(slots, heights, *t["first"], t["twist"], *t["second"])


def analysis_kernel(msg_ref, panel_ref, diag_ref, factor_ref, out_ref):
    step = pl.program_id(0)
    for pair in range(2):
        accs = [None, None]
        for R in range(16):
            both = msg_ref[pl.ds(pl.multiple_of(R * 160 + step * 32 + pair * 16, 16), 16), :]
            both = both.astype(F32)
            for e in range(2):
                one = both[e * 8 : e * 8 + 8]
                two = jnp.concatenate([one, one], 0).astype(BF16)
                left = jnp.concatenate([two] * 8, 0) * diag_ref[...]
                g = pair * 2 + e
                right = panel_ref[R * 16 : R * 16 + 16, g * 16 : g * 16 + 16, :].reshape(256, DEG)
                d = dot(left, right)
                accs[e] = d if accs[e] is None else accs[e] + d
        for e in range(2):
            g = pair * 2 + e
            acc = accs[e].reshape(16, 8, DEG)
            for c in range(2):
                out_ref[c, g * 16 : g * 16 + 16, :] = jnp.sum(acc * factor_ref[c][None], axis=1)


def analysis(msg, panels, factors):
    t = tables()
    return pl.pallas_call(
        analysis_kernel,
        grid=(5,),
        out_shape=jax.ShapeDtypeStruct((2, 320, DEG), F32),
        in_specs=[
            pl.BlockSpec((ORDERS // 2, 256), lambda i: (0, 0)),
            pl.BlockSpec((256, 64, DEG), lambda i: (0, i, 0)),
            pl.BlockSpec((128, 256), lambda i: (0, 0)),
            pl.BlockSpec((2, 8, DEG), lambda i: (0, 0, 0)),
        ],
        out_specs=pl.BlockSpec((2, 64, DEG), lambda i: (0, i, 0)),
        compiler_params=pltpu.CompilerParams(vmem_limit_bytes=48 * MIB),
        name="analysis",
    )(msg, panels, t["diag"], factors)


def synthesis_kernel(coeff_ref, panel_ref, pick_ref, out_ref):
    for g in range(4):
        left = jnp.concatenate([coeff_ref[c, g * 16 : g * 16 + 16, :] for c in range(2)], 0)
        for R in range(16):
            right = panel_ref[R * 16 : R * 16 + 16, g * 16 : g * 16 + 16, :].reshape(256, DEG)
            d = lax.dot_general(left, right, (((1,), (1,)), ((), ())), preferred_element_type=F32)
            d = d * pick_ref[...]
            out_ref[R, g * 2 : g * 2 + 1, :] = jnp.sum(d[:16], axis=0, keepdims=True)
            out_ref[R, g * 2 + 1 : g * 2 + 2, :] = jnp.sum(d[16:], axis=0, keepdims=True)


def synthesize(coeffs, panels):
    t = tables()
    return pl.pallas_call(
        synthesis_kernel,
        grid=(5,),
        out_shape=jax.ShapeDtypeStruct((16, 40, 256), F32),
        in_specs=[
            pl.BlockSpec((2, 64, DEG), lambda i: (0, i, 0)),
            pl.BlockSpec((256, 64, DEG), lambda i: (0, i, 0)),
            pl.BlockSpec((32, 256), lambda i: (0, 0)),
        ],
        out_specs=pl.BlockSpec((16, 8, 256), lambda i: (0, i, 0)),
        compiler_params=pltpu.CompilerParams(vmem_limit_bytes=48 * MIB),
        name="synthesis",
    )(coeffs, panels, t["pick"])


def inverse_kernel(slot_ref, msg_ref, back_ref, twist_ref, lh_ref, ll_ref, out_ref, ts, ls, ys):
    ts[0:8, :] = jnp.zeros((8, 128), F32)
    ts[ORDERS:TROWS, :] = jnp.zeros((TROWS - ORDERS, 128), F32)

    def one_peer(o, carry):
        for part in range(3):
            rows = msg_ref[pl.ds(pl.multiple_of(o * 48 + part * 16, 16), 16), :].astype(F32)
            count = 128 if part < 2 else 64
            blocks = []
            for h in range(2):
                side = rows[:, h * 128 : h * 128 + 128]
                groups = []
                for g in range(8):
                    v = side[g // 4 * 8 : g // 4 * 8 + 8]
                    if g % 4:
                        v = pltpu.roll(v, 8 - 2 * (g % 4), 0)
                    groups.append(v)
                blocks += swap_chunks(groups)
            t = jnp.concatenate(blocks, 0).T
            base = o * 320 + part * 128
            for i in range(count):
                ts[pl.ds(slot_ref[base + i] + 1, 1), :] = t[i : i + 1]
        return carry

    lax.fori_loop(0, 16, one_peer, 0)

    def one_k(k, carry):
        plus = ts[pl.ds(k, 32, stride=SLOW), :]
        minus = ts[pl.ds(SLOW - k, 32, stride=SLOW), :]
        minus = jnp.where(jnp.logical_and(k > 0, k < 90), minus, 0.0)
        both = jnp.concatenate([plus, minus, jnp.zeros((64, 128), F32)], 0)
        ls[pl.ds(k, 128, stride=HALF), :] = both.T
        return carry

    lax.fori_loop(0, HALF, one_k, 0)

    def one_cycle(r, carry):
        parts = []
        for c in range(2):
            parts.append(ls[pl.ds(pl.multiple_of((r * 8 + c) * HALF, HALF), HALF), :][:, :64])
        left = jnp.concatenate(parts, 1).astype(BF16)
        w = dot(jnp.concatenate([left, left], 1), back_ref[...])
        re, im = w[:, :256], w[:, 256:]
        c, s = twist_ref[0], twist_ref[1]
        v = jnp.concatenate([re * c - im * s, im * c + re * s], 0).astype(BF16)
        field = dot(lh_ref[...], v) + dot(ll_ref[...], v)
        for lane in range(2):
            ys[lane, pl.ds(pl.multiple_of(r * 192, 192), 192), :] = field[:, lane * 128 : lane * 128 + 128]
        return carry

    lax.fori_loop(0, CYC, one_cycle, 0)
    for a in range(SLOW):
        v = jnp.concatenate([ys.at[lane][pl.ds(a, CYC, stride=192), :] for lane in range(2)], 1)
        out_ref[:, FAST * a : FAST * a + FAST] = v[:, :FAST]


def inverse(msg, slots):
    t = tables()
    return pl.pallas_call(
        inverse_kernel,
        out_shape=jax.ShapeDtypeStruct((CYC, LON), F32),
        in_specs=[pl.BlockSpec(memory_space=pltpu.SMEM)] + [vmem()] * 5,
        out_specs=vmem(),
        scratch_shapes=[
            pltpu.VMEM((TROWS, 128), F32),
            pltpu.VMEM((128 * HALF, 128), F32),
            pltpu.VMEM((2, CYC * 192, 128), F32),
        ],
        compiler_params=pltpu.CompilerParams(vmem_limit_bytes=48 * MIB),
        name="inverse",
    )(slots, msg, t["back"], t["twist"], *t["last"])


def degrees():
    stride = (NMAX - ORDERS) // DEG
    return ORDERS + np.arange(DEG, dtype=np.int32) * stride


def factor_rows():
    degree = degrees().astype(np.float64)
    rows = np.zeros((2, 8, DEG), np.float32)
    for c in range(2):
        rows[c, 3 * c] = 1.0
        rows[c, 3 * c + 1] = (degree + 2.0) / (2.0 * NMAX)
        rows[c, 3 * c + 2] = (degree + 2.0) * (degree + 1.0) / (6.0 * NMAX * NMAX)
    return rows


def local(heights, panels, ord_slot, cutoffs):
    msg = forward(heights, ord_slot)
    got = lax.all_to_all(msg, "ord", split_axis=0, concat_axis=0, tiled=True)
    folded = lax.psum(analysis(got, panels, factor_rows()), "lat")
    keep = (degrees()[None, :] <= cutoffs[:, None]).astype(F32)
    coeffs = (folded * keep[None]).astype(BF16)
    synth = synthesize(coeffs, panels)
    synth = jnp.pad(synth.astype(BF16), ((0, 0), (0, 8), (0, 0))).reshape(16 * 48, 256)
    back = lax.all_to_all(synth, "ord", split_axis=0, concat_axis=0, tiled=True)
    return inverse(back, ord_slot)


def solution(mesh):
    return jax.shard_map(
        local,
        mesh=mesh,
        in_specs=(P(("lat", "ord"), None), P("lat", "ord", None), P(), P("ord")),
        out_specs=P(("lat", "ord"), None),
        check_vma=False,
    )
```

```python
import functools
import math

import jax
import jax.numpy as jnp
import numpy as np
from jax import lax
from jax.experimental import pallas as pl
from jax.experimental.pallas import tpu as pltpu
from jax.sharding import PartitionSpec as P

LON = 43200
SLOW = 180
FAST = 240
HALF = 96
ORDERS = 5120
DEG = 128
NMAX = 21600
CYC = 16
TROWS = 6016
F32 = jnp.float32
BF16 = jnp.bfloat16
MIB = 1024 * 1024


def split16(table):
    high = table.astype(np.float32).astype(jnp.bfloat16)
    low = (table - high.astype(np.float64)).astype(np.float32).astype(jnp.bfloat16)
    return high, low


def angles(left, right, total):
    return 2.0 * np.pi / total * ((left[:, None] * right[None, :]) % total)


@functools.cache
def tables():
    k = np.arange(91)
    a = np.arange(SLOW)
    b = np.arange(FAST)
    q = np.arange(29)
    ka = angles(k, a, SLOW)
    first = np.zeros((2, HALF, 192))
    first[0, :91, :SLOW] = np.cos(ka)
    first[1, :91, :SLOW] = -np.sin(ka)
    first = first.reshape(2 * HALF, 192)
    kb = angles(k, b, LON)
    twist = np.zeros((2, HALF, 256), np.float32)
    twist[0, :91, :FAST] = np.cos(kb)
    twist[1, :91, :FAST] = np.sin(kb)
    bq = angles(b, q, FAST)
    bq1 = angles(b, q + 1, FAST)
    second = np.zeros((2, 256, 2, 128))
    second[0, :FAST, 0, 0:29] = np.cos(bq)
    second[1, :FAST, 0, 0:29] = np.sin(bq)
    second[0, :FAST, 1, 0:29] = -np.sin(bq)
    second[1, :FAST, 1, 0:29] = np.cos(bq)
    second[0, :FAST, 0, 32:61] = np.cos(bq1)
    second[1, :FAST, 0, 32:61] = -np.sin(bq1)
    second[0, :FAST, 1, 32:61] = -np.sin(bq1)
    second[1, :FAST, 1, 32:61] = -np.cos(bq1)
    second = second.reshape(512, 256) / math.sqrt(LON)
    back = np.zeros((2, 2, 32, 2, 256))
    back[0, 0, :29, 0, :FAST] = np.cos(bq).T
    back[0, 0, :29, 1, :FAST] = np.sin(bq).T
    back[1, 0, :29, 0, :FAST] = -np.sin(bq).T
    back[1, 0, :29, 1, :FAST] = np.cos(bq).T
    back[0, 1, :29, 0, :FAST] = np.cos(bq1).T
    back[0, 1, :29, 1, :FAST] = -np.sin(bq1).T
    back[1, 1, :29, 0, :FAST] = -np.sin(bq1).T
    back[1, 1, :29, 1, :FAST] = -np.cos(bq1).T
    back = np.concatenate(split16(back.reshape(128, 512)), 0)
    last = np.zeros((192, 2, HALF))
    last[:SLOW, 0, :91] = np.cos(ka).T
    last[:SLOW, 1, :91] = -np.sin(ka).T
    last = last.reshape(192, 2 * HALF) * math.sqrt(2048 / (DEG * ORDERS))
    rows = np.arange(128)
    lanes = np.arange(256)
    diag = (lanes[None, :] % 16 == rows[:, None] // 8).astype(jnp.bfloat16)
    pick = (lanes[None, :] % 16 == np.arange(32)[:, None] % 16).astype(np.float32)
    return dict(
        first=split16(first), twist=twist, second=split16(second), back=back,
        last=split16(last), diag=diag, pick=pick,
    )


def swap_chunks(rows):
    rows = list(rows)
    chunk = lax.broadcasted_iota(jnp.int32, (8, 128), 1) // 16
    for d in (4, 2, 1):
        low = (chunk & d) == 0
        new = list(rows)
        for r in range(8):
            if r & d:
                continue
            new[r] = jnp.where(low, rows[r], pltpu.roll(rows[r + d], d * 16, 1))
            new[r + d] = jnp.where(low, pltpu.roll(rows[r], 128 - d * 16, 1), rows[r + d])
        rows = new
    return rows


def dot(left, right):
    return jnp.dot(left, right, preferred_element_type=F32)


def halves(value):
    high = value.astype(BF16)
    return high, (value - high.astype(F32)).astype(BF16)


def forward_kernel(slot_ref, x_ref, fh_ref, fl_ref, twist_ref, sh_ref, sl_ref, out_ref,
                   xs, qs, ts, gs):
    keep = lax.broadcasted_iota(jnp.int32, (CYC, 256), 1) < FAST
    for r in range(CYC):
        for lane in range(2):
            xs[lane, r * 192 + 176 : r * 192 + 192, :] = jnp.zeros((16, 128), F32)
    for a in range(SLOW):
        start = FAST * a // 128 * 128
        off = FAST * a - start
        if start + 384 <= LON:
            v = x_ref[:, start : start + 384].astype(F32)
        else:
            v = jnp.concatenate(
                [x_ref[:, start:LON].astype(F32), jnp.zeros((CYC, start + 384 - LON), F32)], 1
            )
        if off:
            v = pltpu.roll(v, 384 - off, 1)
        v = jnp.where(keep, v[:, :256], 0.0)
        for lane in range(2):
            xs.at[lane][pl.ds(a, CYC, stride=192), :] = v[:, lane * 128 : lane * 128 + 128]

    def one_cycle(r, carry):
        rows = pl.ds(pl.multiple_of(r * 192, 192), 192)
        level = jnp.concatenate([xs[0, rows, :], xs[1, rows, :]], 1)
        value = level
        for p in range(3):
            if p:
                value = value * level
            if p == 0:
                high = value.astype(BF16)
                y = dot(fh_ref[...], high) + dot(fl_ref[...], high)
            else:
                high, low = halves(value)
                y = dot(fh_ref[...], high) + dot(fl_ref[...], high) + dot(fh_ref[...], low)
            re, im = y[:HALF], y[HALF:]
            c, s = twist_ref[0], twist_ref[1]
            z = jnp.concatenate([re * c + im * s, im * c - re * s], 1)
            zh, zl = halves(z)
            o = dot(zh, sh_ref[...]) + dot(zh, sl_ref[...]) + dot(zl, sh_ref[...])
            qs[pl.ds(r * 8 + p, HALF, stride=128), :] = o[:, :128]
            qs[pl.ds(r * 8 + 3 + p, HALF, stride=128), :] = o[:, 128:]
        for x in (6, 7):
            qs[pl.ds(r * 8 + x, HALF, stride=128), :] = jnp.zeros((HALF, 128), F32)
        return carry

    lax.fori_loop(0, CYC, one_cycle, 0)

    def one_k(k, carry):
        t = qs[pl.ds(pl.multiple_of(k * 128, 128), 128), :].T
        ts[pl.ds(k, 32, stride=SLOW), :] = t[0:32]
        ts[pl.ds(SLOW - k, 32, stride=SLOW), :] = t[32:64]
        return carry

    lax.fori_loop(0, 91, one_k, 0)

    def one_tile(tile, carry):
        for i in range(128):
            gs[i : i + 1, :] = ts[pl.ds(slot_ref[tile * 128 + i] + 1, 1), :]
        t = gs[...].T
        sides = []
        for h in range(2):
            sides.append(
                jnp.concatenate(swap_chunks([t[(h * 8 + r) * 8 : (h * 8 + r + 1) * 8] for r in range(8)]), 0)
            )
        out_ref[pl.ds(pl.multiple_of(tile * 64, 64), 64), :] = jnp.concatenate(sides, 1).astype(BF16)
        return carry

    lax.fori_loop(0, ORDERS // 128, one_tile, 0)


def vmem():
    return pl.BlockSpec(memory_space=pltpu.VMEM)


def forward(heights, slots):
    t = tables()
    return pl.pallas_call(
        forward_kernel,
        out_shape=jax.ShapeDtypeStruct((ORDERS // 2, 256), BF16),
        in_specs=[pl.BlockSpec(memory_space=pltpu.SMEM)] + [vmem()] * 6,
        out_specs=vmem(),
        scratch_shapes=[
            pltpu.VMEM((2, CYC * 192, 128), F32),
            pltpu.VMEM((HALF * 128, 128), F32),
            pltpu.VMEM((TROWS, 128), F32),
            pltpu.VMEM((128, 128), F32),
        ],
        compiler_params=pltpu.CompilerParams(vmem_limit_bytes=48 * MIB),
        name="forward",
    )(slots, heights, *t["first"], t["twist"], *t["second"])


MESH = pl.DeviceIdType.MESH
ROWS_IN = 160
ROWS_OUT = 48
SLAB = 80


def middle_kernel(msg_ref, panel_ref, keep_ref, diag_ref, factor_ref, pick_ref, out_ref,
                  pan, got, acc, mine, parts, coeff, syn,
                  psem, s1, r1, s2, r2, s3, r3, s4, r4):
    lat = lax.axis_index("lat")
    me = lax.axis_index("ord")
    hy, hz, hc = me // 8, me // 2 % 4, me % 2

    def ahead(d):
        return (hy + d // 8) % 2 * 8 + (hz + d // 2 % 4) % 4 * 2 + (hc + d % 2) % 2

    def behind(d):
        return (hy + 2 - d // 8) % 2 * 8 + (hz + 4 - d // 2 % 4) % 4 * 2 + (hc + 2 - d % 2) % 2

    def panel_copy(d):
        place = pl.ds(pl.multiple_of(behind(d) * 16, 16), 16)
        return pltpu.make_async_copy(panel_ref.at[place], pan.at[place], psem.at[d])

    def in_copy(d):
        return pltpu.make_async_remote_copy(
            src_ref=msg_ref.at[pl.ds(pl.multiple_of(ahead(d) * ROWS_IN, 16), ROWS_IN)],
            dst_ref=got.at[pl.ds(pl.multiple_of(me * ROWS_IN, 16), ROWS_IN)],
            send_sem=s1.at[d], recv_sem=r1.at[d],
            device_id=(lat, ahead(d)), device_id_type=MESH,
        )

    def slab_copy(d):
        peer = (lat + d) % 8
        return pltpu.make_async_remote_copy(
            src_ref=mine.at[pl.ds(pl.multiple_of(peer * SLAB, 16), SLAB)],
            dst_ref=parts.at[pl.ds(pl.multiple_of(lat * SLAB, 16), SLAB)],
            send_sem=s2.at[d], recv_sem=r2.at[d],
            device_id=(peer, me), device_id_type=MESH,
        )

    def coeff_copy(d):
        peer = (lat + d) % 8
        place = pl.ds(pl.multiple_of(lat * SLAB, 16), SLAB)
        return pltpu.make_async_remote_copy(
            src_ref=coeff.at[place], dst_ref=coeff.at[place],
            send_sem=s3.at[d], recv_sem=r3.at[d],
            device_id=(peer, me), device_id_type=MESH,
        )

    def out_copy(d):
        return pltpu.make_async_remote_copy(
            src_ref=syn.at[pl.ds(pl.multiple_of(ahead(d) * ROWS_OUT, 16), ROWS_OUT)],
            dst_ref=out_ref.at[pl.ds(pl.multiple_of(me * ROWS_OUT, 16), ROWS_OUT)],
            send_sem=s4.at[d], recv_sem=r4.at[d],
            device_id=(lat, ahead(d)), device_id_type=MESH,
        )

    def loop(low, high, body):
        def step(d, carry):
            body(d)
            return carry
        lax.fori_loop(low, high, step, 0)

    loop(0, 16, lambda d: panel_copy(d).start())
    barrier = pltpu.get_barrier_semaphore()
    loop(1, 16, lambda d: pl.semaphore_signal(barrier, inc=1, device_id=(lat, ahead(d)), device_id_type=MESH))
    loop(1, 8, lambda d: pl.semaphore_signal(barrier, inc=1, device_id=((lat + d) % 8, me), device_id_type=MESH))
    pl.semaphore_wait(barrier, 22)
    loop(1, 16, lambda d: in_copy(d).start())

    def analyse(ref, peer, fresh):
        def pair(i):
            both = ref[pl.ds(pl.multiple_of(peer * ROWS_IN + i * 16, 16), 16), :].astype(F32)
            for e in range(2):
                one = both[e * 8 : e * 8 + 8]
                two = jnp.concatenate([one, one], 0).astype(BF16)
                left = jnp.concatenate([two] * 8, 0) * diag_ref[...]
                right = pan[
                    pl.ds(pl.multiple_of(peer * 16, 16), 16),
                    pl.ds(pl.multiple_of(i * 32 + e * 16, 16), 16), :
                ].reshape(256, DEG)
                place = pl.ds(pl.multiple_of(i * 256 + e * 128, 128), 128)
                d = dot(left, right)
                acc[place, :] = d if fresh else acc[place, :] + d
        loop(0, 10, pair)

    panel_copy(0).wait()
    analyse(msg_ref, me, True)

    def arrived(d):
        in_copy(d).wait_recv()
        panel_copy(d).wait()
        analyse(got, behind(d), False)

    loop(1, 16, arrived)

    def fold(g):
        rows = acc[pl.ds(pl.multiple_of(g * 128, 128), 128), :].reshape(16, 8, DEG)
        for c in range(2):
            mine[pl.ds(pl.multiple_of(c * 320 + g * 16, 16), 16), :] = jnp.sum(
                rows * factor_ref[c][None], axis=1
            )

    loop(0, 20, fold)
    loop(1, 8, lambda d: slab_copy(d).start())
    own = pl.ds(pl.multiple_of(lat * SLAB, 16), SLAB)
    total = mine[own, :]
    for d in range(1, 8):
        slab_copy(d).wait_recv()
        total = total + parts[pl.ds(pl.multiple_of((lat + 8 - d) % 8 * SLAB, 16), SLAB), :]
    keep = keep_ref[pl.ds(pl.multiple_of(lat % 4 * SLAB, 16), SLAB), :]
    coeff[own, :] = (total * keep).astype(BF16)
    loop(1, 8, lambda d: coeff_copy(d).start())
    loop(1, 8, lambda d: coeff_copy(d).wait_recv())

    def synthesise(ref, peer, row):
        def four(i):
            outs = []
            for e in range(8):
                g = jnp.minimum(i * 8 + e, 19)
                left = jnp.concatenate(
                    [coeff[pl.ds(pl.multiple_of(c * 320 + g * 16, 16), 16), :] for c in range(2)], 0
                )
                right = pan[
                    pl.ds(pl.multiple_of(peer * 16, 16), 16), pl.ds(pl.multiple_of(g * 16, 16), 16), :
                ].reshape(256, DEG)
                d = lax.dot_general(left, right, (((1,), (1,)), ((), ())), preferred_element_type=F32)
                d = d * pick_ref[...]
                for c in range(2):
                    outs.append(jnp.sum(d[c * 16 : c * 16 + 16], axis=0, keepdims=True))
            ref[pl.ds(pl.multiple_of(row * ROWS_OUT + i * 16, 16), 16), :] = jnp.concatenate(outs, 0).astype(BF16)
        loop(0, 3, four)

    def leaving(i):
        d = 16 - i
        synthesise(syn, ahead(d), ahead(d))
        out_copy(d).start()

    loop(1, 16, leaving)
    synthesise(out_ref, me, me)

    def finish(d):
        in_copy(d).wait_send()
        out_copy(d).wait()

    loop(1, 16, finish)

    def finish_lat(d):
        slab_copy(d).wait_send()
        coeff_copy(d).wait_send()

    loop(1, 8, finish_lat)


def middle(msg, panels, keep, factors):
    t = tables()
    dma = pltpu.SemaphoreType.DMA
    return pl.pallas_call(
        middle_kernel,
        out_shape=jax.ShapeDtypeStruct((16 * ROWS_OUT, 256), BF16),
        in_specs=[vmem(), pl.BlockSpec(memory_space=pl.ANY)] + [vmem()] * 4,
        out_specs=vmem(),
        scratch_shapes=[
            pltpu.VMEM((256, 320, DEG), BF16),
            pltpu.VMEM((16 * ROWS_IN, 256), BF16),
            pltpu.VMEM((20 * 128, DEG), F32),
            pltpu.VMEM((640, DEG), F32),
            pltpu.VMEM((640, DEG), F32),
            pltpu.VMEM((640, DEG), BF16),
            pltpu.VMEM((16 * ROWS_OUT, 256), BF16),
            dma((16,)), dma((16,)), dma((16,)), dma((8,)), dma((8,)), dma((8,)), dma((8,)), dma((16,)), dma((16,)),
        ],
        compiler_params=pltpu.CompilerParams(
            vmem_limit_bytes=48 * MIB, collective_id=0, has_side_effects=True
        ),
        cost_estimate=pl.CostEstimate(flops=8 * 10**9, bytes_accessed=24 * 10**6, transcendentals=0),
        name="middle",
    )(msg, panels, keep, t["diag"], factors, t["pick"])


def inverse_kernel(slot_ref, msg_ref, back_ref, twist_ref, lh_ref, ll_ref, out_ref, ts, ls, ys):
    ts[0:8, :] = jnp.zeros((8, 128), F32)
    ts[ORDERS:TROWS, :] = jnp.zeros((TROWS - ORDERS, 128), F32)

    def one_peer(o, carry):
        for part in range(3):
            rows = msg_ref[pl.ds(pl.multiple_of(o * 48 + part * 16, 16), 16), :].astype(F32)
            count = 128 if part < 2 else 64
            blocks = []
            for h in range(2):
                side = rows[:, h * 128 : h * 128 + 128]
                groups = []
                for g in range(8):
                    v = side[g // 4 * 8 : g // 4 * 8 + 8]
                    if g % 4:
                        v = pltpu.roll(v, 8 - 2 * (g % 4), 0)
                    groups.append(v)
                blocks += swap_chunks(groups)
            t = jnp.concatenate(blocks, 0).T
            base = o * 320 + part * 128
            for i in range(count):
                ts[pl.ds(slot_ref[base + i] + 1, 1), :] = t[i : i + 1]
        return carry

    lax.fori_loop(0, 16, one_peer, 0)

    def one_k(k, carry):
        plus = ts[pl.ds(k, 32, stride=SLOW), :]
        minus = ts[pl.ds(SLOW - k, 32, stride=SLOW), :]
        minus = jnp.where(jnp.logical_and(k > 0, k < 90), minus, 0.0)
        both = jnp.concatenate([plus, minus, jnp.zeros((64, 128), F32)], 0)
        ls[pl.ds(k, 128, stride=HALF), :] = both.T
        return carry

    lax.fori_loop(0, HALF, one_k, 0)

    def one_cycle(r, carry):
        parts = []
        for c in range(2):
            parts.append(ls[pl.ds(pl.multiple_of((r * 8 + c) * HALF, HALF), HALF), :][:, :64])
        left = jnp.concatenate(parts, 1).astype(BF16)
        w = dot(jnp.concatenate([left, left], 1), back_ref[...])
        re, im = w[:, :256], w[:, 256:]
        c, s = twist_ref[0], twist_ref[1]
        v = jnp.concatenate([re * c - im * s, im * c + re * s], 0).astype(BF16)
        field = dot(lh_ref[...], v) + dot(ll_ref[...], v)
        for lane in range(2):
            ys[lane, pl.ds(pl.multiple_of(r * 192, 192), 192), :] = field[:, lane * 128 : lane * 128 + 128]
        return carry

    lax.fori_loop(0, CYC, one_cycle, 0)
    for a in range(SLOW):
        v = jnp.concatenate([ys.at[lane][pl.ds(a, CYC, stride=192), :] for lane in range(2)], 1)
        out_ref[:, FAST * a : FAST * a + FAST] = v[:, :FAST]


def inverse(msg, slots):
    t = tables()
    return pl.pallas_call(
        inverse_kernel,
        out_shape=jax.ShapeDtypeStruct((CYC, LON), F32),
        in_specs=[pl.BlockSpec(memory_space=pltpu.SMEM)] + [vmem()] * 5,
        out_specs=vmem(),
        scratch_shapes=[
            pltpu.VMEM((TROWS, 128), F32),
            pltpu.VMEM((128 * HALF, 128), F32),
            pltpu.VMEM((2, CYC * 192, 128), F32),
        ],
        compiler_params=pltpu.CompilerParams(vmem_limit_bytes=48 * MIB),
        name="inverse",
    )(slots, msg, t["back"], t["twist"], *t["last"])


def degrees():
    stride = (NMAX - ORDERS) // DEG
    return ORDERS + np.arange(DEG, dtype=np.int32) * stride


def factor_rows():
    degree = degrees().astype(np.float64)
    rows = np.zeros((2, 8, DEG), np.float32)
    for c in range(2):
        rows[c, 3 * c] = 1.0
        rows[c, 3 * c + 1] = (degree + 2.0) / (2.0 * NMAX)
        rows[c, 3 * c + 2] = (degree + 2.0) * (degree + 1.0) / (6.0 * NMAX * NMAX)
    return rows


def local(heights, panels, ord_slot, cutoffs):
    msg = forward(heights, ord_slot)
    keep = (degrees()[None, :] <= cutoffs[:, None]).astype(F32)
    back = middle(msg, panels, keep, factor_rows())
    return inverse(back, ord_slot)


def solution(mesh):
    return jax.shard_map(
        local,
        mesh=mesh,
        in_specs=(P(("lat", "ord"), None), P("lat", "ord", None), P(), P("ord")),
        out_specs=P(("lat", "ord"), None),
        check_vma=False,
    )
```

```python
import functools
import math

import jax
import jax.numpy as jnp
import numpy as np
from jax import lax
from jax.experimental import pallas as pl
from jax.experimental.pallas import tpu as pltpu
from jax.sharding import PartitionSpec as P

LON = 43200
SLOW = 180
FAST = 240
HALF = 96
ORDERS = 5120
DEG = 128
NMAX = 21600
CYC = 16
TROWS = 6016
F32 = jnp.float32
BF16 = jnp.bfloat16
MIB = 1024 * 1024


def split16(table):
    high = table.astype(np.float32).astype(jnp.bfloat16)
    low = (table - high.astype(np.float64)).astype(np.float32).astype(jnp.bfloat16)
    return high, low


def angles(left, right, total):
    return 2.0 * np.pi / total * ((left[:, None] * right[None, :]) % total)


@functools.cache
def tables():
    k = np.arange(91)
    a = np.arange(SLOW)
    b = np.arange(FAST)
    q = np.arange(29)
    ka = angles(k, a, SLOW)
    first = np.zeros((2, HALF, 192))
    first[0, :91, :SLOW] = np.cos(ka)
    first[1, :91, :SLOW] = -np.sin(ka)
    first = first.reshape(2 * HALF, 192)
    kb = angles(k, b, LON)
    twist = np.zeros((2, HALF, 256), np.float32)
    twist[0, :91, :FAST] = np.cos(kb)
    twist[1, :91, :FAST] = np.sin(kb)
    bq = angles(b, q, FAST)
    bq1 = angles(b, q + 1, FAST)
    second = np.zeros((2, 256, 2, 128))
    second[0, :FAST, 0, 0:29] = np.cos(bq)
    second[1, :FAST, 0, 0:29] = np.sin(bq)
    second[0, :FAST, 1, 0:29] = -np.sin(bq)
    second[1, :FAST, 1, 0:29] = np.cos(bq)
    second[0, :FAST, 0, 32:61] = np.cos(bq1)
    second[1, :FAST, 0, 32:61] = -np.sin(bq1)
    second[0, :FAST, 1, 32:61] = -np.sin(bq1)
    second[1, :FAST, 1, 32:61] = -np.cos(bq1)
    second[..., 64:] = second[..., :64]
    second = second.reshape(512, 256) / math.sqrt(LON)
    back = np.zeros((2, 2, 32, 2, 256))
    back[0, 0, :29, 0, :FAST] = np.cos(bq).T
    back[0, 0, :29, 1, :FAST] = np.sin(bq).T
    back[1, 0, :29, 0, :FAST] = -np.sin(bq).T
    back[1, 0, :29, 1, :FAST] = np.cos(bq).T
    back[0, 1, :29, 0, :FAST] = np.cos(bq1).T
    back[0, 1, :29, 1, :FAST] = -np.sin(bq1).T
    back[1, 1, :29, 0, :FAST] = -np.sin(bq1).T
    back[1, 1, :29, 1, :FAST] = -np.cos(bq1).T
    back = np.concatenate(split16(back.reshape(128, 512)), 0)
    last = np.zeros((192, 2, HALF))
    last[:SLOW, 0, :91] = np.cos(ka).T
    last[:SLOW, 1, :91] = -np.sin(ka).T
    last = last.reshape(192, 2 * HALF) * math.sqrt(2048 / (DEG * ORDERS))
    rows = np.arange(128)
    lanes = np.arange(256)
    diag = (lanes[None, :] % 16 == rows[:, None] // 8).astype(jnp.bfloat16)
    pick = (lanes[None, :] % 16 == np.arange(32)[:, None] % 16).astype(np.float32)
    return dict(
        first=split16(first), twist=twist, second=split16(second), back=back,
        last=split16(last), diag=diag, pick=pick,
    )


def swap_chunks(rows):
    rows = list(rows)
    chunk = lax.broadcasted_iota(jnp.int32, (8, 128), 1) // 16
    for d in (4, 2, 1):
        low = (chunk & d) == 0
        new = list(rows)
        for r in range(8):
            if r & d:
                continue
            new[r] = jnp.where(low, rows[r], pltpu.roll(rows[r + d], d * 16, 1))
            new[r + d] = jnp.where(low, pltpu.roll(rows[r], 128 - d * 16, 1), rows[r + d])
        rows = new
    return rows


def dot(left, right):
    return jnp.dot(left, right, preferred_element_type=F32)


def halves(value):
    high = value.astype(BF16)
    return high, (value - high.astype(F32)).astype(BF16)


def vmem():
    return pl.BlockSpec(memory_space=pltpu.VMEM)


MESH = pl.DeviceIdType.MESH
ROWS_IN = 160
ROWS_OUT = 48
SLAB = 80


def main_kernel(slot_ref, x_hbm, fh_hbm, fl_hbm, twist_hbm, sh_hbm, sl_hbm, panel_ref, keep_ref, diag_ref,
                factor_ref, pick_ref, out_ref,
                x_ref, fh_ref, fl_ref, twist_ref, sh_ref, sl_ref, xs, qs, ts, gs, msg_ref,
                pan, got, mine, parts, coeff, syn,
                xsem, tsem, psem, s1, r1, s2, r2, s3, r3, s4, r4):
    lat = lax.axis_index("lat")
    me = lax.axis_index("ord")
    hy, hz, hc = me // 8, me // 2 % 4, me % 2

    def ahead(d):
        return (hy + d // 8) % 2 * 8 + (hz + d // 2 % 4) % 4 * 2 + (hc + d % 2) % 2

    def behind(d):
        return (hy + 2 - d // 8) % 2 * 8 + (hz + 4 - d // 2 % 4) % 4 * 2 + (hc + 2 - d % 2) % 2

    def panel_copy(d):
        place = pl.ds(pl.multiple_of(behind(d) * 16, 16), 16)
        return pltpu.make_async_copy(panel_ref.at[place], pan.at[place], psem.at[d])

    def in_copy(d):
        return pltpu.make_async_remote_copy(
            src_ref=msg_ref.at[pl.ds(pl.multiple_of(ahead(d) * ROWS_IN, 16), ROWS_IN)],
            dst_ref=got.at[pl.ds(pl.multiple_of(me * ROWS_IN, 16), ROWS_IN)],
            send_sem=s1.at[d], recv_sem=r1.at[d],
            device_id=(lat, ahead(d)), device_id_type=MESH,
        )

    def slab_copy(d):
        peer = (lat + d) % 8
        return pltpu.make_async_remote_copy(
            src_ref=mine.at[pl.ds(pl.multiple_of(peer * SLAB, 16), SLAB)],
            dst_ref=parts.at[pl.ds(pl.multiple_of(lat * SLAB, 16), SLAB)],
            send_sem=s2.at[d], recv_sem=r2.at[d],
            device_id=(peer, me), device_id_type=MESH,
        )

    def coeff_copy(d):
        peer = (lat + d) % 8
        place = pl.ds(pl.multiple_of(lat * SLAB, 16), SLAB)
        return pltpu.make_async_remote_copy(
            src_ref=coeff.at[place], dst_ref=coeff.at[place],
            send_sem=s3.at[d], recv_sem=r3.at[d],
            device_id=(peer, me), device_id_type=MESH,
        )

    def out_copy(d):
        return pltpu.make_async_remote_copy(
            src_ref=syn.at[pl.ds(pl.multiple_of(ahead(d) * ROWS_OUT, 16), ROWS_OUT)],
            dst_ref=out_ref.at[pl.ds(pl.multiple_of(me * ROWS_OUT, 16), ROWS_OUT)],
            send_sem=s4.at[d], recv_sem=r4.at[d],
            device_id=(lat, ahead(d)), device_id_type=MESH,
        )

    def loop(low, high, body):
        def step(d, carry):
            body(d)
            return carry
        lax.fori_loop(low, high, step, 0)

    heights_copy = pltpu.make_async_copy(x_hbm, x_ref, xsem)
    heights_copy.start()
    held = ((fh_hbm, fh_ref), (fl_hbm, fl_ref), (twist_hbm, twist_ref), (sh_hbm, sh_ref), (sl_hbm, sl_ref))

    def table_copy(i):
        return pltpu.make_async_copy(held[i][0], held[i][1], tsem.at[i])

    for i in range(5):
        table_copy(i).start()
    loop(0, 16, lambda d: panel_copy(d).start())
    barrier = pltpu.get_barrier_semaphore()
    loop(1, 16, lambda d: pl.semaphore_signal(barrier, inc=1, device_id=(lat, ahead(d)), device_id_type=MESH))
    loop(1, 8, lambda d: pl.semaphore_signal(barrier, inc=1, device_id=((lat + d) % 8, me), device_id_type=MESH))
    heights_copy.wait()
    inside = lax.broadcasted_iota(jnp.int32, (CYC, 256), 1) < FAST
    for r in range(CYC):
        for lane in range(2):
            xs[lane, r * 192 + 176 : r * 192 + 192, :] = jnp.zeros((16, 128), F32)
    for a in range(SLOW):
        start = FAST * a // 128 * 128
        off = FAST * a - start
        if start + 384 <= LON:
            v = x_ref[:, start : start + 384].astype(F32)
        else:
            v = jnp.concatenate(
                [x_ref[:, start:LON].astype(F32), jnp.zeros((CYC, start + 384 - LON), F32)], 1
            )
        if off:
            v = pltpu.roll(v, 384 - off, 1)
        v = jnp.where(inside, v[:, :256], 0.0)
        for lane in range(2):
            xs.at[lane][pl.ds(a, CYC, stride=192), :] = v[:, lane * 128 : lane * 128 + 128]

    first = lax.broadcasted_iota(jnp.int32, (48, 128), 1) < 64

    def one_cycle(r, carry):
        rows = pl.ds(pl.multiple_of(r * 192, 192), 192)
        level = jnp.concatenate([xs[0, rows, :], xs[1, rows, :]], 1)
        value = level
        for p in range(3):
            if p:
                value = value * level
            if p == 0:
                high = value.astype(BF16)
                y = dot(fh_ref[...], high) + dot(fl_ref[...], high)
            else:
                high, low = halves(value)
                y = dot(fh_ref[...], high) + dot(fl_ref[...], high) + dot(fh_ref[...], low)
            re, im = y[:HALF], y[HALF:]
            tc, tsin = twist_ref[0], twist_ref[1]
            z = jnp.concatenate([re * tc + im * tsin, im * tc - re * tsin], 1)
            zh, zl = halves(z)
            o = dot(zh, sh_ref[...]) + dot(zh, sl_ref[...]) + dot(zl, sh_ref[...])
            for c in range(2):
                part = o[:, c * 128 : c * 128 + 128]
                qs[pl.ds(r * 8 + c * 3 + p, 48, stride=128), :] = jnp.where(first, part[:48], part[48:])
        for x in (6, 7):
            qs[pl.ds(r * 8 + x, 48, stride=128), :] = jnp.zeros((48, 128), F32)
        return carry

    for i in range(5):
        table_copy(i).wait()
    lax.fori_loop(0, CYC, one_cycle, 0)

    def one_k(k, carry):
        t = qs[pl.ds(pl.multiple_of(k * 128, 128), 128), :].T
        ts[pl.ds(k, 32, stride=SLOW), :] = t[0:32]
        ts[pl.ds(SLOW - k, 32, stride=SLOW), :] = t[32:64]
        return t

    def two_k(k, carry):
        t = one_k(k, carry)
        ts[pl.ds(k + 48, 32, stride=SLOW), :] = t[64:96]
        ts[pl.ds(SLOW - 48 - k, 32, stride=SLOW), :] = t[96:128]
        return carry

    def only_k(k, carry):
        one_k(k, carry)
        return carry

    lax.fori_loop(0, 43, two_k, 0)
    lax.fori_loop(43, 48, only_k, 0)

    pl.semaphore_wait(barrier, 22)

    def one_chip(i, carry):
        far = 7 - i
        chip = (hy + far // 4) % 2 * 4 + (hz + far % 4) % 4
        for j in range(5):
            tile = chip * 5 + j
            for i in range(0, 128, 32):
                rows = [ts[pl.ds(slot_ref[tile * 128 + i + e] + 1, 1), :] for e in range(32)]
                for e in range(32):
                    gs[j, i + e : i + e + 1, :] = rows[e]
            t = gs[j].T
            sides = []
            for h in range(2):
                sides.append(
                    jnp.concatenate(swap_chunks([t[(h * 8 + r) * 8 : (h * 8 + r + 1) * 8] for r in range(8)]), 0)
                )
            msg_ref[pl.ds(pl.multiple_of(tile * 64, 64), 64), :] = jnp.concatenate(sides, 1).astype(BF16)

        @pl.when(far > 0)
        def _():
            in_copy(far * 2).start()

        in_copy(far * 2 + 1).start()
        return carry

    lax.fori_loop(0, 8, one_chip, 0)
    own_in = pl.ds(pl.multiple_of(me * ROWS_IN, 16), ROWS_IN)
    got[own_in, :] = msg_ref[own_in, :]
    loop(0, 16, lambda d: panel_copy(d).wait())
    loop(1, 16, lambda d: in_copy(d).wait_recv())

    def analyse(i):
        accs = [None, None]
        for R in range(16):
            both = got[pl.ds(pl.multiple_of(R * ROWS_IN + i * 16, 16), 16), :].astype(F32)
            for e in range(2):
                one = both[e * 8 : e * 8 + 8]
                two = jnp.concatenate([one, one], 0).astype(BF16)
                left = jnp.concatenate([two] * 8, 0) * diag_ref[...]
                right = pan[
                    R * 16 : R * 16 + 16, pl.ds(pl.multiple_of(i * 32 + e * 16, 16), 16), :
                ].reshape(256, DEG)
                d = dot(left, right)
                accs[e] = d if R == 0 else accs[e] + d
        for e in range(2):
            rows = accs[e].reshape(16, 8, DEG)
            for c in range(2):
                mine[pl.ds(pl.multiple_of(c * 320 + i * 32 + e * 16, 16), 16), :] = jnp.sum(
                    rows * factor_ref[c][None], axis=1
                )

    loop(0, 10, analyse)
    loop(1, 8, lambda d: slab_copy(d).start())
    own = pl.ds(pl.multiple_of(lat * SLAB, 16), SLAB)
    total = mine[own, :]
    for d in range(1, 8):
        slab_copy(d).wait_recv()
        total = total + parts[pl.ds(pl.multiple_of((lat + 8 - d) % 8 * SLAB, 16), SLAB), :]
    keep = keep_ref[pl.ds(pl.multiple_of(lat % 4 * SLAB, 16), SLAB), :]
    coeff[own, :] = (total * keep).astype(BF16)
    loop(1, 8, lambda d: coeff_copy(d).start())
    loop(1, 8, lambda d: coeff_copy(d).wait_recv())

    def synthesise(ref, peer, row):
        def four(i):
            outs = []
            for e in range(8):
                g = jnp.minimum(i * 8 + e, 19)
                left = jnp.concatenate(
                    [coeff[pl.ds(pl.multiple_of(c * 320 + g * 16, 16), 16), :] for c in range(2)], 0
                )
                right = pan[
                    pl.ds(pl.multiple_of(peer * 16, 16), 16), pl.ds(pl.multiple_of(g * 16, 16), 16), :
                ].reshape(256, DEG)
                d = lax.dot_general(left, right, (((1,), (1,)), ((), ())), preferred_element_type=F32)
                d = d * pick_ref[...]
                for c in range(2):
                    outs.append(jnp.sum(d[c * 16 : c * 16 + 16], axis=0, keepdims=True))
            ref[pl.ds(pl.multiple_of(row * ROWS_OUT + i * 16, 16), 16), :] = jnp.concatenate(outs, 0).astype(BF16)
        loop(0, 3, four)

    def leaving(i):
        d = 16 - i
        synthesise(syn, ahead(d), ahead(d))
        out_copy(d).start()

    loop(1, 16, leaving)
    synthesise(out_ref, me, me)

    def finish(d):
        in_copy(d).wait_send()
        out_copy(d).wait()

    loop(1, 16, finish)

    def finish_lat(d):
        slab_copy(d).wait_send()
        coeff_copy(d).wait_send()

    loop(1, 8, finish_lat)


def main(heights, slots, panels, keep, factors):
    t = tables()
    dma = pltpu.SemaphoreType.DMA
    vec = pltpu.VMEM
    hbm = pl.BlockSpec(memory_space=pl.ANY)
    return pl.pallas_call(
        main_kernel,
        out_shape=jax.ShapeDtypeStruct((16 * ROWS_OUT, 256), BF16),
        in_specs=[pl.BlockSpec(memory_space=pltpu.SMEM)] + [hbm] * 7 + [vmem()] * 4,
        out_specs=vmem(),
        scratch_shapes=[
            vec((CYC, LON), BF16),
            vec((192, 192), BF16),
            vec((192, 192), BF16),
            vec((2, HALF, 256), F32),
            vec((512, 256), BF16),
            vec((512, 256), BF16),
            vec((2, CYC * 192, 128), F32),
            vec((48 * 128, 128), F32),
            vec((TROWS, 128), F32),
            vec((5, 128, 128), F32),
            vec((16 * ROWS_IN, 256), BF16),
            vec((256, 320, DEG), BF16),
            vec((16 * ROWS_IN, 256), BF16),
            vec((640, DEG), F32),
            vec((640, DEG), F32),
            vec((640, DEG), BF16),
            vec((16 * ROWS_OUT, 256), BF16),
            dma, dma((5,)), dma((16,)), dma((16,)), dma((16,)), dma((8,)), dma((8,)), dma((8,)), dma((8,)),
            dma((16,)), dma((16,)),
        ],
        compiler_params=pltpu.CompilerParams(
            vmem_limit_bytes=56 * MIB, collective_id=0, has_side_effects=True
        ),
        cost_estimate=pl.CostEstimate(flops=2 * 10**10, bytes_accessed=24 * 10**6, transcendentals=0),
        name="main",
    )(slots, heights, *t["first"], t["twist"], *t["second"], panels, keep, t["diag"], factors, t["pick"])


def inverse_kernel(slot_ref, msg_ref, back_ref, twist_ref, lh_ref, ll_ref, out_ref, ts, ls, ys):
    ts[0:8, :] = jnp.zeros((8, 128), F32)
    ts[ORDERS:TROWS, :] = jnp.zeros((TROWS - ORDERS, 128), F32)

    sub = lax.broadcasted_iota(jnp.int32, (8, 128), 0)

    def one_peer(o, carry):
        for part in range(3):
            rows = msg_ref[pl.ds(pl.multiple_of(o * 48 + part * 16, 16), 16), :].astype(F32)
            count = 128 if part < 2 else 64
            groups = []
            for g in range(8):
                half = rows[g // 4 * 8 : g // 4 * 8 + 8]
                v0, v1 = half[:, :128], half[:, 128:]
                at = g % 4
                v0 = pltpu.roll(v0, 8 - 2 * at, 0) if at else v0
                v1 = pltpu.roll(v1, (10 - 2 * at) % 8, 0) if at != 1 else v1
                groups.append(jnp.where(sub < 2, v0, v1))
            blocks = swap_chunks(groups)
            packed = [jnp.where(sub < 4, blocks[2 * i], pltpu.roll(blocks[2 * i + 1], 4, 0)) for i in range(4)]
            t = jnp.concatenate(packed, 0).T
            base = o * 320 + part * 128
            for i in range(count):
                ts[pl.ds(slot_ref[base + i] + 1, 1), 0:32] = t[i : i + 1]
        return carry

    lax.fori_loop(0, 16, one_peer, 0)

    def one_k(k, carry):
        stack = []
        for base in (0, 48):
            plus = ts[pl.ds(k + base, 32, stride=SLOW), :]
            minus = ts[pl.ds(SLOW - base - k, 32, stride=SLOW), :]
            lone = k == 0 if base == 0 else k == 90 - base
            stack += [plus, jnp.where(lone, 0.0, minus)]
        ls[pl.ds(k, 32, stride=48), :] = jnp.concatenate(stack, 0)[:, :32].T
        return carry

    lax.fori_loop(0, 48, one_k, 0)
    first = lax.broadcasted_iota(jnp.int32, (48, 128), 1) < 64

    def one_cycle(r, carry):
        at = (r % 8 * 4 + r // 8 * 2) * 48
        l0 = ls[pl.ds(pl.multiple_of(at, 48), 48), :]
        l1 = ls[pl.ds(pl.multiple_of(at + 48, 48), 48), :]
        left = jnp.concatenate(
            [jnp.where(first, l0, pltpu.roll(l1, 64, 1)), jnp.where(first, pltpu.roll(l0, 64, 1), l1)], 0
        ).astype(BF16)
        w = dot(jnp.concatenate([left, left], 1), back_ref[...])
        re, im = w[:, :256], w[:, 256:]
        c, s = twist_ref[0], twist_ref[1]
        v = jnp.concatenate([re * c - im * s, im * c + re * s], 0).astype(BF16)
        field = dot(lh_ref[...], v) + dot(ll_ref[...], v)
        for lane in range(2):
            ys[lane, pl.ds(pl.multiple_of(r * 192, 192), 192), :] = field[:, lane * 128 : lane * 128 + 128]
        return carry

    lax.fori_loop(0, CYC, one_cycle, 0, unroll=2)
    for a in range(SLOW):
        v = jnp.concatenate([ys.at[lane][pl.ds(a, CYC, stride=192), :] for lane in range(2)], 1)
        out_ref[:, FAST * a : FAST * a + FAST] = v[:, :FAST]


def inverse(msg, slots):
    t = tables()
    return pl.pallas_call(
        inverse_kernel,
        out_shape=jax.ShapeDtypeStruct((CYC, LON), F32),
        in_specs=[pl.BlockSpec(memory_space=pltpu.SMEM)] + [vmem()] * 5,
        out_specs=vmem(),
        scratch_shapes=[
            pltpu.VMEM((TROWS, 128), F32),
            pltpu.VMEM((32 * 48, 128), F32),
            pltpu.VMEM((2, CYC * 192, 128), F32),
        ],
        compiler_params=pltpu.CompilerParams(vmem_limit_bytes=48 * MIB),
        name="inverse",
    )(slots, msg, t["back"], t["twist"], *t["last"])


def degrees():
    stride = (NMAX - ORDERS) // DEG
    return ORDERS + np.arange(DEG, dtype=np.int32) * stride


def factor_rows():
    degree = degrees().astype(np.float64)
    rows = np.zeros((2, 8, DEG), np.float32)
    for c in range(2):
        rows[c, 3 * c] = 1.0
        rows[c, 3 * c + 1] = (degree + 2.0) / (2.0 * NMAX)
        rows[c, 3 * c + 2] = (degree + 2.0) * (degree + 1.0) / (6.0 * NMAX * NMAX)
    return rows


def local(heights, panels, ord_slot, cutoffs):
    keep = (degrees()[None, :] <= cutoffs[:, None]).astype(F32)
    back = main(heights, ord_slot, panels, keep, factor_rows())
    return inverse(back, ord_slot)


def solution(mesh):
    return jax.shard_map(
        local,
        mesh=mesh,
        in_specs=(P(("lat", "ord"), None), P("lat", "ord", None), P(), P("ord")),
        out_specs=P(("lat", "ord"), None),
        check_vma=False,
    )
```

```python
import functools
import math

import jax
import jax.numpy as jnp
import numpy as np
from jax import lax
from jax.experimental import pallas as pl
from jax.experimental.pallas import tpu as pltpu
from jax.sharding import PartitionSpec as P

LON = 43200
SLOW = 180
FAST = 240
HALF = 96
ORDERS = 5120
DEG = 128
NMAX = 21600
CYC = 16
TROWS = 6016
F32 = jnp.float32
BF16 = jnp.bfloat16
MIB = 1024 * 1024


def split16(table):
    high = table.astype(np.float32).astype(jnp.bfloat16)
    low = (table - high.astype(np.float64)).astype(np.float32).astype(jnp.bfloat16)
    return high, low


def angles(left, right, total):
    return 2.0 * np.pi / total * ((left[:, None] * right[None, :]) % total)


@functools.cache
def tables():
    k = np.arange(91)
    a = np.arange(SLOW)
    b = np.arange(FAST)
    q = np.arange(29)
    ka = angles(k, a, SLOW)
    first = np.zeros((2, HALF, 192))
    first[0, :91, :SLOW] = np.cos(ka)
    first[1, :91, :SLOW] = -np.sin(ka)
    first = first.reshape(2 * HALF, 192)
    kb = angles(k, b, LON)
    twist = np.zeros((2, HALF, 256), np.float32)
    twist[0, :91, :FAST] = np.cos(kb)
    twist[1, :91, :FAST] = np.sin(kb)
    bq = angles(b, q, FAST)
    bq1 = angles(b, q + 1, FAST)
    second = np.zeros((2, 256, 2, 128))
    second[0, :FAST, 0, 0:29] = np.cos(bq)
    second[1, :FAST, 0, 0:29] = np.sin(bq)
    second[0, :FAST, 1, 0:29] = -np.sin(bq)
    second[1, :FAST, 1, 0:29] = np.cos(bq)
    second[0, :FAST, 0, 32:61] = np.cos(bq1)
    second[1, :FAST, 0, 32:61] = -np.sin(bq1)
    second[0, :FAST, 1, 32:61] = -np.sin(bq1)
    second[1, :FAST, 1, 32:61] = -np.cos(bq1)
    second = second / math.sqrt(LON)
    high, low = split16(second[..., :64])
    second = np.concatenate([high, low], -1).reshape(512, 256)
    back = np.zeros((2, 2, 32, 2, 256))
    back[0, 0, :29, 0, :FAST] = np.cos(bq).T
    back[0, 0, :29, 1, :FAST] = np.sin(bq).T
    back[1, 0, :29, 0, :FAST] = -np.sin(bq).T
    back[1, 0, :29, 1, :FAST] = np.cos(bq).T
    back[0, 1, :29, 0, :FAST] = np.cos(bq1).T
    back[0, 1, :29, 1, :FAST] = -np.sin(bq1).T
    back[1, 1, :29, 0, :FAST] = -np.sin(bq1).T
    back[1, 1, :29, 1, :FAST] = -np.cos(bq1).T
    back = np.concatenate(split16(back.reshape(128, 512)), 0)
    last = np.zeros((192, 2, HALF))
    last[:SLOW, 0, :91] = np.cos(ka).T
    last[:SLOW, 1, :91] = -np.sin(ka).T
    last = last.reshape(192, 2 * HALF) * math.sqrt(2048 / (DEG * ORDERS))
    rows = np.arange(128)
    lanes = np.arange(256)
    diag = (lanes[None, :] % 16 == rows[:, None] // 8).astype(jnp.bfloat16)
    pick = (lanes[None, :] % 16 == np.arange(16)[:, None]).astype(np.float32)
    return dict(
        first=split16(first), twist=twist, second=second, back=back,
        last=split16(last), diag=diag, pick=pick,
    )


def swap_chunks(rows):
    rows = list(rows)
    chunk = lax.broadcasted_iota(jnp.int32, (8, 128), 1) // 16
    for d in (4, 2, 1):
        low = (chunk & d) == 0
        new = list(rows)
        for r in range(8):
            if r & d:
                continue
            new[r] = jnp.where(low, rows[r], pltpu.roll(rows[r + d], d * 16, 1))
            new[r + d] = jnp.where(low, pltpu.roll(rows[r], 128 - d * 16, 1), rows[r + d])
        rows = new
    return rows


def dot(left, right):
    return jnp.dot(left, right, preferred_element_type=F32)


def halves(value):
    high = value.astype(BF16)
    return high, (value - high.astype(F32)).astype(BF16)


def vmem():
    return pl.BlockSpec(memory_space=pltpu.VMEM)


MESH = pl.DeviceIdType.MESH
ROWS_IN = 160
ROWS_OUT = 48
SLAB = 80


def main_kernel(slot_ref, cut_ref, x_hbm, fh_hbm, fl_hbm, twist_hbm, second_hbm, panel_ref, diag_ref,
                factor_ref, pick_ref, out_ref,
                x_ref, fh_ref, fl_ref, twist_ref, second_ref, xs, qs, ts, gs, msg_ref,
                pan, got, mine, parts, coeff, keeps, wide, syn,
                xsem, tsem, psem, s1, r1, s2, r2, s3, r3, s4, r4):
    lat = lax.axis_index("lat")
    me = lax.axis_index("ord")
    hy, hz, hc = me // 8, me // 2 % 4, me % 2

    def ahead(d):
        return (hy + d // 8) % 2 * 8 + (hz + d // 2 % 4) % 4 * 2 + (hc + d % 2) % 2

    def behind(d):
        return (hy + 2 - d // 8) % 2 * 8 + (hz + 4 - d // 2 % 4) % 4 * 2 + (hc + 2 - d % 2) % 2

    def panel_copy(d):
        place = pl.ds(pl.multiple_of(behind(d) * 16, 16), 16)
        return pltpu.make_async_copy(panel_ref.at[place], pan.at[place], psem.at[d])

    def in_copy(d):
        return pltpu.make_async_remote_copy(
            src_ref=msg_ref.at[pl.ds(pl.multiple_of(ahead(d) * ROWS_IN, 16), ROWS_IN)],
            dst_ref=got.at[pl.ds(pl.multiple_of(me * ROWS_IN, 16), ROWS_IN)],
            send_sem=s1.at[d], recv_sem=r1.at[d],
            device_id=(lat, ahead(d)), device_id_type=MESH,
        )

    base = (0, 256, 512)
    share = (32, 32, 16)

    def slab_copy(T, d):
        peer = (lat + d) % 8
        size = share[T]
        return pltpu.make_async_remote_copy(
            src_ref=mine.at[pl.ds(pl.multiple_of(base[T] + peer * size, 16), size)],
            dst_ref=parts.at[pl.ds(pl.multiple_of(base[T] + lat * size, 16), size)],
            send_sem=s2.at[T, d], recv_sem=r2.at[T, d],
            device_id=(peer, me), device_id_type=MESH,
        )

    def coeff_copy(T, d):
        peer = (lat + d) % 8
        place = pl.ds(pl.multiple_of(base[T] + lat * share[T], 16), share[T])
        return pltpu.make_async_remote_copy(
            src_ref=coeff.at[place], dst_ref=coeff.at[place],
            send_sem=s3.at[T, d], recv_sem=r3.at[T, d],
            device_id=(peer, me), device_id_type=MESH,
        )

    def out_copy(T, d):
        return pltpu.make_async_remote_copy(
            src_ref=syn.at[pl.ds(pl.multiple_of(ahead(d) * ROWS_OUT + T * 16, 16), 16)],
            dst_ref=out_ref.at[pl.ds(pl.multiple_of(me * ROWS_OUT + T * 16, 16), 16)],
            send_sem=s4.at[T, d], recv_sem=r4.at[T, d],
            device_id=(lat, ahead(d)), device_id_type=MESH,
        )

    def loop(low, high, body):
        def step(d, carry):
            body(d)
            return carry
        lax.fori_loop(low, high, step, 0)

    heights_copy = pltpu.make_async_copy(x_hbm, x_ref, xsem)
    heights_copy.start()
    held = ((fh_hbm, fh_ref), (fl_hbm, fl_ref), (twist_hbm, twist_ref), (second_hbm, second_ref))

    def table_copy(i):
        return pltpu.make_async_copy(held[i][0], held[i][1], tsem.at[i])

    for i in range(4):
        table_copy(i).start()
    loop(0, 16, lambda d: panel_copy(d).start())
    barrier = pltpu.get_barrier_semaphore()
    loop(1, 16, lambda d: pl.semaphore_signal(barrier, inc=1, device_id=(lat, ahead(d)), device_id_type=MESH))
    loop(1, 8, lambda d: pl.semaphore_signal(barrier, inc=1, device_id=((lat + d) % 8, me), device_id_type=MESH))
    degree = ORDERS + (NMAX - ORDERS) // DEG * lax.broadcasted_iota(jnp.int32, (1, DEG), 1)
    for T in range(3):
        size = share[T]
        for i in range(size):
            slot = T * 128 + (lat * size + i) % (4 * size)
            row = T * 32 + i
            keeps[row : row + 1, :] = jnp.where(degree <= cut_ref[slot], 1.0, 0.0)
    heights_copy.wait()
    inside = lax.broadcasted_iota(jnp.int32, (CYC, 256), 1) < FAST
    for r in range(CYC):
        for lane in range(2):
            xs[lane, r * 192 + 176 : r * 192 + 192, :] = jnp.zeros((16, 128), F32)
    for a in range(SLOW):
        start = FAST * a // 128 * 128
        off = FAST * a - start
        if start + 384 <= LON:
            v = x_ref[:, start : start + 384].astype(F32)
        else:
            v = jnp.concatenate(
                [x_ref[:, start:LON].astype(F32), jnp.zeros((CYC, start + 384 - LON), F32)], 1
            )
        if off:
            v = pltpu.roll(v, 384 - off, 1)
        v = jnp.where(inside, v[:, :256], 0.0)
        for lane in range(2):
            xs.at[lane][pl.ds(a, CYC, stride=192), :] = v[:, lane * 128 : lane * 128 + 128]

    first = lax.broadcasted_iota(jnp.int32, (48, 128), 1) < 64

    def one_cycle(r, carry):
        rows = pl.ds(pl.multiple_of(r * 192, 192), 192)
        level = jnp.concatenate([xs[0, rows, :], xs[1, rows, :]], 1)
        value = level
        for p in range(3):
            if p:
                value = value * level
            if p == 0:
                high = value.astype(BF16)
                y = dot(fh_ref[...], high) + dot(fl_ref[...], high)
            else:
                high, low = halves(value)
                y = dot(fh_ref[...], high) + dot(fl_ref[...], high) + dot(fh_ref[...], low)
            re, im = y[:HALF], y[HALF:]
            tc, tsin = twist_ref[0], twist_ref[1]
            z = jnp.concatenate([re * tc + im * tsin, im * tc - re * tsin], 1)
            zh, zl = halves(z)
            o = dot(zh, second_ref[...]) + dot(zl, second_ref[...])
            for c in range(2):
                part = o[:, c * 128 : c * 128 + 128]
                part = part + pltpu.roll(part, 64, 1)
                qs[pl.ds(r * 8 + c * 3 + p, 48, stride=128), :] = jnp.where(first, part[:48], part[48:])
        for x in (6, 7):
            qs[pl.ds(r * 8 + x, 48, stride=128), :] = jnp.zeros((48, 128), F32)
        return carry

    for i in range(4):
        table_copy(i).wait()
    lax.fori_loop(0, CYC, one_cycle, 0)

    def one_k(k, carry):
        t = qs[pl.ds(pl.multiple_of(k * 128, 128), 128), :].T
        ts[pl.ds(k, 32, stride=SLOW), :] = t[0:32]
        ts[pl.ds(SLOW - k, 32, stride=SLOW), :] = t[32:64]
        return t

    def two_k(k, carry):
        t = one_k(k, carry)
        ts[pl.ds(k + 48, 32, stride=SLOW), :] = t[64:96]
        ts[pl.ds(SLOW - 48 - k, 32, stride=SLOW), :] = t[96:128]
        return carry

    def only_k(k, carry):
        one_k(k, carry)
        return carry

    lax.fori_loop(0, 43, two_k, 0)
    lax.fori_loop(43, 48, only_k, 0)

    pl.semaphore_wait(barrier, 22)

    def one_chip(i, carry):
        far = 7 - i
        chip = (hy + far // 4) % 2 * 4 + (hz + far % 4) % 4
        for j in range(5):
            tile = chip * 5 + j
            for i in range(0, 128, 32):
                rows = [ts[pl.ds(slot_ref[tile * 128 + i + e] + 1, 1), :] for e in range(32)]
                for e in range(32):
                    gs[j, i + e : i + e + 1, :] = rows[e]
            t = gs[j].T
            sides = []
            for h in range(2):
                sides.append(
                    jnp.concatenate(swap_chunks([t[(h * 8 + r) * 8 : (h * 8 + r + 1) * 8] for r in range(8)]), 0)
                )
            msg_ref[pl.ds(pl.multiple_of(tile * 64, 64), 64), :] = jnp.concatenate(sides, 1).astype(BF16)

        @pl.when(far > 0)
        def _():
            in_copy(far * 2).start()

        in_copy(far * 2 + 1).start()
        return carry

    lax.fori_loop(0, 8, one_chip, 0)
    own_in = pl.ds(pl.multiple_of(me * ROWS_IN, 16), ROWS_IN)
    got[own_in, :] = msg_ref[own_in, :]
    loop(0, 16, lambda d: panel_copy(d).wait())
    loop(1, 16, lambda d: in_copy(d).wait_recv())

    def analyse(T, i):
        accs = [None, None]
        for R in range(16):
            both = got[pl.ds(pl.multiple_of(R * ROWS_IN + i * 16, 16), 16), :].astype(F32)
            for e in range(2):
                one = both[e * 8 : e * 8 + 8]
                two = jnp.concatenate([one, one], 0).astype(BF16)
                left = jnp.concatenate([two] * 8, 0) * diag_ref[...]
                right = pan[
                    R * 16 : R * 16 + 16, pl.ds(pl.multiple_of(i * 32 + e * 16, 16), 16), :
                ].reshape(256, DEG)
                d = dot(left, right)
                accs[e] = d if R == 0 else accs[e] + d
        for e in range(2):
            rows = accs[e].reshape(16, 8, DEG)
            for c in range(2):
                row = base[T] + c * 4 * share[T] + (i - 4 * T) * 32 + e * 16
                mine[pl.ds(pl.multiple_of(row, 16), 16), :] = jnp.sum(rows * factor_ref[c][None], axis=1)

    def analyse_part(T):
        loop(4 * T, min(4 * T + 4, 10), lambda i: analyse(T, i))
        loop(1, 8, lambda d: slab_copy(T, d).start())

    def total_part(T):
        size = share[T]
        own = pl.ds(pl.multiple_of(base[T] + lat * size, 16), size)
        total = mine[own, :]
        for d in range(1, 8):
            slab_copy(T, d).wait_recv()
            total = total + parts[pl.ds(pl.multiple_of(base[T] + (lat + 8 - d) % 8 * size, 16), size), :]
        coeff[own, :] = (total * keeps[T * 32 : T * 32 + size, :]).astype(BF16)
        loop(1, 8, lambda d: coeff_copy(T, d).start())

    chunk = lax.broadcasted_iota(jnp.int32, (DEG, 128), 1) // 16

    def synthesis_part(T):
        groups = share[T] // 4
        loop(1, 8, lambda d: coeff_copy(T, d).wait_recv())
        for c in range(2):
            rows = coeff[base[T] + c * groups * 16 : base[T] + (c + 1) * groups * 16, :].astype(F32)
            if groups < 8:
                rows = jnp.concatenate([rows, jnp.zeros((128 - groups * 16, DEG), F32)], 0)
            turned = rows.T
            for g in range(groups):
                wide[g * DEG : g * DEG + DEG, c * 128 : c * 128 + 128] = jnp.where(
                    chunk == g, turned, 0.0
                ).astype(BF16)

        def one_peer(ref, peer, row):
            left = jnp.concatenate(
                [
                    pan[
                        pl.ds(pl.multiple_of(peer * 16, 16), 16), T * 128 + g * 16 : T * 128 + g * 16 + 16, :
                    ].reshape(256, DEG)
                    for g in range(groups)
                ],
                1,
            )
            o = dot(left, wide[: groups * DEG, :]).reshape(16, 16, 256)
            o = jnp.sum(o * pick_ref[...][None], axis=1)
            ref[pl.ds(pl.multiple_of(row * ROWS_OUT + T * 16, 16), 16), :] = o.astype(BF16)

        def leaving(i):
            d = 16 - i
            one_peer(syn, ahead(d), ahead(d))
            out_copy(T, d).start()

        loop(1, 16, leaving)
        one_peer(out_ref, me, me)

    analyse_part(0)
    analyse_part(1)
    total_part(0)
    analyse_part(2)
    total_part(1)
    synthesis_part(0)
    total_part(2)
    synthesis_part(1)
    synthesis_part(2)
    loop(1, 16, lambda d: in_copy(d).wait_send())
    for T in range(3):
        loop(1, 16, lambda d: out_copy(T, d).wait())

        def finish_lat(d):
            slab_copy(T, d).wait_send()
            coeff_copy(T, d).wait_send()

        loop(1, 8, finish_lat)


def main(heights, slots, cutoffs, panels, factors):
    t = tables()
    dma = pltpu.SemaphoreType.DMA
    vec = pltpu.VMEM
    hbm = pl.BlockSpec(memory_space=pl.ANY)
    return pl.pallas_call(
        main_kernel,
        out_shape=jax.ShapeDtypeStruct((16 * ROWS_OUT, 256), BF16),
        in_specs=[pl.BlockSpec(memory_space=pltpu.SMEM)] * 2 + [hbm] * 6 + [vmem()] * 3,
        out_specs=vmem(),
        scratch_shapes=[
            vec((CYC, LON), BF16),
            vec((192, 192), BF16),
            vec((192, 192), BF16),
            vec((2, HALF, 256), F32),
            vec((512, 256), BF16),
            vec((2, CYC * 192, 128), F32),
            vec((48 * 128, 128), F32),
            vec((TROWS, 128), F32),
            vec((5, 128, 128), F32),
            vec((16 * ROWS_IN, 256), BF16),
            vec((256, 320, DEG), BF16),
            vec((16 * ROWS_IN, 256), BF16),
            vec((640, DEG), F32),
            vec((640, DEG), F32),
            vec((640, DEG), BF16),
            vec((80, DEG), F32),
            vec((8 * DEG, 256), BF16),
            vec((16 * ROWS_OUT, 256), BF16),
            dma, dma((4,)), dma((16,)), dma((16,)), dma((16,)), dma((3, 8)), dma((3, 8)), dma((3, 8)), dma((3, 8)),
            dma((3, 16)), dma((3, 16)),
        ],
        compiler_params=pltpu.CompilerParams(
            vmem_limit_bytes=56 * MIB, collective_id=0, has_side_effects=True
        ),
        cost_estimate=pl.CostEstimate(flops=2 * 10**10, bytes_accessed=24 * 10**6, transcendentals=0),
        name="main",
    )(slots, cutoffs, heights, *t["first"], t["twist"], t["second"], panels, t["diag"], factors, t["pick"])


def inverse_kernel(slot_ref, msg_ref, back_ref, twist_ref, lh_ref, ll_ref, out_ref, ts, ls, ys):
    ts[0:8, :] = jnp.zeros((8, 128), F32)
    ts[ORDERS:TROWS, :] = jnp.zeros((TROWS - ORDERS, 128), F32)

    def one_peer(o, carry):
        for part in range(3):
            rows = msg_ref[pl.ds(pl.multiple_of(o * 48 + part * 16, 16), 16), :].astype(F32)
            count = 128 if part < 2 else 64
            t = jnp.concatenate([rows[:, :128], rows[:, 128:]], 0).T
            base = o * 320 + part * 128
            for i in range(count):
                ts[pl.ds(slot_ref[base + i] + 1, 1), 0:32] = t[i : i + 1]
        return carry

    lax.fori_loop(0, 16, one_peer, 0)

    def one_k(k, carry):
        stack = []
        for base in (0, 48):
            plus = ts[pl.ds(k + base, 32, stride=SLOW), :]
            minus = ts[pl.ds(SLOW - base - k, 32, stride=SLOW), :]
            lone = k == 0 if base == 0 else k == 90 - base
            stack += [plus, jnp.where(lone, 0.0, minus)]
        ls[pl.ds(k, 32, stride=48), :] = jnp.concatenate(stack, 0)[:, :32].T
        return carry

    lax.fori_loop(0, 48, one_k, 0, unroll=4)
    first = lax.broadcasted_iota(jnp.int32, (48, 128), 1) < 64

    def one_cycle(r, carry):
        l0 = ls[pl.ds(pl.multiple_of(r * 48, 48), 48), :]
        l1 = ls[pl.ds(pl.multiple_of((r + CYC) * 48, 48), 48), :]
        left = jnp.concatenate(
            [jnp.where(first, l0, pltpu.roll(l1, 64, 1)), jnp.where(first, pltpu.roll(l0, 64, 1), l1)], 0
        ).astype(BF16)
        w = dot(jnp.concatenate([left, left], 1), back_ref[...])
        re, im = w[:, :256], w[:, 256:]
        c, s = twist_ref[0], twist_ref[1]
        v = jnp.concatenate([re * c - im * s, im * c + re * s], 0).astype(BF16)
        field = dot(lh_ref[...], v) + dot(ll_ref[...], v)
        for lane in range(2):
            ys[lane, pl.ds(pl.multiple_of(r * 192, 192), 192), :] = field[:, lane * 128 : lane * 128 + 128]
        return carry

    lax.fori_loop(0, CYC, one_cycle, 0, unroll=2)
    for a in range(SLOW):
        v = jnp.concatenate([ys.at[lane][pl.ds(a, CYC, stride=192), :] for lane in range(2)], 1)
        out_ref[:, FAST * a : FAST * a + FAST] = v[:, :FAST]


def inverse(msg, slots):
    t = tables()
    return pl.pallas_call(
        inverse_kernel,
        out_shape=jax.ShapeDtypeStruct((CYC, LON), F32),
        in_specs=[pl.BlockSpec(memory_space=pltpu.SMEM)] + [vmem()] * 5,
        out_specs=vmem(),
        scratch_shapes=[
            pltpu.VMEM((TROWS, 128), F32),
            pltpu.VMEM((32 * 48, 128), F32),
            pltpu.VMEM((2, CYC * 192, 128), F32),
        ],
        compiler_params=pltpu.CompilerParams(vmem_limit_bytes=48 * MIB),
        name="inverse",
    )(slots, msg, t["back"], t["twist"], *t["last"])


def degrees():
    stride = (NMAX - ORDERS) // DEG
    return ORDERS + np.arange(DEG, dtype=np.int32) * stride


def factor_rows():
    degree = degrees().astype(np.float64)
    rows = np.zeros((2, 8, DEG), np.float32)
    for c in range(2):
        rows[c, 3 * c] = 1.0
        rows[c, 3 * c + 1] = (degree + 2.0) / (2.0 * NMAX)
        rows[c, 3 * c + 2] = (degree + 2.0) * (degree + 1.0) / (6.0 * NMAX * NMAX)
    return rows


def local(heights, panels, ord_slot, cutoffs):
    back = main(heights, ord_slot, cutoffs, panels, factor_rows())
    return inverse(back, ord_slot)


def solution(mesh):
    return jax.shard_map(
        local,
        mesh=mesh,
        in_specs=(P(("lat", "ord"), None), P("lat", "ord", None), P(), P("ord")),
        out_specs=P(("lat", "ord"), None),
        check_vma=False,
    )
```

```python
import functools
import math

import jax
import jax.numpy as jnp
import numpy as np
from jax import lax
from jax.experimental import pallas as pl
from jax.experimental.pallas import tpu as pltpu
from jax.sharding import PartitionSpec as P

LON = 43200
SLOW = 180
FAST = 240
HALF = 96
ORDERS = 5120
DEG = 128
NMAX = 21600
CYC = 16
TROWS = 6016
F32 = jnp.float32
BF16 = jnp.bfloat16
MIB = 1024 * 1024


def split16(table):
    high = table.astype(np.float32).astype(jnp.bfloat16)
    low = (table - high.astype(np.float64)).astype(np.float32).astype(jnp.bfloat16)
    return high, low


def angles(left, right, total):
    return 2.0 * np.pi / total * ((left[:, None] * right[None, :]) % total)


@functools.cache
def tables():
    k = np.arange(91)
    a = np.arange(SLOW)
    b = np.arange(FAST)
    q = np.arange(29)
    ka = angles(k, a, SLOW)
    first = np.zeros((2, HALF, 192))
    first[0, :91, :SLOW] = np.cos(ka)
    first[1, :91, :SLOW] = -np.sin(ka)
    first = first.reshape(2 * HALF, 192)
    kb = angles(k, b, LON)
    twist = np.zeros((2, HALF, 256), np.float32)
    twist[0, :91, :FAST] = np.cos(kb)
    twist[1, :91, :FAST] = np.sin(kb)
    bq = angles(b, q, FAST)
    bq1 = angles(b, q + 1, FAST)
    second = np.zeros((2, 256, 2, 128))
    second[0, :FAST, 0, 0:29] = np.cos(bq)
    second[1, :FAST, 0, 0:29] = np.sin(bq)
    second[0, :FAST, 1, 0:29] = -np.sin(bq)
    second[1, :FAST, 1, 0:29] = np.cos(bq)
    second[0, :FAST, 0, 32:61] = np.cos(bq1)
    second[1, :FAST, 0, 32:61] = -np.sin(bq1)
    second[0, :FAST, 1, 32:61] = -np.sin(bq1)
    second[1, :FAST, 1, 32:61] = -np.cos(bq1)
    second = second / math.sqrt(LON)
    high, low = split16(second[..., :64])
    second = np.concatenate([high, low], -1).reshape(512, 256)
    back = np.zeros((2, 2, 32, 2, 256))
    back[0, 0, :29, 0, :FAST] = np.cos(bq).T
    back[0, 0, :29, 1, :FAST] = np.sin(bq).T
    back[1, 0, :29, 0, :FAST] = -np.sin(bq).T
    back[1, 0, :29, 1, :FAST] = np.cos(bq).T
    back[0, 1, :29, 0, :FAST] = np.cos(bq1).T
    back[0, 1, :29, 1, :FAST] = -np.sin(bq1).T
    back[1, 1, :29, 0, :FAST] = -np.sin(bq1).T
    back[1, 1, :29, 1, :FAST] = -np.cos(bq1).T
    back = np.concatenate(split16(back.reshape(128, 512)), 0)
    last = np.zeros((192, 2, HALF))
    last[:SLOW, 0, :91] = np.cos(ka).T
    last[:SLOW, 1, :91] = -np.sin(ka).T
    last = last.reshape(192, 2 * HALF) * math.sqrt(2048 / (DEG * ORDERS))
    rows = np.arange(128)
    lanes = np.arange(256)
    diag = (lanes[None, :] % 16 == rows[:, None] // 8).astype(jnp.bfloat16)
    pick = (lanes[None, :] % 16 == np.arange(16)[:, None]).astype(np.float32)
    return dict(
        first=split16(first), twist=twist, second=second, back=back,
        last=split16(last), diag=diag, pick=pick,
    )


def swap_chunks(rows):
    rows = list(rows)
    chunk = lax.broadcasted_iota(jnp.int32, (8, 128), 1) // 16
    for d in (4, 2, 1):
        low = (chunk & d) == 0
        new = list(rows)
        for r in range(8):
            if r & d:
                continue
            new[r] = jnp.where(low, rows[r], pltpu.roll(rows[r + d], d * 16, 1))
            new[r + d] = jnp.where(low, pltpu.roll(rows[r], 128 - d * 16, 1), rows[r + d])
        rows = new
    return rows


def dot(left, right):
    return jnp.dot(left, right, preferred_element_type=F32)


def halves(value):
    high = value.astype(BF16)
    return high, (value - high.astype(F32)).astype(BF16)


def vmem():
    return pl.BlockSpec(memory_space=pltpu.VMEM)


MESH = pl.DeviceIdType.MESH
ROWS_IN = 80
ROWS_OUT = 48
SLAB = 80


def main_kernel(slot_ref, cut_ref, x_hbm, fh_hbm, fl_hbm, twist_hbm, second_hbm, panel_ref, diag_ref,
                factor_ref, pick_ref, out_ref,
                x_ref, fh_ref, fl_ref, twist_ref, second_ref, xs, qs, ts, gs, msg_ref,
                pan, got, acc, mine, parts, coeff, keeps, wide, syn,
                xsem, tsem, psem, s1, r1, s2, r2, s3, r3, s4, r4):
    lat = lax.axis_index("lat")
    me = lax.axis_index("ord")
    hy, hz, hc = me // 8, me // 2 % 4, me % 2

    def ahead(d):
        return (hy + d // 8) % 2 * 8 + (hz + d // 2 % 4) % 4 * 2 + (hc + d % 2) % 2

    def behind(d):
        return (hy + 2 - d // 8) % 2 * 8 + (hz + 4 - d // 2 % 4) % 4 * 2 + (hc + 2 - d % 2) % 2

    def panel_copy(d):
        place = pl.ds(pl.multiple_of(behind(d) * 16, 16), 16)
        return pltpu.make_async_copy(panel_ref.at[place], pan.at[place], psem.at[d])

    def in_copy(d):
        return pltpu.make_async_remote_copy(
            src_ref=msg_ref.at[pl.ds(pl.multiple_of(ahead(d) * ROWS_IN, 16), ROWS_IN)],
            dst_ref=got.at[pl.ds(pl.multiple_of(me * ROWS_IN, 16), ROWS_IN)],
            send_sem=s1.at[d], recv_sem=r1.at[d],
            device_id=(lat, ahead(d)), device_id_type=MESH,
        )

    base = (0, 256, 512)
    share = (32, 32, 16)

    def slab_copy(T, d):
        peer = (lat + d) % 8
        size = share[T]
        return pltpu.make_async_remote_copy(
            src_ref=mine.at[pl.ds(pl.multiple_of(base[T] + peer * size, 16), size)],
            dst_ref=parts.at[pl.ds(pl.multiple_of(base[T] + lat * size, 16), size)],
            send_sem=s2.at[T, d], recv_sem=r2.at[T, d],
            device_id=(peer, me), device_id_type=MESH,
        )

    def coeff_copy(T, d):
        peer = (lat + d) % 8
        place = pl.ds(pl.multiple_of(base[T] + lat * share[T], 16), share[T])
        return pltpu.make_async_remote_copy(
            src_ref=coeff.at[place], dst_ref=coeff.at[place],
            send_sem=s3.at[T, d], recv_sem=r3.at[T, d],
            device_id=(peer, me), device_id_type=MESH,
        )

    def out_copy(T, d):
        return pltpu.make_async_remote_copy(
            src_ref=syn.at[pl.ds(pl.multiple_of(ahead(d) * ROWS_OUT + T * 16, 16), 16)],
            dst_ref=out_ref.at[pl.ds(pl.multiple_of(me * ROWS_OUT + T * 16, 16), 16)],
            send_sem=s4.at[T, d], recv_sem=r4.at[T, d],
            device_id=(lat, ahead(d)), device_id_type=MESH,
        )

    def loop(low, high, body):
        def step(d, carry):
            body(d)
            return carry
        lax.fori_loop(low, high, step, 0)

    heights_copy = pltpu.make_async_copy(x_hbm, x_ref, xsem)
    heights_copy.start()
    held = ((fh_hbm, fh_ref), (fl_hbm, fl_ref), (twist_hbm, twist_ref), (second_hbm, second_ref))

    def table_copy(i):
        return pltpu.make_async_copy(held[i][0], held[i][1], tsem.at[i])

    for i in range(4):
        table_copy(i).start()
    loop(0, 16, lambda d: panel_copy(d).start())
    barrier = pltpu.get_barrier_semaphore()
    loop(1, 16, lambda d: pl.semaphore_signal(barrier, inc=1, device_id=(lat, ahead(d)), device_id_type=MESH))
    loop(1, 8, lambda d: pl.semaphore_signal(barrier, inc=1, device_id=((lat + d) % 8, me), device_id_type=MESH))
    degree = ORDERS + (NMAX - ORDERS) // DEG * lax.broadcasted_iota(jnp.int32, (1, DEG), 1)
    for T in range(3):
        size = share[T]
        for i in range(size):
            slot = T * 128 + (lat * size + i) % (4 * size)
            row = T * 32 + i
            keeps[row : row + 1, :] = jnp.where(degree <= cut_ref[slot], 1.0, 0.0)
    heights_copy.wait()
    inside = lax.broadcasted_iota(jnp.int32, (CYC, 256), 1) < FAST
    for r in range(CYC):
        for lane in range(2):
            xs[lane, r * 192 + 176 : r * 192 + 192, :] = jnp.zeros((16, 128), F32)
    for a in range(SLOW):
        start = FAST * a // 128 * 128
        off = FAST * a - start
        if start + 384 <= LON:
            v = x_ref[:, start : start + 384].astype(F32)
        else:
            v = jnp.concatenate(
                [x_ref[:, start:LON].astype(F32), jnp.zeros((CYC, start + 384 - LON), F32)], 1
            )
        if off:
            v = pltpu.roll(v, 384 - off, 1)
        v = jnp.where(inside, v[:, :256], 0.0)
        for lane in range(2):
            xs.at[lane][pl.ds(a, CYC, stride=192), :] = v[:, lane * 128 : lane * 128 + 128]

    first = lax.broadcasted_iota(jnp.int32, (48, 128), 1) < 64

    def one_cycle(r, carry):
        rows = pl.ds(pl.multiple_of(r * 192, 192), 192)
        level = jnp.concatenate([xs[0, rows, :], xs[1, rows, :]], 1)
        value = level
        stack = []
        tc, tsin = twist_ref[0], twist_ref[1]
        for p in range(3):
            if p:
                value = value * level
            if p == 0:
                high = value.astype(BF16)
                y = dot(fh_ref[...], high) + dot(fl_ref[...], high)
            else:
                high, low = halves(value)
                y = dot(fh_ref[...], high) + dot(fl_ref[...], high) + dot(fh_ref[...], low)
            re, im = y[:HALF], y[HALF:]
            stack += list(halves(jnp.concatenate([re * tc + im * tsin, im * tc - re * tsin], 1)))
        o = dot(jnp.concatenate(stack, 0), second_ref[...])
        for p in range(3):
            both = o[p * 192 : p * 192 + HALF] + o[p * 192 + HALF : p * 192 + 192]
            for c in range(2):
                part = both[:, c * 128 : c * 128 + 128]
                part = part + pltpu.roll(part, 64, 1)
                qs[pl.ds(r * 8 + c * 3 + p, 48, stride=128), :] = jnp.where(first, part[:48], part[48:])
        return carry

    for i in range(4):
        table_copy(i).wait()
    lax.fori_loop(0, CYC, one_cycle, 0, unroll=2)

    def one_k(k, carry):
        t = qs[pl.ds(pl.multiple_of(k * 128, 128), 128), :].T
        ts[pl.ds(k, 32, stride=SLOW), :] = t[0:32]
        ts[pl.ds(SLOW - k, 32, stride=SLOW), :] = t[32:64]
        return t

    def two_k(k, carry):
        t = one_k(k, carry)
        ts[pl.ds(k + 48, 32, stride=SLOW), :] = t[64:96]
        ts[pl.ds(SLOW - 48 - k, 32, stride=SLOW), :] = t[96:128]
        return carry

    def only_k(k, carry):
        one_k(k, carry)
        return carry

    lax.fori_loop(0, 43, two_k, 0)
    lax.fori_loop(43, 48, only_k, 0)

    pl.semaphore_wait(barrier, 22)

    sub = lax.broadcasted_iota(jnp.int32, (8, 128), 0)

    def one_chip(i, carry):
        far = 7 - i // 2 - i % 2 * 4
        chip = (hy + far // 4) % 2 * 4 + (hz + far % 4) % 4
        for j in range(5):
            tile = chip * 5 + j
            for i in range(0, 128, 32):
                rows = [ts[pl.ds(slot_ref[tile * 128 + i + e] + 1, 1), :] for e in range(32)]
                for e in range(32):
                    gs[j, i + e : i + e + 1, :] = rows[e]
            t = gs[j].T
            sides = [swap_chunks([t[(h * 8 + r) * 8 : (h * 8 + r + 1) * 8] for r in range(8)]) for h in range(2)]
            rows = []
            for u in (0, 4):
                for side in sides:
                    rows.append(
                        jnp.concatenate(
                            [jnp.where(sub < 6, side[u + v], pltpu.roll(side[u + 3], 6 - 2 * v, 0)) for v in range(3)], 1
                        )
                    )
            msg_ref[pl.ds(pl.multiple_of(tile * 32, 32), 32), :] = jnp.concatenate(rows, 0).astype(BF16)

        @pl.when(far > 0)
        def _():
            in_copy(far * 2).start()

        in_copy(far * 2 + 1).start()
        return carry

    lax.fori_loop(0, 8, one_chip, 0)
    own_in = pl.ds(pl.multiple_of(me * ROWS_IN, 16), ROWS_IN)
    got[own_in, :] = msg_ref[own_in, :]
    loop(0, 16, lambda d: panel_copy(d).wait())
    def contract(q, far_set):
        sums = []
        for pair in range(2):
            accs = [None, None]
            for d in far_set:
                peer = behind(d)
                rows = got[pl.ds(pl.multiple_of(peer * ROWS_IN + q * 16, 16), 16), :].astype(F32)
                for e in range(2):
                    v = pair * 2 + e
                    sides = []
                    for h in (0, 8):
                        if v < 3:
                            sides.append(rows[h : h + 8, v * 128 : v * 128 + 128])
                        else:
                            x, y, z = (
                                pltpu.roll(rows[h : h + 8, w * 128 : w * 128 + 128], 2 + 2 * w, 0) for w in range(3)
                            )
                            sides.append(jnp.where(sub < 2, x, jnp.where(sub < 4, y, z)))
                    one = jnp.concatenate(sides, 1)
                    two = jnp.concatenate([one, one], 0).astype(BF16)
                    left = jnp.concatenate([two] * 8, 0) * diag_ref[...]
                    right = pan[
                        pl.ds(pl.multiple_of(peer * 16, 16), 16), pl.ds(pl.multiple_of(q * 64 + v * 16, 16), 16), :
                    ].reshape(256, DEG)
                    t = dot(left, right)
                    accs[e] = t if accs[e] is None else accs[e] + t
            sums += accs
        return sums

    early = (14, 15, 6, 7, 12, 13, 4, 5)
    late = (10, 11, 2, 3, 8, 9, 0, 1)

    def first_half(q):
        for v, t in enumerate(contract(q, early)):
            acc[pl.ds(pl.multiple_of(q * 512 + v * 128, 128), 128), :] = t

    def second_half(T, q):
        for v, t in enumerate(contract(q, late)):
            t = t + acc[pl.ds(pl.multiple_of(q * 512 + v * 128, 128), 128), :]
            rows = t.reshape(16, 8, DEG)
            for c in range(2):
                row = base[T] + c * 4 * share[T] + (q - 2 * T) * 64 + v * 16
                mine[pl.ds(pl.multiple_of(row, 16), 16), :] = jnp.sum(rows * factor_ref[c][None], axis=1)

    for d in early:
        in_copy(d).wait_recv()
    loop(0, 5, first_half)
    for d in late:
        if d:
            in_copy(d).wait_recv()

    def analyse_part(T):
        loop(2 * T, min(2 * T + 2, 5), lambda q: second_half(T, q))
        loop(1, 8, lambda d: slab_copy(T, d).start())

    def total_part(T):
        size = share[T]
        own = pl.ds(pl.multiple_of(base[T] + lat * size, 16), size)
        total = mine[own, :]
        for d in range(1, 8):
            slab_copy(T, d).wait_recv()
            total = total + parts[pl.ds(pl.multiple_of(base[T] + (lat + 8 - d) % 8 * size, 16), size), :]
        coeff[own, :] = (total * keeps[T * 32 : T * 32 + size, :]).astype(BF16)
        loop(1, 8, lambda d: coeff_copy(T, d).start())

    chunk = lax.broadcasted_iota(jnp.int32, (DEG, 128), 1) // 16

    def synthesis_part(T):
        groups = share[T] // 4
        loop(1, 8, lambda d: coeff_copy(T, d).wait_recv())
        for c in range(2):
            rows = coeff[base[T] + c * groups * 16 : base[T] + (c + 1) * groups * 16, :].astype(F32)
            if groups < 8:
                rows = jnp.concatenate([rows, jnp.zeros((128 - groups * 16, DEG), F32)], 0)
            turned = rows.T
            for g in range(groups):
                wide[g * DEG : g * DEG + DEG, c * 128 : c * 128 + 128] = jnp.where(
                    chunk == g, turned, 0.0
                ).astype(BF16)

        def one_peer(ref, peer, row):
            left = jnp.concatenate(
                [
                    pan[
                        pl.ds(pl.multiple_of(peer * 16, 16), 16), T * 128 + g * 16 : T * 128 + g * 16 + 16, :
                    ].reshape(256, DEG)
                    for g in range(groups)
                ],
                1,
            )
            o = dot(left, wide[: groups * DEG, :]).reshape(16, 16, 256)
            o = jnp.sum(o * pick_ref[...][None], axis=1)
            ref[pl.ds(pl.multiple_of(row * ROWS_OUT + T * 16, 16), 16), :] = o.astype(BF16)

        def leaving(i):
            d = 16 - i
            one_peer(syn, ahead(d), ahead(d))
            out_copy(T, d).start()

        loop(1, 16, leaving)
        one_peer(out_ref, me, me)

    analyse_part(0)
    analyse_part(1)
    total_part(0)
    analyse_part(2)
    total_part(1)
    synthesis_part(0)
    total_part(2)
    synthesis_part(1)
    synthesis_part(2)
    loop(1, 16, lambda d: in_copy(d).wait_send())
    for T in range(3):
        loop(1, 16, lambda d: out_copy(T, d).wait())

        def finish_lat(d):
            slab_copy(T, d).wait_send()
            coeff_copy(T, d).wait_send()

        loop(1, 8, finish_lat)


def main(heights, slots, cutoffs, panels, factors):
    t = tables()
    dma = pltpu.SemaphoreType.DMA
    vec = pltpu.VMEM
    hbm = pl.BlockSpec(memory_space=pl.ANY)
    return pl.pallas_call(
        main_kernel,
        out_shape=jax.ShapeDtypeStruct((16 * ROWS_OUT, 256), BF16),
        in_specs=[pl.BlockSpec(memory_space=pltpu.SMEM)] * 2 + [hbm] * 6 + [vmem()] * 3,
        out_specs=vmem(),
        scratch_shapes=[
            vec((CYC, LON), BF16),
            vec((192, 192), BF16),
            vec((192, 192), BF16),
            vec((2, HALF, 256), F32),
            vec((512, 256), BF16),
            vec((2, CYC * 192, 128), F32),
            vec((48 * 128, 128), F32),
            vec((TROWS, 128), F32),
            vec((5, 128, 128), F32),
            vec((16 * ROWS_IN, 384), BF16),
            vec((256, 320, DEG), BF16),
            vec((16 * ROWS_IN, 384), BF16),
            vec((20 * 128, DEG), F32),
            vec((640, DEG), F32),
            vec((640, DEG), F32),
            vec((640, DEG), BF16),
            vec((80, DEG), F32),
            vec((8 * DEG, 256), BF16),
            vec((16 * ROWS_OUT, 256), BF16),
            dma, dma((4,)), dma((16,)), dma((16,)), dma((16,)), dma((3, 8)), dma((3, 8)), dma((3, 8)), dma((3, 8)),
            dma((3, 16)), dma((3, 16)),
        ],
        compiler_params=pltpu.CompilerParams(
            vmem_limit_bytes=56 * MIB, collective_id=0, has_side_effects=True
        ),
        cost_estimate=pl.CostEstimate(flops=2 * 10**10, bytes_accessed=24 * 10**6, transcendentals=0),
        name="main",
    )(slots, cutoffs, heights, *t["first"], t["twist"], t["second"], panels, t["diag"], factors, t["pick"])


def inverse_kernel(slot_ref, msg_ref, back_ref, twist_ref, lh_ref, ll_ref, out_ref, ts, ls, ys):
    ts[0:8, :] = jnp.zeros((8, 128), F32)
    ts[ORDERS:TROWS, :] = jnp.zeros((TROWS - ORDERS, 128), F32)

    def one_peer(o, carry):
        for part in range(3):
            rows = msg_ref[pl.ds(pl.multiple_of(o * 48 + part * 16, 16), 16), :].astype(F32)
            count = 128 if part < 2 else 64
            t = jnp.concatenate([rows[:, :128], rows[:, 128:]], 0).T
            base = o * 320 + part * 128
            for i in range(count):
                ts[pl.ds(slot_ref[base + i] + 1, 1), 0:32] = t[i : i + 1]
        return carry

    lax.fori_loop(0, 16, one_peer, 0)

    def one_k(k, carry):
        stack = []
        for base in (0, 48):
            plus = ts[pl.ds(k + base, 32, stride=SLOW), :]
            minus = ts[pl.ds(SLOW - base - k, 32, stride=SLOW), :]
            lone = k == 0 if base == 0 else k == 90 - base
            stack += [plus, jnp.where(lone, 0.0, minus)]
        ls[pl.ds(k, 32, stride=48), :] = jnp.concatenate(stack, 0)[:, :32].T
        return carry

    lax.fori_loop(0, 48, one_k, 0, unroll=4)
    first = lax.broadcasted_iota(jnp.int32, (48, 128), 1) < 64

    def one_cycle(r, carry):
        l0 = ls[pl.ds(pl.multiple_of(r * 48, 48), 48), :]
        l1 = ls[pl.ds(pl.multiple_of((r + CYC) * 48, 48), 48), :]
        left = jnp.concatenate(
            [jnp.where(first, l0, pltpu.roll(l1, 64, 1)), jnp.where(first, pltpu.roll(l0, 64, 1), l1)], 0
        ).astype(BF16)
        w = dot(jnp.concatenate([left, left], 1), back_ref[...])
        re, im = w[:, :256], w[:, 256:]
        c, s = twist_ref[0], twist_ref[1]
        v = jnp.concatenate([re * c - im * s, im * c + re * s], 0).astype(BF16)
        field = dot(lh_ref[...], v) + dot(ll_ref[...], v)
        for lane in range(2):
            ys[lane, pl.ds(pl.multiple_of(r * 192, 192), 192), :] = field[:, lane * 128 : lane * 128 + 128]
        return carry

    lax.fori_loop(0, CYC, one_cycle, 0, unroll=2)
    for a in range(SLOW):
        v = jnp.concatenate([ys.at[lane][pl.ds(a, CYC, stride=192), :] for lane in range(2)], 1)
        out_ref[:, FAST * a : FAST * a + FAST] = v[:, :FAST]


def inverse(msg, slots):
    t = tables()
    return pl.pallas_call(
        inverse_kernel,
        out_shape=jax.ShapeDtypeStruct((CYC, LON), F32),
        in_specs=[pl.BlockSpec(memory_space=pltpu.SMEM)] + [vmem()] * 5,
        out_specs=vmem(),
        scratch_shapes=[
            pltpu.VMEM((TROWS, 128), F32),
            pltpu.VMEM((32 * 48, 128), F32),
            pltpu.VMEM((2, CYC * 192, 128), F32),
        ],
        compiler_params=pltpu.CompilerParams(vmem_limit_bytes=48 * MIB),
        name="inverse",
    )(slots, msg, t["back"], t["twist"], *t["last"])


def degrees():
    stride = (NMAX - ORDERS) // DEG
    return ORDERS + np.arange(DEG, dtype=np.int32) * stride


def factor_rows():
    degree = degrees().astype(np.float64)
    rows = np.zeros((2, 8, DEG), np.float32)
    for c in range(2):
        rows[c, 3 * c] = 1.0
        rows[c, 3 * c + 1] = (degree + 2.0) / (2.0 * NMAX)
        rows[c, 3 * c + 2] = (degree + 2.0) * (degree + 1.0) / (6.0 * NMAX * NMAX)
    return rows


def local(heights, panels, ord_slot, cutoffs):
    back = main(heights, ord_slot, cutoffs, panels, factor_rows())
    return inverse(back, ord_slot)


def solution(mesh):
    return jax.shard_map(
        local,
        mesh=mesh,
        in_specs=(P(("lat", "ord"), None), P("lat", "ord", None), P(), P("ord")),
        out_specs=P(("lat", "ord"), None),
        check_vma=False,
    )
```

```python
import functools
import math

import jax
import jax.numpy as jnp
import numpy as np
from jax import lax
from jax.experimental import pallas as pl
from jax.experimental.pallas import tpu as pltpu
from jax.sharding import PartitionSpec as P

LON = 43200
SLOW = 180
FAST = 240
HALF = 96
ORDERS = 5120
DEG = 128
NMAX = 21600
CYC = 16
TROWS = 6016
F32 = jnp.float32
BF16 = jnp.bfloat16
MIB = 1024 * 1024


def split16(table):
    high = table.astype(np.float32).astype(jnp.bfloat16)
    low = (table - high.astype(np.float64)).astype(np.float32).astype(jnp.bfloat16)
    return high, low


def angles(left, right, total):
    return 2.0 * np.pi / total * ((left[:, None] * right[None, :]) % total)


@functools.cache
def tables():
    k = np.arange(91)
    a = np.arange(SLOW)
    b = np.arange(FAST)
    q = np.arange(29)
    ka = angles(k, a, SLOW)
    first = np.zeros((2, HALF, 192))
    first[0, :91, :SLOW] = np.cos(ka)
    first[1, :91, :SLOW] = -np.sin(ka)
    first = first.reshape(2 * HALF, 192)
    kb = angles(k, b, LON)
    twist = np.zeros((2, HALF, 256), np.float32)
    twist[0, :91, :FAST] = np.cos(kb)
    twist[1, :91, :FAST] = np.sin(kb)
    bq = angles(b, q, FAST)
    bq1 = angles(b, q + 1, FAST)
    second = np.zeros((2, 256, 2, 128))
    second[0, :FAST, 0, 0:29] = np.cos(bq)
    second[1, :FAST, 0, 0:29] = np.sin(bq)
    second[0, :FAST, 1, 0:29] = -np.sin(bq)
    second[1, :FAST, 1, 0:29] = np.cos(bq)
    second[0, :FAST, 0, 32:61] = np.cos(bq1)
    second[1, :FAST, 0, 32:61] = -np.sin(bq1)
    second[0, :FAST, 1, 32:61] = -np.sin(bq1)
    second[1, :FAST, 1, 32:61] = -np.cos(bq1)
    second = second / math.sqrt(LON)
    high, low = split16(second[..., :64])
    second = np.concatenate([high, low], -1).reshape(512, 256)
    back = np.zeros((2, 2, 32, 2, 256))
    back[0, 0, :29, 0, :FAST] = np.cos(bq).T
    back[0, 0, :29, 1, :FAST] = np.sin(bq).T
    back[1, 0, :29, 0, :FAST] = -np.sin(bq).T
    back[1, 0, :29, 1, :FAST] = np.cos(bq).T
    back[0, 1, :29, 0, :FAST] = np.cos(bq1).T
    back[0, 1, :29, 1, :FAST] = -np.sin(bq1).T
    back[1, 1, :29, 0, :FAST] = -np.sin(bq1).T
    back[1, 1, :29, 1, :FAST] = -np.cos(bq1).T
    back = np.concatenate(split16(back.reshape(128, 512)), 0)
    last = np.zeros((192, 2, HALF))
    last[:SLOW, 0, :91] = np.cos(ka).T
    last[:SLOW, 1, :91] = -np.sin(ka).T
    last = last.reshape(192, 2 * HALF) * math.sqrt(2048 / (DEG * ORDERS))
    rows = np.arange(128)
    lanes = np.arange(256)
    diag = (lanes[None, :] % 16 == rows[:, None] // 8).astype(jnp.bfloat16)
    pick = (lanes[None, :] % 16 == np.arange(16)[:, None]).astype(np.float32)
    return dict(
        first=split16(first), twist=twist, second=second, back=back,
        last=split16(last), diag=diag, pick=pick,
    )


def swap_chunks(rows):
    rows = list(rows)
    chunk = lax.broadcasted_iota(jnp.int32, (8, 128), 1) // 16
    for d in (4, 2, 1):
        low = (chunk & d) == 0
        new = list(rows)
        for r in range(8):
            if r & d:
                continue
            new[r] = jnp.where(low, rows[r], pltpu.roll(rows[r + d], d * 16, 1))
            new[r + d] = jnp.where(low, pltpu.roll(rows[r], 128 - d * 16, 1), rows[r + d])
        rows = new
    return rows


def dot(left, right):
    return jnp.dot(left, right, preferred_element_type=F32)


def halves(value):
    high = value.astype(BF16)
    return high, (value - high.astype(F32)).astype(BF16)


def vmem():
    return pl.BlockSpec(memory_space=pltpu.VMEM)


MESH = pl.DeviceIdType.MESH
ROWS_IN = 80
ROWS_OUT = 48
SLAB = 80


def main_kernel(slot_ref, cut_ref, x_hbm, fh_hbm, fl_hbm, twist_hbm, second_hbm, panel_ref, diag_ref,
                factor_ref, pick_ref, out_ref,
                x_ref, fh_ref, fl_ref, twist_ref, second_ref, xs, qs, ts, gs, msg_ref,
                pan, got, acc, mine, parts, coeff, keeps, wide, syn,
                xsem, tsem, psem, s1, r1, s2, r2, s3, r3, s4, r4):
    lat = lax.axis_index("lat")
    me = lax.axis_index("ord")
    hy, hz, hc = me // 8, me // 2 % 4, me % 2

    def ahead(d):
        return (hy + d // 8) % 2 * 8 + (hz + d // 2 % 4) % 4 * 2 + (hc + d % 2) % 2

    def behind(d):
        return (hy + 2 - d // 8) % 2 * 8 + (hz + 4 - d // 2 % 4) % 4 * 2 + (hc + 2 - d % 2) % 2

    def panel_copy(d):
        place = pl.ds(pl.multiple_of(behind(d) * 16, 16), 16)
        return pltpu.make_async_copy(panel_ref.at[place], pan.at[place], psem.at[d])

    def in_copy(d):
        return pltpu.make_async_remote_copy(
            src_ref=msg_ref.at[pl.ds(pl.multiple_of(ahead(d) * ROWS_IN, 16), ROWS_IN)],
            dst_ref=got.at[pl.ds(pl.multiple_of(me * ROWS_IN, 16), ROWS_IN)],
            send_sem=s1.at[d], recv_sem=r1.at[d],
            device_id=(lat, ahead(d)), device_id_type=MESH,
        )

    base = (0, 256, 512)
    share = (32, 32, 16)

    def slab_copy(T, d):
        peer = (lat + d) % 8
        size = share[T]
        return pltpu.make_async_remote_copy(
            src_ref=mine.at[pl.ds(pl.multiple_of(base[T] + peer * size, 16), size)],
            dst_ref=parts.at[pl.ds(pl.multiple_of(base[T] + lat * size, 16), size)],
            send_sem=s2.at[T, d], recv_sem=r2.at[T, d],
            device_id=(peer, me), device_id_type=MESH,
        )

    def coeff_copy(T, d):
        peer = (lat + d) % 8
        place = pl.ds(pl.multiple_of(base[T] + lat * share[T], 16), share[T])
        return pltpu.make_async_remote_copy(
            src_ref=coeff.at[place], dst_ref=coeff.at[place],
            send_sem=s3.at[T, d], recv_sem=r3.at[T, d],
            device_id=(peer, me), device_id_type=MESH,
        )

    def out_copy(T, d):
        return pltpu.make_async_remote_copy(
            src_ref=syn.at[pl.ds(pl.multiple_of(ahead(d) * ROWS_OUT + T * 16, 16), 16)],
            dst_ref=out_ref.at[pl.ds(pl.multiple_of(me * ROWS_OUT + T * 16, 16), 16)],
            send_sem=s4.at[T, d], recv_sem=r4.at[T, d],
            device_id=(lat, ahead(d)), device_id_type=MESH,
        )

    def loop(low, high, body):
        def step(d, carry):
            body(d)
            return carry
        lax.fori_loop(low, high, step, 0)

    heights_copy = pltpu.make_async_copy(x_hbm, x_ref, xsem)
    heights_copy.start()
    held = ((fh_hbm, fh_ref), (fl_hbm, fl_ref), (twist_hbm, twist_ref), (second_hbm, second_ref))

    def table_copy(i):
        return pltpu.make_async_copy(held[i][0], held[i][1], tsem.at[i])

    for i in range(4):
        table_copy(i).start()
    barrier = pltpu.get_barrier_semaphore()
    loop(1, 16, lambda d: pl.semaphore_signal(barrier, inc=1, device_id=(lat, ahead(d)), device_id_type=MESH))
    loop(1, 8, lambda d: pl.semaphore_signal(barrier, inc=1, device_id=((lat + d) % 8, me), device_id_type=MESH))
    degree = ORDERS + (NMAX - ORDERS) // DEG * lax.broadcasted_iota(jnp.int32, (1, DEG), 1)
    for T in range(3):
        size = share[T]
        for i in range(size):
            slot = T * 128 + (lat * size + i) % (4 * size)
            row = T * 32 + i
            keeps[row : row + 1, :] = jnp.where(degree <= cut_ref[slot], 1.0, 0.0)
    heights_copy.wait()
    inside = lax.broadcasted_iota(jnp.int32, (CYC, 256), 1) < FAST
    for r in range(CYC):
        for lane in range(2):
            xs[lane, r * 192 + 176 : r * 192 + 192, :] = jnp.zeros((16, 128), F32)
    for a in range(SLOW):
        start = FAST * a // 128 * 128
        off = FAST * a - start
        if start + 384 <= LON:
            v = x_ref[:, start : start + 384].astype(F32)
        else:
            v = jnp.concatenate(
                [x_ref[:, start:LON].astype(F32), jnp.zeros((CYC, start + 384 - LON), F32)], 1
            )
        if off:
            v = pltpu.roll(v, 384 - off, 1)
        v = jnp.where(inside, v[:, :256], 0.0)
        for lane in range(2):
            xs.at[lane][pl.ds(a, CYC, stride=192), :] = v[:, lane * 128 : lane * 128 + 128]

    first = lax.broadcasted_iota(jnp.int32, (48, 128), 1) < 64

    def one_cycle(r, carry):
        rows = pl.ds(pl.multiple_of(r * 192, 192), 192)
        level = jnp.concatenate([xs[0, rows, :], xs[1, rows, :]], 1)
        value = level
        stack = []
        tc, tsin = twist_ref[0], twist_ref[1]
        for p in range(3):
            if p:
                value = value * level
            if p == 0:
                high = value.astype(BF16)
                y = dot(fh_ref[...], high) + dot(fl_ref[...], high)
            else:
                high, low = halves(value)
                y = dot(fh_ref[...], high) + dot(fl_ref[...], high) + dot(fh_ref[...], low)
            re, im = y[:HALF], y[HALF:]
            stack += list(halves(jnp.concatenate([re * tc + im * tsin, im * tc - re * tsin], 1)))
        o = dot(jnp.concatenate(stack, 0), second_ref[...])
        for p in range(3):
            both = o[p * 192 : p * 192 + HALF] + o[p * 192 + HALF : p * 192 + 192]
            for c in range(2):
                part = both[:, c * 128 : c * 128 + 128]
                part = part + pltpu.roll(part, 64, 1)
                qs[pl.ds(r * 8 + c * 3 + p, 48, stride=128), :] = jnp.where(first, part[:48], part[48:])
        return carry

    for i in range(4):
        table_copy(i).wait()
    loop(0, 16, lambda d: panel_copy(d).start())
    lax.fori_loop(0, CYC, one_cycle, 0, unroll=2)

    def one_k(k, carry):
        t = qs[pl.ds(k * 128 if isinstance(k, int) else pl.multiple_of(k * 128, 128), 128), :].T
        ts[pl.ds(k, 32, stride=SLOW), :] = t[0:32]
        ts[pl.ds(SLOW - k, 32, stride=SLOW), :] = t[32:64]
        return t

    def two_k(k, carry):
        t = one_k(k, carry)
        ts[pl.ds(k + 48, 32, stride=SLOW), :] = t[64:96]
        ts[pl.ds(SLOW - 48 - k, 32, stride=SLOW), :] = t[96:128]
        return carry

    lax.fori_loop(0, 40, two_k, 0, unroll=4)
    for k in range(40, 43):
        two_k(k, 0)
    for k in range(43, 48):
        one_k(k, 0)

    pl.semaphore_wait(barrier, 22)

    sub = lax.broadcasted_iota(jnp.int32, (8, 128), 0)

    def one_chip(i, carry):
        far = 7 - i // 2 - i % 2 * 4
        chip = (hy + far // 4) % 2 * 4 + (hz + far % 4) % 4
        for j in range(5):
            tile = chip * 5 + j
            for i in range(0, 128, 32):
                rows = [ts[pl.ds(slot_ref[tile * 128 + i + e] + 1, 1), :] for e in range(32)]
                for e in range(32):
                    gs[j, i + e : i + e + 1, :] = rows[e]
            t = gs[j].T
            sides = [swap_chunks([t[(h * 8 + r) * 8 : (h * 8 + r + 1) * 8] for r in range(8)]) for h in range(2)]
            rows = []
            for u in (0, 4):
                for side in sides:
                    rows.append(
                        jnp.concatenate(
                            [jnp.where(sub < 6, side[u + v], pltpu.roll(side[u + 3], 6 - 2 * v, 0)) for v in range(3)], 1
                        )
                    )
            msg_ref[pl.ds(pl.multiple_of(tile * 32, 32), 32), :] = jnp.concatenate(rows, 0).astype(BF16)

        @pl.when(far > 0)
        def _():
            in_copy(far * 2).start()

        in_copy(far * 2 + 1).start()
        return carry

    lax.fori_loop(0, 8, one_chip, 0)
    own_in = pl.ds(pl.multiple_of(me * ROWS_IN, 16), ROWS_IN)
    got[own_in, :] = msg_ref[own_in, :]
    loop(0, 16, lambda d: panel_copy(d).wait())
    def contract(q, far_set):
        sums = []
        for pair in range(2):
            accs = [None, None]
            for d in far_set:
                peer = behind(d)
                rows = got[pl.ds(pl.multiple_of(peer * ROWS_IN + q * 16, 16), 16), :].astype(F32)
                for e in range(2):
                    v = pair * 2 + e
                    sides = []
                    for h in (0, 8):
                        if v < 3:
                            sides.append(rows[h : h + 8, v * 128 : v * 128 + 128])
                        else:
                            x, y, z = (
                                pltpu.roll(rows[h : h + 8, w * 128 : w * 128 + 128], 2 + 2 * w, 0) for w in range(3)
                            )
                            sides.append(jnp.where(sub < 2, x, jnp.where(sub < 4, y, z)))
                    one = jnp.concatenate(sides, 1)
                    two = jnp.concatenate([one, one], 0).astype(BF16)
                    left = jnp.concatenate([two] * 8, 0) * diag_ref[...]
                    right = pan[
                        pl.ds(pl.multiple_of(peer * 16, 16), 16), pl.ds(pl.multiple_of(q * 64 + v * 16, 16), 16), :
                    ].reshape(256, DEG)
                    t = dot(left, right)
                    accs[e] = t if accs[e] is None else accs[e] + t
            sums += accs
        return sums

    early = (14, 15, 6, 7, 12, 13, 4, 5)
    late = (10, 11, 2, 3, 8, 9, 0, 1)

    def first_half(q):
        for v, t in enumerate(contract(q, early)):
            acc[pl.ds(pl.multiple_of(q * 512 + v * 128, 128), 128), :] = t

    def second_half(T, q):
        for v, t in enumerate(contract(q, late)):
            t = t + acc[pl.ds(pl.multiple_of(q * 512 + v * 128, 128), 128), :]
            rows = t.reshape(16, 8, DEG)
            for c in range(2):
                row = base[T] + c * 4 * share[T] + (q - 2 * T) * 64 + v * 16
                mine[pl.ds(pl.multiple_of(row, 16), 16), :] = jnp.sum(rows * factor_ref[c][None], axis=1)

    for d in early:
        in_copy(d).wait_recv()
    loop(0, 5, first_half)
    for d in late:
        if d:
            in_copy(d).wait_recv()

    def analyse_part(T):
        loop(2 * T, min(2 * T + 2, 5), lambda q: second_half(T, q))
        loop(1, 8, lambda d: slab_copy(T, d).start())

    def total_part(T):
        size = share[T]
        own = pl.ds(pl.multiple_of(base[T] + lat * size, 16), size)
        total = mine[own, :]
        for d in range(1, 8):
            slab_copy(T, d).wait_recv()
            total = total + parts[pl.ds(pl.multiple_of(base[T] + (lat + 8 - d) % 8 * size, 16), size), :]
        coeff[own, :] = (total * keeps[T * 32 : T * 32 + size, :]).astype(BF16)
        loop(1, 8, lambda d: coeff_copy(T, d).start())

    chunk = lax.broadcasted_iota(jnp.int32, (DEG, 128), 1) // 16

    def synthesis_part(T):
        groups = share[T] // 4
        loop(1, 8, lambda d: coeff_copy(T, d).wait_recv())
        for c in range(2):
            rows = coeff[base[T] + c * groups * 16 : base[T] + (c + 1) * groups * 16, :].astype(F32)
            if groups < 8:
                rows = jnp.concatenate([rows, jnp.zeros((128 - groups * 16, DEG), F32)], 0)
            turned = rows.T
            for g in range(groups):
                wide[g * DEG : g * DEG + DEG, c * 128 : c * 128 + 128] = jnp.where(
                    chunk == g, turned, 0.0
                ).astype(BF16)

        def two_peers(d, refs):
            left = jnp.concatenate(
                [
                    jnp.concatenate(
                        [
                            pan[
                                pl.ds(pl.multiple_of(ahead(d + e) * 16, 16), 16),
                                T * 128 + g * 16 : T * 128 + g * 16 + 16, :
                            ].reshape(256, DEG)
                            for g in range(groups)
                        ],
                        1,
                    )
                    for e in range(2)
                ],
                0,
            )
            o = dot(left, wide[: groups * DEG, :]).reshape(32, 16, 256)
            o = jnp.sum(o * pick_ref[...][None], axis=1)
            for e in range(2):
                place = pl.ds(pl.multiple_of(ahead(d + e) * ROWS_OUT + T * 16, 16), 16)
                refs[e][place, :] = o[e * 16 : e * 16 + 16].astype(BF16)

        def leaving(i):
            d = 16 - 2 * i
            two_peers(d, (syn, syn))
            out_copy(T, d).start()
            out_copy(T, d + 1).start()

        loop(1, 8, leaving)
        two_peers(0, (out_ref, syn))
        out_copy(T, 1).start()

    analyse_part(0)
    analyse_part(1)
    total_part(0)
    analyse_part(2)
    total_part(1)
    synthesis_part(0)
    total_part(2)
    synthesis_part(1)
    synthesis_part(2)
    loop(1, 16, lambda d: in_copy(d).wait_send())
    for T in range(3):
        loop(1, 16, lambda d: out_copy(T, d).wait())

        def finish_lat(d):
            slab_copy(T, d).wait_send()
            coeff_copy(T, d).wait_send()

        loop(1, 8, finish_lat)


def main(heights, slots, cutoffs, panels, factors):
    t = tables()
    dma = pltpu.SemaphoreType.DMA
    vec = pltpu.VMEM
    hbm = pl.BlockSpec(memory_space=pl.ANY)
    return pl.pallas_call(
        main_kernel,
        out_shape=jax.ShapeDtypeStruct((16 * ROWS_OUT, 256), BF16),
        in_specs=[pl.BlockSpec(memory_space=pltpu.SMEM)] * 2 + [hbm] * 6 + [vmem()] * 3,
        out_specs=vmem(),
        scratch_shapes=[
            vec((CYC, LON), BF16),
            vec((192, 192), BF16),
            vec((192, 192), BF16),
            vec((2, HALF, 256), F32),
            vec((512, 256), BF16),
            vec((2, CYC * 192, 128), F32),
            vec((48 * 128, 128), F32),
            vec((TROWS, 128), F32),
            vec((5, 128, 128), F32),
            vec((16 * ROWS_IN, 384), BF16),
            vec((256, 320, DEG), BF16),
            vec((16 * ROWS_IN, 384), BF16),
            vec((20 * 128, DEG), F32),
            vec((640, DEG), F32),
            vec((640, DEG), F32),
            vec((640, DEG), BF16),
            vec((80, DEG), F32),
            vec((8 * DEG, 256), BF16),
            vec((16 * ROWS_OUT, 256), BF16),
            dma, dma((4,)), dma((16,)), dma((16,)), dma((16,)), dma((3, 8)), dma((3, 8)), dma((3, 8)), dma((3, 8)),
            dma((3, 16)), dma((3, 16)),
        ],
        compiler_params=pltpu.CompilerParams(
            vmem_limit_bytes=56 * MIB, collective_id=0, has_side_effects=True
        ),
        cost_estimate=pl.CostEstimate(flops=2 * 10**10, bytes_accessed=24 * 10**6, transcendentals=0),
        name="main",
    )(slots, cutoffs, heights, *t["first"], t["twist"], t["second"], panels, t["diag"], factors, t["pick"])


def inverse_kernel(slot_ref, msg_ref, back_hbm, twist_hbm, lh_hbm, ll_hbm, out_hbm,
                   back_ref, twist_ref, lh_ref, ll_ref, out_ref, ts, ls, ys, tsem, osem):
    held = ((back_hbm, back_ref), (twist_hbm, twist_ref), (lh_hbm, lh_ref), (ll_hbm, ll_ref))
    copies = [pltpu.make_async_copy(held[i][0], held[i][1], tsem.at[i]) for i in range(4)]
    for copy in copies:
        copy.start()
    ts[0:8, :] = jnp.zeros((8, 128), F32)
    ts[ORDERS:TROWS, :] = jnp.zeros((TROWS - ORDERS, 128), F32)

    def one_peer(o, carry):
        for part in range(3):
            rows = msg_ref[pl.ds(pl.multiple_of(o * 48 + part * 16, 16), 16), :].astype(F32)
            count = 128 if part < 2 else 64
            t = jnp.concatenate([rows[:, :128], rows[:, 128:]], 0).T
            base = o * 320 + part * 128
            for i in range(count):
                ts[pl.ds(slot_ref[base + i] + 1, 1), 0:32] = t[i : i + 1]
        return carry

    lax.fori_loop(0, 16, one_peer, 0)

    def one_k(k, carry):
        stack = []
        for base in (0, 48):
            plus = ts[pl.ds(k + base, 32, stride=SLOW), :]
            minus = ts[pl.ds(SLOW - base - k, 32, stride=SLOW), :]
            lone = k == 0 if base == 0 else k == 90 - base
            stack += [plus, jnp.where(lone, 0.0, minus)]
        ls[pl.ds(k, 32, stride=48), :] = jnp.concatenate(stack, 0)[:, :32].T
        return carry

    lax.fori_loop(0, 48, one_k, 0, unroll=4)
    first = lax.broadcasted_iota(jnp.int32, (48, 128), 1) < 64

    def four_cycles(step, carry):
        lefts = []
        for i in range(4):
            r = step * 4 + i
            l0 = ls[pl.ds(pl.multiple_of(r * 48, 48), 48), :]
            l1 = ls[pl.ds(pl.multiple_of((r + CYC) * 48, 48), 48), :]
            lefts += [jnp.where(first, l0, pltpu.roll(l1, 64, 1)), jnp.where(first, pltpu.roll(l0, 64, 1), l1)]
        left = jnp.concatenate(lefts, 0).astype(BF16)
        w = dot(jnp.concatenate([left, left], 1), back_ref[...])
        c, s = twist_ref[0], twist_ref[1]
        for i in range(4):
            re, im = w[i * HALF : i * HALF + HALF, :256], w[i * HALF : i * HALF + HALF, 256:]
            v = jnp.concatenate([re * c - im * s, im * c + re * s], 0).astype(BF16)
            field = dot(lh_ref[...], v) + dot(ll_ref[...], v)
            for lane in range(2):
                ys[lane, pl.ds(pl.multiple_of((step * 4 + i) * 192, 192), 192), :] = field[
                    :, lane * 128 : lane * 128 + 128
                ]
        return carry

    for copy in copies:
        copy.wait()
    lax.fori_loop(0, 4, four_cycles, 0)
    leaving = []
    for a in range(SLOW):
        v = jnp.concatenate([ys.at[lane][pl.ds(a, CYC, stride=192), :] for lane in range(2)], 1)
        out_ref[:, FAST * a : FAST * a + FAST] = v[:, :FAST]
        if a % 48 == 47 or a == SLOW - 1:
            place = slice(FAST * (a // 48 * 48), FAST * a + FAST)
            leaving.append(pltpu.make_async_copy(out_ref.at[:, place], out_hbm.at[:, place], osem.at[a // 48]))
            leaving[-1].start()
    for copy in leaving:
        copy.wait()


def inverse(msg, slots):
    t = tables()
    return pl.pallas_call(
        inverse_kernel,
        out_shape=jax.ShapeDtypeStruct((CYC, LON), F32),
        in_specs=[pl.BlockSpec(memory_space=pltpu.SMEM), vmem()] + [pl.BlockSpec(memory_space=pl.ANY)] * 4,
        out_specs=pl.BlockSpec(memory_space=pl.ANY),
        scratch_shapes=[
            pltpu.VMEM((256, 512), BF16),
            pltpu.VMEM((2, HALF, 256), F32),
            pltpu.VMEM((192, 192), BF16),
            pltpu.VMEM((192, 192), BF16),
            pltpu.VMEM((CYC, LON), F32),
            pltpu.VMEM((TROWS, 128), F32),
            pltpu.VMEM((32 * 48, 128), F32),
            pltpu.VMEM((2, CYC * 192, 128), F32),
            pltpu.SemaphoreType.DMA((4,)),
            pltpu.SemaphoreType.DMA((4,)),
        ],
        compiler_params=pltpu.CompilerParams(vmem_limit_bytes=48 * MIB),
        name="inverse",
    )(slots, msg, t["back"], t["twist"], *t["last"])


def degrees():
    stride = (NMAX - ORDERS) // DEG
    return ORDERS + np.arange(DEG, dtype=np.int32) * stride


def factor_rows():
    degree = degrees().astype(np.float64)
    rows = np.zeros((2, 8, DEG), np.float32)
    for c in range(2):
        rows[c, 3 * c] = 1.0
        rows[c, 3 * c + 1] = (degree + 2.0) / (2.0 * NMAX)
        rows[c, 3 * c + 2] = (degree + 2.0) * (degree + 1.0) / (6.0 * NMAX * NMAX)
    return rows


def local(heights, panels, ord_slot, cutoffs):
    back = main(heights, ord_slot, cutoffs, panels, factor_rows())
    return inverse(back, ord_slot)


def solution(mesh):
    return jax.shard_map(
        local,
        mesh=mesh,
        in_specs=(P(("lat", "ord"), None), P("lat", "ord", None), P(), P("ord")),
        out_specs=P(("lat", "ord"), None),
        check_vma=False,
    )
```

```python
import functools
import math

import jax
import jax.numpy as jnp
import numpy as np
from jax import lax
from jax.experimental import pallas as pl
from jax.experimental.pallas import tpu as pltpu
from jax.sharding import PartitionSpec as P

LON = 43200
SLOW = 180
FAST = 240
HALF = 96
ORDERS = 5120
DEG = 128
NMAX = 21600
CYC = 16
TROWS = 6016
F32 = jnp.float32
BF16 = jnp.bfloat16
MIB = 1024 * 1024


def split16(table):
    high = table.astype(np.float32).astype(jnp.bfloat16)
    low = (table - high.astype(np.float64)).astype(np.float32).astype(jnp.bfloat16)
    return high, low


def angles(left, right, total):
    return 2.0 * np.pi / total * ((left[:, None] * right[None, :]) % total)


@functools.cache
def tables():
    k = np.arange(91)
    a = np.arange(SLOW)
    b = np.arange(FAST)
    q = np.arange(29)
    ka = angles(k, a, SLOW)
    first = np.zeros((2, HALF, 192))
    first[0, :91, :SLOW] = np.cos(ka)
    first[1, :91, :SLOW] = -np.sin(ka)
    first = first.reshape(2 * HALF, 192)
    kb = angles(k, b, LON)
    twist = np.zeros((2, HALF, 256), np.float32)
    twist[0, :91, :FAST] = np.cos(kb)
    twist[1, :91, :FAST] = np.sin(kb)
    bq = angles(b, q, FAST)
    bq1 = angles(b, q + 1, FAST)
    second = np.zeros((2, 256, 2, 128))
    second[0, :FAST, 0, 0:29] = np.cos(bq)
    second[1, :FAST, 0, 0:29] = np.sin(bq)
    second[0, :FAST, 1, 0:29] = -np.sin(bq)
    second[1, :FAST, 1, 0:29] = np.cos(bq)
    second[0, :FAST, 0, 32:61] = np.cos(bq1)
    second[1, :FAST, 0, 32:61] = -np.sin(bq1)
    second[0, :FAST, 1, 32:61] = -np.sin(bq1)
    second[1, :FAST, 1, 32:61] = -np.cos(bq1)
    second = second / math.sqrt(LON)
    high, low = split16(second[..., :64])
    second = np.concatenate([high, low], -1).reshape(512, 256)
    back = np.zeros((2, 2, 32, 2, 256))
    back[0, 0, :29, 0, :FAST] = np.cos(bq).T
    back[0, 0, :29, 1, :FAST] = np.sin(bq).T
    back[1, 0, :29, 0, :FAST] = -np.sin(bq).T
    back[1, 0, :29, 1, :FAST] = np.cos(bq).T
    back[0, 1, :29, 0, :FAST] = np.cos(bq1).T
    back[0, 1, :29, 1, :FAST] = -np.sin(bq1).T
    back[1, 1, :29, 0, :FAST] = -np.sin(bq1).T
    back[1, 1, :29, 1, :FAST] = -np.cos(bq1).T
    back = np.concatenate(split16(back.reshape(128, 512)), 0)
    last = np.zeros((192, 2, HALF))
    last[:SLOW, 0, :91] = np.cos(ka).T
    last[:SLOW, 1, :91] = -np.sin(ka).T
    last = last.reshape(192, 2 * HALF) * math.sqrt(2048 / (DEG * ORDERS))
    rows = np.arange(128)
    lanes = np.arange(256)
    diag = (lanes[None, :] % 16 == rows[:, None] // 8).astype(jnp.bfloat16)
    pick = (lanes[None, :] % 16 == np.arange(16)[:, None]).astype(np.float32)
    return dict(
        first=split16(first), twist=twist, second=second, back=back,
        last=split16(last), diag=diag, pick=pick,
    )


def swap_chunks(rows):
    rows = list(rows)
    chunk = lax.broadcasted_iota(jnp.int32, (8, 128), 1) // 16
    for d in (4, 2, 1):
        low = (chunk & d) == 0
        new = list(rows)
        for r in range(8):
            if r & d:
                continue
            new[r] = jnp.where(low, rows[r], pltpu.roll(rows[r + d], d * 16, 1))
            new[r + d] = jnp.where(low, pltpu.roll(rows[r], 128 - d * 16, 1), rows[r + d])
        rows = new
    return rows


def dot(left, right):
    return jnp.dot(left, right, preferred_element_type=F32)


def halves(value):
    high = value.astype(BF16)
    return high, (value - high.astype(F32)).astype(BF16)


def vmem():
    return pl.BlockSpec(memory_space=pltpu.VMEM)


MESH = pl.DeviceIdType.MESH
ROWS_IN = 80
ROWS_OUT = 48
SLAB = 80


def main_kernel(slot_ref, cut_ref, x_hbm, fh_hbm, fl_hbm, twist_hbm, second_hbm, panel_ref, diag_ref,
                factor_ref, pick_ref, out_ref,
                x_ref, fh_ref, fl_ref, twist_ref, second_ref, xs, qs, ts, gs, msg_ref,
                pan, got, mine, parts, coeff, keeps, wide, syn,
                xsem, tsem, psem, s1, r1, s2, r2, s3, r3, s4, r4):
    lat = lax.axis_index("lat")
    me = lax.axis_index("ord")
    hy, hz, hc = me // 8, me // 2 % 4, me % 2

    def ahead(d):
        return (hy + d // 8) % 2 * 8 + (hz + d // 2 % 4) % 4 * 2 + (hc + d % 2) % 2

    def behind(d):
        return (hy + 2 - d // 8) % 2 * 8 + (hz + 4 - d // 2 % 4) % 4 * 2 + (hc + 2 - d % 2) % 2

    def panel_copy(d):
        place = pl.ds(pl.multiple_of(behind(d) * 16, 16), 16)
        return pltpu.make_async_copy(panel_ref.at[place], pan.at[place], psem.at[d])

    base = (0, 256, 512)
    share = (32, 32, 16)

    def in_copy(T, d):
        size = share[T]
        return pltpu.make_async_remote_copy(
            src_ref=msg_ref.at[pl.ds(pl.multiple_of(ahead(d) * ROWS_IN + T * 32, 16), size)],
            dst_ref=got.at[pl.ds(pl.multiple_of(me * ROWS_IN + T * 32, 16), size)],
            send_sem=s1.at[T, d], recv_sem=r1.at[T, d],
            device_id=(lat, ahead(d)), device_id_type=MESH,
        )

    def slab_copy(T, d):
        peer = (lat + d) % 8
        size = share[T]
        return pltpu.make_async_remote_copy(
            src_ref=mine.at[pl.ds(pl.multiple_of(base[T] + peer * size, 16), size)],
            dst_ref=parts.at[pl.ds(pl.multiple_of(base[T] + lat * size, 16), size)],
            send_sem=s2.at[T, d], recv_sem=r2.at[T, d],
            device_id=(peer, me), device_id_type=MESH,
        )

    def coeff_copy(T, d):
        peer = (lat + d) % 8
        place = pl.ds(pl.multiple_of(base[T] + lat * share[T], 16), share[T])
        return pltpu.make_async_remote_copy(
            src_ref=coeff.at[place], dst_ref=coeff.at[place],
            send_sem=s3.at[T, d], recv_sem=r3.at[T, d],
            device_id=(peer, me), device_id_type=MESH,
        )

    def out_copy(T, d):
        return pltpu.make_async_remote_copy(
            src_ref=syn.at[pl.ds(pl.multiple_of(ahead(d) * ROWS_OUT + T * 16, 16), 16)],
            dst_ref=out_ref.at[pl.ds(pl.multiple_of(me * ROWS_OUT + T * 16, 16), 16)],
            send_sem=s4.at[T, d], recv_sem=r4.at[T, d],
            device_id=(lat, ahead(d)), device_id_type=MESH,
        )

    def loop(low, high, body):
        def step(d, carry):
            body(d)
            return carry
        lax.fori_loop(low, high, step, 0)

    heights_copy = pltpu.make_async_copy(x_hbm, x_ref, xsem)
    heights_copy.start()
    held = ((fh_hbm, fh_ref), (fl_hbm, fl_ref), (twist_hbm, twist_ref), (second_hbm, second_ref))

    def table_copy(i):
        return pltpu.make_async_copy(held[i][0], held[i][1], tsem.at[i])

    for i in range(4):
        table_copy(i).start()
    barrier = pltpu.get_barrier_semaphore()
    loop(1, 16, lambda d: pl.semaphore_signal(barrier, inc=1, device_id=(lat, ahead(d)), device_id_type=MESH))
    loop(1, 8, lambda d: pl.semaphore_signal(barrier, inc=1, device_id=((lat + d) % 8, me), device_id_type=MESH))
    degree = ORDERS + (NMAX - ORDERS) // DEG * lax.broadcasted_iota(jnp.int32, (1, DEG), 1)
    for T in range(3):
        size = share[T]
        for i in range(size):
            slot = T * 128 + (lat * size + i) % (4 * size)
            row = T * 32 + i
            keeps[row : row + 1, :] = jnp.where(degree <= cut_ref[slot], 1.0, 0.0)
    heights_copy.wait()
    inside = lax.broadcasted_iota(jnp.int32, (CYC, 256), 1) < FAST
    for r in range(CYC):
        for lane in range(2):
            xs[lane, r * 192 + 176 : r * 192 + 192, :] = jnp.zeros((16, 128), F32)
    for a in range(SLOW):
        start = FAST * a // 128 * 128
        off = FAST * a - start
        if start + 384 <= LON:
            v = x_ref[:, start : start + 384].astype(F32)
        else:
            v = jnp.concatenate(
                [x_ref[:, start:LON].astype(F32), jnp.zeros((CYC, start + 384 - LON), F32)], 1
            )
        if off:
            v = pltpu.roll(v, 384 - off, 1)
        v = jnp.where(inside, v[:, :256], 0.0)
        for lane in range(2):
            xs.at[lane][pl.ds(a, CYC, stride=192), :] = v[:, lane * 128 : lane * 128 + 128]

    first = lax.broadcasted_iota(jnp.int32, (48, 128), 1) < 64

    def one_cycle(r, carry):
        rows = pl.ds(pl.multiple_of(r * 192, 192), 192)
        level = jnp.concatenate([xs[0, rows, :], xs[1, rows, :]], 1)
        value = level
        stack = []
        tc, tsin = twist_ref[0], twist_ref[1]
        for p in range(3):
            if p:
                value = value * level
            if p == 0:
                high = value.astype(BF16)
                y = dot(fh_ref[...], high) + dot(fl_ref[...], high)
            else:
                high, low = halves(value)
                y = dot(fh_ref[...], high) + dot(fl_ref[...], high) + dot(fh_ref[...], low)
            re, im = y[:HALF], y[HALF:]
            stack += list(halves(jnp.concatenate([re * tc + im * tsin, im * tc - re * tsin], 1)))
        o = dot(jnp.concatenate(stack, 0), second_ref[...])
        for p in range(3):
            both = o[p * 192 : p * 192 + HALF] + o[p * 192 + HALF : p * 192 + 192]
            for c in range(2):
                part = both[:, c * 128 : c * 128 + 128]
                part = part + pltpu.roll(part, 64, 1)
                qs[pl.ds(r * 8 + c * 3 + p, 48, stride=128), :] = jnp.where(first, part[:48], part[48:])
        return carry

    for i in range(4):
        table_copy(i).wait()
    loop(0, 16, lambda d: panel_copy(d).start())
    lax.fori_loop(0, CYC, one_cycle, 0, unroll=4)

    def one_k(k, carry):
        t = qs[pl.ds(k * 128 if isinstance(k, int) else pl.multiple_of(k * 128, 128), 128), :].T
        ts[pl.ds(k, 32, stride=SLOW), :] = t[0:32]
        ts[pl.ds(SLOW - k, 32, stride=SLOW), :] = t[32:64]
        return t

    def two_k(k, carry):
        t = one_k(k, carry)
        ts[pl.ds(k + 48, 32, stride=SLOW), :] = t[64:96]
        ts[pl.ds(SLOW - 48 - k, 32, stride=SLOW), :] = t[96:128]
        return carry

    lax.fori_loop(0, 40, two_k, 0, unroll=4)
    for k in range(40, 43):
        two_k(k, 0)
    for k in range(43, 48):
        one_k(k, 0)

    pl.semaphore_wait(barrier, 22)

    sub = lax.broadcasted_iota(jnp.int32, (8, 128), 0)

    def chip_of(i):
        far = 7 - i // 2 - i % 2 * 4
        return far, (hy + far // 4) % 2 * 4 + (hz + far % 4) % 4

    def gathered(j, starts):
        for i in range(0, 128, 32):
            at = starts[i // 64] + i % 64
            rows = [ts[pl.ds(slot_ref[at + e] + 1, 1), :] for e in range(32)]
            for e in range(32):
                gs[j, i + e : i + e + 1, :] = rows[e]
        t = gs[j].T
        sides = [swap_chunks([t[(h * 8 + r) * 8 : (h * 8 + r + 1) * 8] for r in range(8)]) for h in range(2)]
        blocks = []
        for u in (0, 4):
            packed = [
                jnp.concatenate(
                    [jnp.where(sub < 6, side[u + v], pltpu.roll(side[u + 3], 6 - 2 * v, 0)) for v in range(3)], 1
                )
                for side in sides
            ]
            blocks.append(jnp.concatenate(packed, 0).astype(BF16))
        return blocks

    def send(T, far):
        @pl.when(far > 0)
        def _():
            in_copy(T, far * 2).start()

        in_copy(T, far * 2 + 1).start()

    for T in range(2):
        def two_chips(step, carry):
            for e in range(2):
                far, chip = chip_of(step * 2 + e)
                for j in range(2):
                    to = chip * 2 + j
                    start = to * 320 + T * 128
                    blocks = gathered(e * 2 + j, (start, start + 64))
                    msg_ref[pl.ds(pl.multiple_of(to * ROWS_IN + T * 32, 16), 32), :] = jnp.concatenate(blocks, 0)
                send(T, far)
            return carry

        lax.fori_loop(0, 4, two_chips, 0)

    def four_chips(step, carry):
        for e in range(4):
            far, chip = chip_of(step * 4 + e)
            start = chip * 640 + 256
            for j, block in enumerate(gathered(e, (start, start + 320))):
                msg_ref[pl.ds(pl.multiple_of((chip * 2 + j) * ROWS_IN + 64, 16), 16), :] = block
            send(2, far)
        return carry

    lax.fori_loop(0, 2, four_chips, 0)
    own_in = pl.ds(pl.multiple_of(me * ROWS_IN, 16), ROWS_IN)
    got[own_in, :] = msg_ref[own_in, :]
    loop(0, 16, lambda d: panel_copy(d).wait())
    def contract(q):
        sums = []
        for pair in range(2):
            accs = [None, None]
            for peer in range(16):
                rows = got[pl.ds(pl.multiple_of(q * 16 + peer * ROWS_IN, 16), 16), :].astype(F32)
                for e in range(2):
                    v = pair * 2 + e
                    sides = []
                    for h in (0, 8):
                        if v < 3:
                            sides.append(rows[h : h + 8, v * 128 : v * 128 + 128])
                        else:
                            x, y, z = (
                                pltpu.roll(rows[h : h + 8, w * 128 : w * 128 + 128], 2 + 2 * w, 0) for w in range(3)
                            )
                            sides.append(jnp.where(sub < 2, x, jnp.where(sub < 4, y, z)))
                    one = jnp.concatenate(sides, 1)
                    two = jnp.concatenate([one, one], 0).astype(BF16)
                    left = jnp.concatenate([two] * 8, 0) * diag_ref[...]
                    right = pan[
                        peer * 16 : peer * 16 + 16, pl.ds(pl.multiple_of(q * 64 + v * 16, 16), 16), :
                    ].reshape(256, DEG)
                    t = dot(left, right)
                    accs[e] = t if accs[e] is None else accs[e] + t
            sums += accs
        return sums

    def sum_slots(T, q):
        for v, t in enumerate(contract(q)):
            rows = t.reshape(16, 8, DEG)
            for c in range(2):
                row = base[T] + c * 4 * share[T] + (q - 2 * T) * 64 + v * 16
                mine[pl.ds(pl.multiple_of(row, 16), 16), :] = jnp.sum(rows * factor_ref[c][None], axis=1)

    def analyse_part(T):
        loop(1, 16, lambda d: in_copy(T, d).wait_recv())
        loop(2 * T, min(2 * T + 2, 5), lambda q: sum_slots(T, q))
        loop(1, 8, lambda d: slab_copy(T, d).start())

    def total_part(T):
        size = share[T]
        own = pl.ds(pl.multiple_of(base[T] + lat * size, 16), size)
        total = mine[own, :]
        for d in range(1, 8):
            slab_copy(T, d).wait_recv()
            total = total + parts[pl.ds(pl.multiple_of(base[T] + (lat + 8 - d) % 8 * size, 16), size), :]
        coeff[own, :] = (total * keeps[T * 32 : T * 32 + size, :]).astype(BF16)
        loop(1, 8, lambda d: coeff_copy(T, d).start())

    chunk = lax.broadcasted_iota(jnp.int32, (DEG, 128), 1) // 16

    def synthesis_part(T):
        groups = share[T] // 4
        loop(1, 8, lambda d: coeff_copy(T, d).wait_recv())
        for c in range(2):
            rows = coeff[base[T] + c * groups * 16 : base[T] + (c + 1) * groups * 16, :].astype(F32)
            if groups < 8:
                rows = jnp.concatenate([rows, jnp.zeros((128 - groups * 16, DEG), F32)], 0)
            turned = rows.T
            for g in range(groups):
                wide[g * DEG : g * DEG + DEG, c * 128 : c * 128 + 128] = jnp.where(
                    chunk == g, turned, 0.0
                ).astype(BF16)

        def two_peers(d, refs):
            left = jnp.concatenate(
                [
                    jnp.concatenate(
                        [
                            pan[
                                pl.ds(pl.multiple_of(ahead(d + e) * 16, 16), 16),
                                T * 128 + g * 16 : T * 128 + g * 16 + 16, :
                            ].reshape(256, DEG)
                            for g in range(groups)
                        ],
                        1,
                    )
                    for e in range(2)
                ],
                0,
            )
            o = dot(left, wide[: groups * DEG, :]).reshape(32, 16, 256)
            o = jnp.sum(o * pick_ref[...][None], axis=1)
            for e in range(2):
                place = pl.ds(pl.multiple_of(ahead(d + e) * ROWS_OUT + T * 16, 16), 16)
                refs[e][place, :] = o[e * 16 : e * 16 + 16].astype(BF16)

        def leaving(i):
            d = 16 - 2 * i
            two_peers(d, (syn, syn))
            out_copy(T, d).start()
            out_copy(T, d + 1).start()

        loop(1, 8, leaving)
        two_peers(0, (out_ref, syn))
        out_copy(T, 1).start()

    analyse_part(0)
    analyse_part(1)
    total_part(0)
    analyse_part(2)
    total_part(1)
    synthesis_part(0)
    total_part(2)
    synthesis_part(1)
    synthesis_part(2)
    for T in range(3):
        loop(1, 16, lambda d: in_copy(T, d).wait_send())
        loop(1, 16, lambda d: out_copy(T, d).wait())

        def finish_lat(d):
            slab_copy(T, d).wait_send()
            coeff_copy(T, d).wait_send()

        loop(1, 8, finish_lat)


def main(heights, slots, cutoffs, panels, factors):
    t = tables()
    dma = pltpu.SemaphoreType.DMA
    vec = pltpu.VMEM
    hbm = pl.BlockSpec(memory_space=pl.ANY)
    return pl.pallas_call(
        main_kernel,
        out_shape=jax.ShapeDtypeStruct((16 * ROWS_OUT, 256), BF16),
        in_specs=[pl.BlockSpec(memory_space=pltpu.SMEM)] * 2 + [hbm] * 6 + [vmem()] * 3,
        out_specs=vmem(),
        scratch_shapes=[
            vec((CYC, LON), BF16),
            vec((192, 192), BF16),
            vec((192, 192), BF16),
            vec((2, HALF, 256), F32),
            vec((512, 256), BF16),
            vec((2, CYC * 192, 128), F32),
            vec((48 * 128, 128), F32),
            vec((TROWS, 128), F32),
            vec((4, 128, 128), F32),
            vec((16 * ROWS_IN, 384), BF16),
            vec((256, 320, DEG), BF16),
            vec((16 * ROWS_IN, 384), BF16),
            vec((640, DEG), F32),
            vec((640, DEG), F32),
            vec((640, DEG), BF16),
            vec((80, DEG), F32),
            vec((8 * DEG, 256), BF16),
            vec((16 * ROWS_OUT, 256), BF16),
            dma, dma((4,)), dma((16,)), dma((3, 16)), dma((3, 16)), dma((3, 8)), dma((3, 8)), dma((3, 8)), dma((3, 8)),
            dma((3, 16)), dma((3, 16)),
        ],
        compiler_params=pltpu.CompilerParams(
            vmem_limit_bytes=56 * MIB, collective_id=0, has_side_effects=True
        ),
        cost_estimate=pl.CostEstimate(flops=2 * 10**10, bytes_accessed=24 * 10**6, transcendentals=0),
        name="main",
    )(slots, cutoffs, heights, *t["first"], t["twist"], t["second"], panels, t["diag"], factors, t["pick"])


def inverse_kernel(slot_ref, msg_hbm, back_hbm, twist_hbm, lh_hbm, ll_hbm, out_hbm,
                   msg_ref, back_ref, twist_ref, lh_ref, ll_ref, out_ref, ts, ls, ys, tsem, osem, msem):
    held = ((back_hbm, back_ref), (twist_hbm, twist_ref), (lh_hbm, lh_ref), (ll_hbm, ll_ref))
    copies = [pltpu.make_async_copy(held[i][0], held[i][1], tsem.at[i]) for i in range(4)]
    pieces = [
        pltpu.make_async_copy(msg_hbm.at[i * 192 : i * 192 + 192], msg_ref.at[i * 192 : i * 192 + 192], msem.at[i])
        for i in range(4)
    ]
    for copy in pieces + copies:
        copy.start()
    ts[0:8, :] = jnp.zeros((8, 128), F32)
    ts[ORDERS:TROWS, :] = jnp.zeros((TROWS - ORDERS, 128), F32)

    def one_peer(o, carry):
        for part in range(3):
            rows = msg_ref[pl.ds(pl.multiple_of(o * 48 + part * 16, 16), 16), :].astype(F32)
            count = 128 if part < 2 else 64
            t = jnp.concatenate([rows[:, :128], rows[:, 128:]], 0).T
            base = o * 320 + part * 128
            for i in range(count):
                ts[pl.ds(slot_ref[base + i] + 1, 1), 0:32] = t[i : i + 1]
        return carry

    for i in range(4):
        pieces[i].wait()
        lax.fori_loop(4 * i, 4 * i + 4, one_peer, 0)

    def one_k(k, carry):
        stack = []
        for base in (0, 48):
            plus = ts[pl.ds(k + base, 32, stride=SLOW), :]
            minus = ts[pl.ds(SLOW - base - k, 32, stride=SLOW), :]
            lone = k == 0 if base == 0 else k == 90 - base
            stack += [plus, jnp.where(lone, 0.0, minus)]
        ls[pl.ds(k, 32, stride=48), :] = jnp.concatenate(stack, 0)[:, :32].T
        return carry

    lax.fori_loop(0, 48, one_k, 0, unroll=4)
    first = lax.broadcasted_iota(jnp.int32, (48, 128), 1) < 64

    def four_cycles(step, carry):
        lefts = []
        for i in range(4):
            r = step * 4 + i
            l0 = ls[pl.ds(pl.multiple_of(r * 48, 48), 48), :]
            l1 = ls[pl.ds(pl.multiple_of((r + CYC) * 48, 48), 48), :]
            lefts += [jnp.where(first, l0, pltpu.roll(l1, 64, 1)), jnp.where(first, pltpu.roll(l0, 64, 1), l1)]
        left = jnp.concatenate(lefts, 0).astype(BF16)
        w = dot(jnp.concatenate([left, left], 1), back_ref[...])
        c, s = twist_ref[0], twist_ref[1]
        for i in range(4):
            re, im = w[i * HALF : i * HALF + HALF, :256], w[i * HALF : i * HALF + HALF, 256:]
            v = jnp.concatenate([re * c - im * s, im * c + re * s], 0).astype(BF16)
            field = dot(lh_ref[...], v) + dot(ll_ref[...], v)
            for lane in range(2):
                ys[lane, pl.ds(pl.multiple_of((step * 4 + i) * 192, 192), 192), :] = field[
                    :, lane * 128 : lane * 128 + 128
                ]
        return carry

    for copy in copies:
        copy.wait()
    lax.fori_loop(0, 4, four_cycles, 0)
    leaving = []
    for a in range(SLOW):
        v = jnp.concatenate([ys.at[lane][pl.ds(a, CYC, stride=192), :] for lane in range(2)], 1)
        out_ref[:, FAST * a : FAST * a + FAST] = v[:, :FAST]
        if a % 48 == 47 or a == SLOW - 1:
            place = slice(FAST * (a // 48 * 48), FAST * a + FAST)
            leaving.append(pltpu.make_async_copy(out_ref.at[:, place], out_hbm.at[:, place], osem.at[a // 48]))
            leaving[-1].start()
    for copy in leaving:
        copy.wait()


def inverse(msg, slots):
    t = tables()
    return pl.pallas_call(
        inverse_kernel,
        out_shape=jax.ShapeDtypeStruct((CYC, LON), F32),
        in_specs=[pl.BlockSpec(memory_space=pltpu.SMEM)] + [pl.BlockSpec(memory_space=pl.ANY)] * 5,
        out_specs=pl.BlockSpec(memory_space=pl.ANY),
        scratch_shapes=[
            pltpu.VMEM((16 * ROWS_OUT, 256), BF16),
            pltpu.VMEM((256, 512), BF16),
            pltpu.VMEM((2, HALF, 256), F32),
            pltpu.VMEM((192, 192), BF16),
            pltpu.VMEM((192, 192), BF16),
            pltpu.VMEM((CYC, LON), F32),
            pltpu.VMEM((TROWS, 128), F32),
            pltpu.VMEM((32 * 48, 128), F32),
            pltpu.VMEM((2, CYC * 192, 128), F32),
            pltpu.SemaphoreType.DMA((4,)),
            pltpu.SemaphoreType.DMA((4,)),
            pltpu.SemaphoreType.DMA((4,)),
        ],
        compiler_params=pltpu.CompilerParams(vmem_limit_bytes=62 * MIB),
        name="inverse",
    )(slots, msg, t["back"], t["twist"], *t["last"])


def degrees():
    stride = (NMAX - ORDERS) // DEG
    return ORDERS + np.arange(DEG, dtype=np.int32) * stride


def factor_rows():
    degree = degrees().astype(np.float64)
    rows = np.zeros((2, 8, DEG), np.float32)
    for c in range(2):
        rows[c, 3 * c] = 1.0
        rows[c, 3 * c + 1] = (degree + 2.0) / (2.0 * NMAX)
        rows[c, 3 * c + 2] = (degree + 2.0) * (degree + 1.0) / (6.0 * NMAX * NMAX)
    return rows


def local(heights, panels, ord_slot, cutoffs):
    back = main(heights, ord_slot, cutoffs, panels, factor_rows())
    return inverse(back, ord_slot)


def solution(mesh):
    return jax.shard_map(
        local,
        mesh=mesh,
        in_specs=(P(("lat", "ord"), None), P("lat", "ord", None), P(), P("ord")),
        out_specs=P(("lat", "ord"), None),
        check_vma=False,
    )
```

```python
import functools
import math

import jax
import jax.numpy as jnp
import numpy as np
from jax import lax
from jax.experimental import pallas as pl
from jax.experimental.pallas import tpu as pltpu
from jax.sharding import PartitionSpec as P

LON = 43200
SLOW = 180
FAST = 240
HALF = 96
ORDERS = 5120
DEG = 128
NMAX = 21600
CYC = 16
TROWS = 6016
FIRST = 8
F32 = jnp.float32
BF16 = jnp.bfloat16
MIB = 1024 * 1024


def split16(table):
    high = table.astype(np.float32).astype(jnp.bfloat16)
    low = (table - high.astype(np.float64)).astype(np.float32).astype(jnp.bfloat16)
    return high, low


def angles(left, right, total):
    return 2.0 * np.pi / total * ((left[:, None] * right[None, :]) % total)


@functools.cache
def tables():
    k = np.arange(91)
    a = np.arange(SLOW)
    b = np.arange(FAST)
    q = np.arange(29)
    ka = angles(k, a, SLOW)
    first = np.zeros((2, HALF, 192))
    first[0, :91, :SLOW] = np.cos(ka)
    first[1, :91, :SLOW] = -np.sin(ka)
    first = first.reshape(2 * HALF, 192)
    kb = angles(k, b, LON)
    twist = np.zeros((2, HALF, 256), np.float32)
    twist[0, :91, :FAST] = np.cos(kb)
    twist[1, :91, :FAST] = np.sin(kb)
    bq = angles(b, q, FAST)
    bq1 = angles(b, q + 1, FAST)
    second = np.zeros((2, 256, 2, 128))
    second[0, :FAST, 0, 0:29] = np.cos(bq)
    second[1, :FAST, 0, 0:29] = np.sin(bq)
    second[0, :FAST, 1, 0:29] = -np.sin(bq)
    second[1, :FAST, 1, 0:29] = np.cos(bq)
    second[0, :FAST, 0, 32:61] = np.cos(bq1)
    second[1, :FAST, 0, 32:61] = -np.sin(bq1)
    second[0, :FAST, 1, 32:61] = -np.sin(bq1)
    second[1, :FAST, 1, 32:61] = -np.cos(bq1)
    second = second / math.sqrt(LON)
    high, low = split16(second[..., :64])
    second = np.concatenate([high, low], -1).reshape(512, 256)
    back = np.zeros((2, 2, 32, 2, 256))
    back[0, 0, :29, 0, :FAST] = np.cos(bq).T
    back[0, 0, :29, 1, :FAST] = np.sin(bq).T
    back[1, 0, :29, 0, :FAST] = -np.sin(bq).T
    back[1, 0, :29, 1, :FAST] = np.cos(bq).T
    back[0, 1, :29, 0, :FAST] = np.cos(bq1).T
    back[0, 1, :29, 1, :FAST] = -np.sin(bq1).T
    back[1, 1, :29, 0, :FAST] = -np.sin(bq1).T
    back[1, 1, :29, 1, :FAST] = -np.cos(bq1).T
    back = np.concatenate(split16(back.reshape(128, 512)), 0)
    last = np.zeros((192, 2, HALF))
    last[:SLOW, 0, :91] = np.cos(ka).T
    last[:SLOW, 1, :91] = -np.sin(ka).T
    last = last.reshape(192, 2 * HALF) * math.sqrt(2048 / (DEG * ORDERS))
    rows = np.arange(128)
    lanes = np.arange(256)
    diag = (lanes[None, :] % 16 == rows[:, None] // 8).astype(jnp.bfloat16)
    pick = (lanes[None, :] % 16 == np.arange(16)[:, None]).astype(np.float32)
    return dict(
        first=split16(first), twist=twist, second=second, back=back,
        last=split16(last), diag=diag, pick=pick,
    )


def swap_chunks(rows):
    rows = list(rows)
    chunk = lax.broadcasted_iota(jnp.int32, (8, 128), 1) // 16
    for d in (4, 2, 1):
        low = (chunk & d) == 0
        new = list(rows)
        for r in range(8):
            if r & d:
                continue
            new[r] = jnp.where(low, rows[r], pltpu.roll(rows[r + d], d * 16, 1))
            new[r + d] = jnp.where(low, pltpu.roll(rows[r], 128 - d * 16, 1), rows[r + d])
        rows = new
    return rows


def dot(left, right):
    return jnp.dot(left, right, preferred_element_type=F32)


def halves(value):
    high = value.astype(BF16)
    return high, (value - high.astype(F32)).astype(BF16)


def vmem():
    return pl.BlockSpec(memory_space=pltpu.VMEM)


MESH = pl.DeviceIdType.MESH
ROWS_IN = 80
ROWS_OUT = 48
SLAB = 80


def main_kernel(slot_ref, cut_ref, x_hbm, fh_hbm, fl_hbm, twist_hbm, second_hbm, panel_ref, diag_ref,
                factor_ref, pick_ref, out_ref,
                x_ref, fh_ref, fl_ref, twist_ref, second_ref, xs, qs, ts, gs, msg_ref,
                pan, got, mine, parts, coeff, keeps, wide, syn,
                xsem, tsem, psem, s1, r1, s2, r2, s3, r3, s4, r4):
    lat = lax.axis_index("lat")
    me = lax.axis_index("ord")
    hy, hz, hc = me // 8, me // 2 % 4, me % 2

    def ahead(d):
        return (hy + d // 8) % 2 * 8 + (hz + d // 2 % 4) % 4 * 2 + (hc + d % 2) % 2

    def behind(d):
        return (hy + 2 - d // 8) % 2 * 8 + (hz + 4 - d // 2 % 4) % 4 * 2 + (hc + 2 - d % 2) % 2

    def panel_copy(d):
        place = pl.ds(pl.multiple_of(behind(d) * 16, 16), 16)
        return pltpu.make_async_copy(panel_ref.at[place], pan.at[place], psem.at[d])

    base = (0, 256, 512)
    share = (32, 32, 16)

    def in_copy(T, d):
        size = share[T]
        return pltpu.make_async_remote_copy(
            src_ref=msg_ref.at[pl.ds(pl.multiple_of(ahead(d) * ROWS_IN + T * 32, 16), size)],
            dst_ref=got.at[pl.ds(pl.multiple_of(me * ROWS_IN + T * 32, 16), size)],
            send_sem=s1.at[T, d], recv_sem=r1.at[T, d],
            device_id=(lat, ahead(d)), device_id_type=MESH,
        )

    def slab_copy(T, d):
        peer = (lat + d) % 8
        size = share[T]
        return pltpu.make_async_remote_copy(
            src_ref=mine.at[pl.ds(pl.multiple_of(base[T] + peer * size, 16), size)],
            dst_ref=parts.at[pl.ds(pl.multiple_of(base[T] + lat * size, 16), size)],
            send_sem=s2.at[T, d], recv_sem=r2.at[T, d],
            device_id=(peer, me), device_id_type=MESH,
        )

    def coeff_copy(T, d):
        peer = (lat + d) % 8
        place = pl.ds(pl.multiple_of(base[T] + lat * share[T], 16), share[T])
        return pltpu.make_async_remote_copy(
            src_ref=coeff.at[place], dst_ref=coeff.at[place],
            send_sem=s3.at[T, d], recv_sem=r3.at[T, d],
            device_id=(peer, me), device_id_type=MESH,
        )

    def out_copy(T, d):
        return pltpu.make_async_remote_copy(
            src_ref=syn.at[pl.ds(pl.multiple_of(ahead(d) * ROWS_OUT + T * 16, 16), 16)],
            dst_ref=out_ref.at[pl.ds(pl.multiple_of(me * ROWS_OUT + T * 16, 16), 16)],
            send_sem=s4.at[T, d], recv_sem=r4.at[T, d],
            device_id=(lat, ahead(d)), device_id_type=MESH,
        )

    def loop(low, high, body):
        def step(d, carry):
            body(d)
            return carry
        lax.fori_loop(low, high, step, 0)

    cuts = (0, 11520, 23040, 34560, LON)
    heights = [
        pltpu.make_async_copy(
            x_hbm.at[:, cuts[i] : cuts[i + 1]], x_ref.at[:, cuts[i] : cuts[i + 1]], xsem.at[i]
        )
        for i in range(4)
    ]
    for copy in heights:
        copy.start()
    held = ((fh_hbm, fh_ref), (fl_hbm, fl_ref), (twist_hbm, twist_ref), (second_hbm, second_ref))

    def table_copy(i):
        return pltpu.make_async_copy(held[i][0], held[i][1], tsem.at[i])

    for i in range(4):
        table_copy(i).start()
    barrier = pltpu.get_barrier_semaphore()
    loop(1, 16, lambda d: pl.semaphore_signal(barrier, inc=1, device_id=(lat, ahead(d)), device_id_type=MESH))
    loop(1, 8, lambda d: pl.semaphore_signal(barrier, inc=1, device_id=((lat + d) % 8, me), device_id_type=MESH))
    degree = ORDERS + (NMAX - ORDERS) // DEG * lax.broadcasted_iota(jnp.int32, (1, DEG), 1)
    for T in range(3):
        size = share[T]
        for i in range(size):
            slot = T * 128 + (lat * size + i) % (4 * size)
            row = T * 32 + i
            keeps[row : row + 1, :] = jnp.where(degree <= cut_ref[slot], 1.0, 0.0)
    landed = 0
    inside = lax.broadcasted_iota(jnp.int32, (CYC, 256), 1) < FAST
    for r in range(CYC):
        for lane in range(2):
            xs[lane, r * 192 + 176 : r * 192 + 192, :] = jnp.zeros((16, 128), F32)
    for a in range(SLOW):
        start = FAST * a // 128 * 128
        off = FAST * a - start
        while landed < min(start + 384, LON):
            i = cuts.index(landed)
            heights[i].wait()
            landed = cuts[i + 1]
        if start + 384 <= LON:
            v = x_ref[:, start : start + 384].astype(F32)
        else:
            v = jnp.concatenate(
                [x_ref[:, start:LON].astype(F32), jnp.zeros((CYC, start + 384 - LON), F32)], 1
            )
        if off:
            v = pltpu.roll(v, 384 - off, 1)
        v = jnp.where(inside, v[:, :256], 0.0)
        for lane in range(2):
            xs.at[lane][pl.ds(a, CYC, stride=192), :] = v[:, lane * 128 : lane * 128 + 128]

    first = lax.broadcasted_iota(jnp.int32, (48, 128), 1) < 64

    def one_cycle(r, carry):
        rows = pl.ds(pl.multiple_of(r * 192, 192), 192)
        level = jnp.concatenate([xs[0, rows, :], xs[1, rows, :]], 1)
        value = level
        stack = []
        tc, tsin = twist_ref[0], twist_ref[1]
        for p in range(3):
            if p:
                value = value * level
            if p == 0:
                high = value.astype(BF16)
                y = dot(fh_ref[...], high) + dot(fl_ref[...], high)
            else:
                high, low = halves(value)
                y = dot(fh_ref[...], high) + dot(fl_ref[...], high) + dot(fh_ref[...], low)
            re, im = y[:HALF], y[HALF:]
            stack += list(halves(jnp.concatenate([re * tc + im * tsin, im * tc - re * tsin], 1)))
        o = dot(jnp.concatenate(stack, 0), second_ref[...])
        for p in range(3):
            both = o[p * 192 : p * 192 + HALF] + o[p * 192 + HALF : p * 192 + 192]
            for c in range(2):
                part = both[:, c * 128 : c * 128 + 128]
                part = part + pltpu.roll(part, 64, 1)
                qs[pl.ds(r * 8 + c * 3 + p, 48, stride=128), :] = jnp.where(first, part[:48], part[48:])
        return carry

    for i in range(4):
        table_copy(i).wait()
    loop(0, 16, lambda d: panel_copy(d).start())
    lax.fori_loop(0, CYC, one_cycle, 0, unroll=4)

    def one_k(k, carry):
        t = qs[pl.ds(k * 128 if isinstance(k, int) else pl.multiple_of(k * 128, 128), 128), :].T
        ts[pl.ds(k + FIRST - 1, 32, stride=SLOW), :] = t[0:32]
        ts[pl.ds(SLOW - k + FIRST - 1, 32, stride=SLOW), :] = t[32:64]
        return t

    def two_k(k, carry):
        t = one_k(k, carry)
        ts[pl.ds(k + 48 + FIRST - 1, 32, stride=SLOW), :] = t[64:96]
        ts[pl.ds(SLOW - 48 - k + FIRST - 1, 32, stride=SLOW), :] = t[96:128]
        return carry

    lax.fori_loop(0, 40, two_k, 0, unroll=4)
    for k in range(40, 43):
        two_k(k, 0)
    for k in range(43, 48):
        one_k(k, 0)

    pl.semaphore_wait(barrier, 22)

    sub = lax.broadcasted_iota(jnp.int32, (8, 128), 0)

    orders = ts.at[pl.ds(FIRST, ORDERS)]

    def chip_of(i):
        far = 7 - i // 2 - i % 2 * 4
        return far, (hy + far // 4) % 2 * 4 + (hz + far % 4) % 4

    def gathered(j, starts):
        for i in range(0, 128, 32):
            at = starts[i // 64] + i % 64
            rows = [orders[pl.ds(slot_ref[at + e], 1), :] for e in range(32)]
            for e in range(32):
                gs[j, i + e : i + e + 1, :] = rows[e]
        t = gs[j].T
        sides = [swap_chunks([t[(h * 8 + r) * 8 : (h * 8 + r + 1) * 8] for r in range(8)]) for h in range(2)]
        blocks = []
        for u in (0, 4):
            packed = [
                jnp.concatenate(
                    [jnp.where(sub < 6, side[u + v], pltpu.roll(side[u + 3], 6 - 2 * v, 0)) for v in range(3)], 1
                )
                for side in sides
            ]
            blocks.append(jnp.concatenate(packed, 0).astype(BF16))
        return blocks

    def send(T, far):
        @pl.when(far > 0)
        def _():
            in_copy(T, far * 2).start()

        in_copy(T, far * 2 + 1).start()

    for T in range(2):
        def two_chips(step, carry):
            for e in range(2):
                far, chip = chip_of(step * 2 + e)
                for j in range(2):
                    to = chip * 2 + j
                    start = to * 320 + T * 128
                    blocks = gathered(e * 2 + j, (start, start + 64))
                    msg_ref[pl.ds(pl.multiple_of(to * ROWS_IN + T * 32, 16), 32), :] = jnp.concatenate(blocks, 0)
                send(T, far)
            return carry

        lax.fori_loop(0, 4, two_chips, 0)

    def four_chips(step, carry):
        for e in range(4):
            far, chip = chip_of(step * 4 + e)
            start = chip * 640 + 256
            for j, block in enumerate(gathered(e, (start, start + 320))):
                msg_ref[pl.ds(pl.multiple_of((chip * 2 + j) * ROWS_IN + 64, 16), 16), :] = block
            send(2, far)
        return carry

    lax.fori_loop(0, 2, four_chips, 0)
    own_in = pl.ds(pl.multiple_of(me * ROWS_IN, 16), ROWS_IN)
    got[own_in, :] = msg_ref[own_in, :]
    loop(0, 16, lambda d: panel_copy(d).wait())
    def contract(q):
        sums = []
        for pair in range(2):
            accs = [None, None]
            for peer in range(16):
                rows = got[pl.ds(pl.multiple_of(q * 16 + peer * ROWS_IN, 16), 16), :].astype(F32)
                for e in range(2):
                    v = pair * 2 + e
                    sides = []
                    for h in (0, 8):
                        if v < 3:
                            sides.append(rows[h : h + 8, v * 128 : v * 128 + 128])
                        else:
                            x, y, z = (
                                pltpu.roll(rows[h : h + 8, w * 128 : w * 128 + 128], 2 + 2 * w, 0) for w in range(3)
                            )
                            sides.append(jnp.where(sub < 2, x, jnp.where(sub < 4, y, z)))
                    one = jnp.concatenate(sides, 1)
                    two = jnp.concatenate([one, one], 0).astype(BF16)
                    left = jnp.concatenate([two] * 8, 0) * diag_ref[...]
                    right = pan[
                        peer * 16 : peer * 16 + 16, pl.ds(pl.multiple_of(q * 64 + v * 16, 16), 16), :
                    ].reshape(256, DEG)
                    t = dot(left, right)
                    accs[e] = t if accs[e] is None else accs[e] + t
            sums += accs
        return sums

    def sum_slots(T, q):
        for v, t in enumerate(contract(q)):
            rows = t.reshape(16, 8, DEG)
            for c in range(2):
                row = base[T] + c * 4 * share[T] + (q - 2 * T) * 64 + v * 16
                mine[pl.ds(pl.multiple_of(row, 16), 16), :] = jnp.sum(rows * factor_ref[c][None], axis=1)

    def analyse_part(T):
        loop(1, 16, lambda d: in_copy(T, d).wait_recv())
        loop(2 * T, min(2 * T + 2, 5), lambda q: sum_slots(T, q))
        loop(1, 8, lambda d: slab_copy(T, d).start())

    def total_part(T):
        size = share[T]
        own = pl.ds(pl.multiple_of(base[T] + lat * size, 16), size)
        total = mine[own, :]
        for d in range(1, 8):
            slab_copy(T, d).wait_recv()
            total = total + parts[pl.ds(pl.multiple_of(base[T] + (lat + 8 - d) % 8 * size, 16), size), :]
        coeff[own, :] = (total * keeps[T * 32 : T * 32 + size, :]).astype(BF16)
        loop(1, 8, lambda d: coeff_copy(T, d).start())

    chunk = lax.broadcasted_iota(jnp.int32, (DEG, 128), 1) // 16

    def synthesis_part(T):
        groups = share[T] // 4
        loop(1, 8, lambda d: coeff_copy(T, d).wait_recv())
        for c in range(2):
            rows = coeff[base[T] + c * groups * 16 : base[T] + (c + 1) * groups * 16, :].astype(F32)
            if groups < 8:
                rows = jnp.concatenate([rows, jnp.zeros((128 - groups * 16, DEG), F32)], 0)
            turned = rows.T
            for g in range(groups):
                wide[g * DEG : g * DEG + DEG, c * 128 : c * 128 + 128] = jnp.where(
                    chunk == g, turned, 0.0
                ).astype(BF16)

        def two_peers(d, refs):
            left = jnp.concatenate(
                [
                    jnp.concatenate(
                        [
                            pan[
                                pl.ds(pl.multiple_of(ahead(d + e) * 16, 16), 16),
                                T * 128 + g * 16 : T * 128 + g * 16 + 16, :
                            ].reshape(256, DEG)
                            for g in range(groups)
                        ],
                        1,
                    )
                    for e in range(2)
                ],
                0,
            )
            o = dot(left, wide[: groups * DEG, :]).reshape(32, 16, 256)
            o = jnp.sum(o * pick_ref[...][None], axis=1)
            for e in range(2):
                place = pl.ds(pl.multiple_of(ahead(d + e) * ROWS_OUT + T * 16, 16), 16)
                refs[e][place, :] = o[e * 16 : e * 16 + 16].astype(BF16)

        def leaving(i):
            d = 16 - 2 * i
            two_peers(d, (syn, syn))
            out_copy(T, d).start()
            out_copy(T, d + 1).start()

        loop(1, 8, leaving)
        two_peers(0, (out_ref, syn))
        out_copy(T, 1).start()

    analyse_part(0)
    analyse_part(1)
    total_part(0)
    analyse_part(2)
    total_part(1)
    synthesis_part(0)
    total_part(2)
    synthesis_part(1)
    synthesis_part(2)
    for T in range(3):
        loop(1, 16, lambda d: in_copy(T, d).wait_send())
        loop(1, 16, lambda d: out_copy(T, d).wait())

        def finish_lat(d):
            slab_copy(T, d).wait_send()
            coeff_copy(T, d).wait_send()

        loop(1, 8, finish_lat)


def main(heights, slots, cutoffs, panels, factors):
    t = tables()
    dma = pltpu.SemaphoreType.DMA
    vec = pltpu.VMEM
    hbm = pl.BlockSpec(memory_space=pl.ANY)
    return pl.pallas_call(
        main_kernel,
        out_shape=jax.ShapeDtypeStruct((16 * ROWS_OUT, 256), BF16),
        in_specs=[pl.BlockSpec(memory_space=pltpu.SMEM)] * 2 + [hbm] * 6 + [vmem()] * 3,
        out_specs=vmem(),
        scratch_shapes=[
            vec((CYC, LON), BF16),
            vec((192, 192), BF16),
            vec((192, 192), BF16),
            vec((2, HALF, 256), F32),
            vec((512, 256), BF16),
            vec((2, CYC * 192, 128), F32),
            vec((48 * 128, 128), F32),
            vec((TROWS, 128), F32),
            vec((4, 128, 128), F32),
            vec((16 * ROWS_IN, 384), BF16),
            vec((256, 320, DEG), BF16),
            vec((16 * ROWS_IN, 384), BF16),
            vec((640, DEG), F32),
            vec((640, DEG), F32),
            vec((640, DEG), BF16),
            vec((80, DEG), F32),
            vec((8 * DEG, 256), BF16),
            vec((16 * ROWS_OUT, 256), BF16),
            dma((4,)), dma((4,)), dma((16,)), dma((3, 16)), dma((3, 16)), dma((3, 8)), dma((3, 8)), dma((3, 8)), dma((3, 8)),
            dma((3, 16)), dma((3, 16)),
        ],
        compiler_params=pltpu.CompilerParams(
            vmem_limit_bytes=56 * MIB, collective_id=0, has_side_effects=True
        ),
        cost_estimate=pl.CostEstimate(flops=2 * 10**10, bytes_accessed=24 * 10**6, transcendentals=0),
        name="main",
    )(slots, cutoffs, heights, *t["first"], t["twist"], t["second"], panels, t["diag"], factors, t["pick"])


def inverse_kernel(slot_ref, msg_hbm, back_hbm, twist_hbm, lh_hbm, ll_hbm, out_hbm,
                   msg_ref, back_ref, twist_ref, lh_ref, ll_ref, out_ref, ts, ls, ys, tsem, osem, msem):
    held = ((back_hbm, back_ref), (twist_hbm, twist_ref), (lh_hbm, lh_ref), (ll_hbm, ll_ref))
    copies = [pltpu.make_async_copy(held[i][0], held[i][1], tsem.at[i]) for i in range(4)]
    pieces = [
        pltpu.make_async_copy(msg_hbm.at[i * 192 : i * 192 + 192], msg_ref.at[i * 192 : i * 192 + 192], msem.at[i])
        for i in range(4)
    ]
    for copy in pieces + copies:
        copy.start()
    ts[0:FIRST, :] = jnp.zeros((FIRST, 128), F32)
    ts[FIRST + ORDERS : TROWS, :] = jnp.zeros((TROWS - ORDERS - FIRST, 128), F32)
    orders = ts.at[pl.ds(FIRST, ORDERS)]

    def one_peer(o, carry):
        for part in range(3):
            rows = msg_ref[pl.ds(pl.multiple_of(o * 48 + part * 16, 16), 16), :].astype(F32)
            count = 128 if part < 2 else 64
            t = jnp.concatenate([rows[:, :128], rows[:, 128:]], 0).T
            base = o * 320 + part * 128
            for i in range(count):
                orders[pl.ds(slot_ref[base + i], 1), 0:32] = t[i : i + 1]
        return carry

    for i in range(4):
        pieces[i].wait()
        lax.fori_loop(4 * i, 4 * i + 4, one_peer, 0)

    def one_k(k, carry):
        stack = []
        for base in (0, 48):
            plus = ts[pl.ds(k + base + FIRST - 1, 32, stride=SLOW), :]
            minus = ts[pl.ds(SLOW - base - k + FIRST - 1, 32, stride=SLOW), :]
            lone = k == 0 if base == 0 else k == 90 - base
            stack += [plus, jnp.where(lone, 0.0, minus)]
        ls[pl.ds(k, 32, stride=48), :] = jnp.concatenate(stack, 0)[:, :32].T
        return carry

    lax.fori_loop(0, 48, one_k, 0, unroll=4)
    first = lax.broadcasted_iota(jnp.int32, (48, 128), 1) < 64

    def four_cycles(step, carry):
        lefts = []
        for i in range(4):
            r = step * 4 + i
            l0 = ls[pl.ds(pl.multiple_of(r * 48, 48), 48), :]
            l1 = ls[pl.ds(pl.multiple_of((r + CYC) * 48, 48), 48), :]
            lefts += [jnp.where(first, l0, pltpu.roll(l1, 64, 1)), jnp.where(first, pltpu.roll(l0, 64, 1), l1)]
        left = jnp.concatenate(lefts, 0).astype(BF16)
        w = dot(jnp.concatenate([left, left], 1), back_ref[...])
        c, s = twist_ref[0], twist_ref[1]
        for i in range(4):
            re, im = w[i * HALF : i * HALF + HALF, :256], w[i * HALF : i * HALF + HALF, 256:]
            v = jnp.concatenate([re * c - im * s, im * c + re * s], 0).astype(BF16)
            field = dot(lh_ref[...], v) + dot(ll_ref[...], v)
            for lane in range(2):
                ys[lane, pl.ds(pl.multiple_of((step * 4 + i) * 192, 192), 192), :] = field[
                    :, lane * 128 : lane * 128 + 128
                ]
        return carry

    for copy in copies:
        copy.wait()
    lax.fori_loop(0, 4, four_cycles, 0)
    leaving = []
    for a in range(SLOW):
        v = jnp.concatenate([ys.at[lane][pl.ds(a, CYC, stride=192), :] for lane in range(2)], 1)
        out_ref[:, FAST * a : FAST * a + FAST] = v[:, :FAST]
        if a % 48 == 47 or a == SLOW - 1:
            place = slice(FAST * (a // 48 * 48), FAST * a + FAST)
            leaving.append(pltpu.make_async_copy(out_ref.at[:, place], out_hbm.at[:, place], osem.at[a // 48]))
            leaving[-1].start()
    for copy in leaving:
        copy.wait()


def inverse(msg, slots):
    t = tables()
    return pl.pallas_call(
        inverse_kernel,
        out_shape=jax.ShapeDtypeStruct((CYC, LON), F32),
        in_specs=[pl.BlockSpec(memory_space=pltpu.SMEM)] + [pl.BlockSpec(memory_space=pl.ANY)] * 5,
        out_specs=pl.BlockSpec(memory_space=pl.ANY),
        scratch_shapes=[
            pltpu.VMEM((16 * ROWS_OUT, 256), BF16),
            pltpu.VMEM((256, 512), BF16),
            pltpu.VMEM((2, HALF, 256), F32),
            pltpu.VMEM((192, 192), BF16),
            pltpu.VMEM((192, 192), BF16),
            pltpu.VMEM((CYC, LON), F32),
            pltpu.VMEM((TROWS, 128), F32),
            pltpu.VMEM((32 * 48, 128), F32),
            pltpu.VMEM((2, CYC * 192, 128), F32),
            pltpu.SemaphoreType.DMA((4,)),
            pltpu.SemaphoreType.DMA((4,)),
            pltpu.SemaphoreType.DMA((4,)),
        ],
        compiler_params=pltpu.CompilerParams(vmem_limit_bytes=62 * MIB),
        name="inverse",
    )(slots, msg, t["back"], t["twist"], *t["last"])


def degrees():
    stride = (NMAX - ORDERS) // DEG
    return ORDERS + np.arange(DEG, dtype=np.int32) * stride


def factor_rows():
    degree = degrees().astype(np.float64)
    rows = np.zeros((2, 8, DEG), np.float32)
    for c in range(2):
        rows[c, 3 * c] = 1.0
        rows[c, 3 * c + 1] = (degree + 2.0) / (2.0 * NMAX)
        rows[c, 3 * c + 2] = (degree + 2.0) * (degree + 1.0) / (6.0 * NMAX * NMAX)
    return rows


def local(heights, panels, ord_slot, cutoffs):
    back = main(heights, ord_slot, cutoffs, panels, factor_rows())
    return inverse(back, ord_slot)


def solution(mesh):
    return jax.shard_map(
        local,
        mesh=mesh,
        in_specs=(P(("lat", "ord"), None), P("lat", "ord", None), P(), P("ord")),
        out_specs=P(("lat", "ord"), None),
        check_vma=False,
    )
```

```python
import functools
import math

import jax
import jax.numpy as jnp
import numpy as np
from jax import lax
from jax.experimental import pallas as pl
from jax.experimental.pallas import tpu as pltpu
from jax.sharding import PartitionSpec as P

LON = 43200
SLOW = 180
FAST = 240
HALF = 96
ORDERS = 5120
DEG = 128
NMAX = 21600
CYC = 16
TROWS = 6016
FIRST = 8
F32 = jnp.float32
BF16 = jnp.bfloat16
MIB = 1024 * 1024


def split16(table):
    high = table.astype(np.float32).astype(jnp.bfloat16)
    low = (table - high.astype(np.float64)).astype(np.float32).astype(jnp.bfloat16)
    return high, low


def angles(left, right, total):
    return 2.0 * np.pi / total * ((left[:, None] * right[None, :]) % total)


@functools.cache
def tables():
    k = np.arange(91)
    a = np.arange(SLOW)
    b = np.arange(FAST)
    q = np.arange(29)
    ka = angles(k, a, SLOW)
    first = np.zeros((2, HALF, 192))
    first[0, :91, :SLOW] = np.cos(ka)
    first[1, :91, :SLOW] = -np.sin(ka)
    first = first.reshape(2 * HALF, 192)
    kb = angles(k, b, LON)
    twist = np.zeros((2, HALF, 256), np.float32)
    twist[0, :91, :FAST] = np.cos(kb)
    twist[1, :91, :FAST] = np.sin(kb)
    bq = angles(b, q, FAST)
    bq1 = angles(b, q + 1, FAST)
    second = np.zeros((2, 256, 2, 128))
    second[0, :FAST, 0, 0:29] = np.cos(bq)
    second[1, :FAST, 0, 0:29] = np.sin(bq)
    second[0, :FAST, 1, 0:29] = -np.sin(bq)
    second[1, :FAST, 1, 0:29] = np.cos(bq)
    second[0, :FAST, 0, 32:61] = np.cos(bq1)
    second[1, :FAST, 0, 32:61] = -np.sin(bq1)
    second[0, :FAST, 1, 32:61] = -np.sin(bq1)
    second[1, :FAST, 1, 32:61] = -np.cos(bq1)
    second = second / math.sqrt(LON)
    high, low = split16(second[..., :64])
    second = np.concatenate([high, low], -1).reshape(512, 256)
    back = np.zeros((2, 2, 32, 2, 256))
    back[0, 0, :29, 0, :FAST] = np.cos(bq).T
    back[0, 0, :29, 1, :FAST] = np.sin(bq).T
    back[1, 0, :29, 0, :FAST] = -np.sin(bq).T
    back[1, 0, :29, 1, :FAST] = np.cos(bq).T
    back[0, 1, :29, 0, :FAST] = np.cos(bq1).T
    back[0, 1, :29, 1, :FAST] = -np.sin(bq1).T
    back[1, 1, :29, 0, :FAST] = -np.sin(bq1).T
    back[1, 1, :29, 1, :FAST] = -np.cos(bq1).T
    back = np.concatenate(split16(back.reshape(128, 512)), 0)
    last = np.zeros((192, 2, HALF))
    last[:SLOW, 0, :91] = np.cos(ka).T
    last[:SLOW, 1, :91] = -np.sin(ka).T
    last = last.reshape(192, 2 * HALF) * math.sqrt(2048 / (DEG * ORDERS))
    rows = np.arange(128)
    lanes = np.arange(256)
    diag = (lanes[None, :] % 16 == rows[:, None] // 8).astype(jnp.bfloat16)
    pick = (lanes[None, :] % 16 == np.arange(16)[:, None]).astype(np.float32)
    return dict(
        first=split16(first), twist=twist, second=second, back=back,
        last=split16(last), diag=diag, pick=pick,
    )


def swap_chunks(rows):
    rows = list(rows)
    chunk = lax.broadcasted_iota(jnp.int32, (8, 128), 1) // 16
    for d in (4, 2, 1):
        low = (chunk & d) == 0
        new = list(rows)
        for r in range(8):
            if r & d:
                continue
            new[r] = jnp.where(low, rows[r], pltpu.roll(rows[r + d], d * 16, 1))
            new[r + d] = jnp.where(low, pltpu.roll(rows[r], 128 - d * 16, 1), rows[r + d])
        rows = new
    return rows


def dot(left, right):
    return jnp.dot(left, right, preferred_element_type=F32)


def halves(value):
    high = value.astype(BF16)
    return high, (value - high.astype(F32)).astype(BF16)


def vmem():
    return pl.BlockSpec(memory_space=pltpu.VMEM)


MESH = pl.DeviceIdType.MESH
ROWS_IN = 80
ROWS_OUT = 48
SLAB = 80


def main_kernel(slot_ref, cut_ref, x_hbm, fh_hbm, fl_hbm, twist_hbm, second_hbm, panel_ref, diag_ref,
                factor_ref, pick_ref, out_ref,
                x_ref, fh_ref, fl_ref, twist_ref, second_ref, xs, qs, ts, gs, msg_ref,
                pan, got, mine, parts, coeff, keeps, wide, syn,
                xsem, tsem, psem, s1, r1, s2, r2, s3, r3, s4, r4):
    lat = lax.axis_index("lat")
    me = lax.axis_index("ord")
    hy, hz, hc = me // 8, me // 2 % 4, me % 2

    def ahead(d):
        return (hy + d // 8) % 2 * 8 + (hz + d // 2 % 4) % 4 * 2 + (hc + d % 2) % 2

    def behind(d):
        return (hy + 2 - d // 8) % 2 * 8 + (hz + 4 - d // 2 % 4) % 4 * 2 + (hc + 2 - d % 2) % 2

    def panel_copy(d):
        place = pl.ds(pl.multiple_of(behind(d) * 16, 16), 16)
        return pltpu.make_async_copy(panel_ref.at[place], pan.at[place], psem.at[d])

    base = (0, 256, 512)
    share = (32, 32, 16)

    def in_copy(T, d):
        size = share[T]
        return pltpu.make_async_remote_copy(
            src_ref=msg_ref.at[pl.ds(pl.multiple_of(ahead(d) * ROWS_IN + T * 32, 16), size)],
            dst_ref=got.at[pl.ds(pl.multiple_of(me * ROWS_IN + T * 32, 16), size)],
            send_sem=s1.at[T, d], recv_sem=r1.at[T, d],
            device_id=(lat, ahead(d)), device_id_type=MESH,
        )

    def slab_copy(T, d):
        peer = (lat + d) % 8
        size = share[T]
        return pltpu.make_async_remote_copy(
            src_ref=mine.at[pl.ds(pl.multiple_of(base[T] + peer * size, 16), size)],
            dst_ref=parts.at[pl.ds(pl.multiple_of(base[T] + lat * size, 16), size)],
            send_sem=s2.at[T, d], recv_sem=r2.at[T, d],
            device_id=(peer, me), device_id_type=MESH,
        )

    def coeff_copy(T, d):
        peer = (lat + d) % 8
        place = pl.ds(pl.multiple_of(base[T] + lat * share[T], 16), share[T])
        return pltpu.make_async_remote_copy(
            src_ref=coeff.at[place], dst_ref=coeff.at[place],
            send_sem=s3.at[T, d], recv_sem=r3.at[T, d],
            device_id=(peer, me), device_id_type=MESH,
        )

    def out_copy(T, d):
        return pltpu.make_async_remote_copy(
            src_ref=syn.at[pl.ds(pl.multiple_of(ahead(d) * ROWS_OUT + T * 16, 16), 16)],
            dst_ref=out_ref.at[pl.ds(pl.multiple_of(me * ROWS_OUT + T * 16, 16), 16)],
            send_sem=s4.at[T, d], recv_sem=r4.at[T, d],
            device_id=(lat, ahead(d)), device_id_type=MESH,
        )

    def loop(low, high, body):
        def step(d, carry):
            body(d)
            return carry
        lax.fori_loop(low, high, step, 0)

    cuts = (0, 11520, 23040, 34560, LON)
    heights = [
        pltpu.make_async_copy(
            x_hbm.at[:, cuts[i] : cuts[i + 1]], x_ref.at[:, cuts[i] : cuts[i + 1]], xsem.at[i]
        )
        for i in range(4)
    ]
    for copy in heights:
        copy.start()
    held = ((fh_hbm, fh_ref), (fl_hbm, fl_ref), (twist_hbm, twist_ref), (second_hbm, second_ref))

    def table_copy(i):
        return pltpu.make_async_copy(held[i][0], held[i][1], tsem.at[i])

    for i in range(4):
        table_copy(i).start()
    barrier = pltpu.get_barrier_semaphore()
    loop(1, 16, lambda d: pl.semaphore_signal(barrier, inc=1, device_id=(lat, ahead(d)), device_id_type=MESH))
    loop(1, 8, lambda d: pl.semaphore_signal(barrier, inc=1, device_id=((lat + d) % 8, me), device_id_type=MESH))
    degree = ORDERS + (NMAX - ORDERS) // DEG * lax.broadcasted_iota(jnp.int32, (1, DEG), 1)
    for T in range(3):
        size = share[T]
        for i in range(size):
            slot = T * 128 + (lat * size + i) % (4 * size)
            row = T * 32 + i
            keeps[row : row + 1, :] = jnp.where(degree <= cut_ref[slot], 1.0, 0.0)
    landed = 0
    inside = lax.broadcasted_iota(jnp.int32, (CYC, 256), 1) < FAST
    for r in range(CYC):
        for lane in range(2):
            xs[lane, r * 192 + 176 : r * 192 + 192, :] = jnp.zeros((16, 128), F32)
    for a in range(SLOW):
        start = FAST * a // 128 * 128
        off = FAST * a - start
        while landed < min(start + 384, LON):
            i = cuts.index(landed)
            heights[i].wait()
            landed = cuts[i + 1]
        if start + 384 <= LON:
            v = x_ref[:, start : start + 384].astype(F32)
        else:
            v = jnp.concatenate(
                [x_ref[:, start:LON].astype(F32), jnp.zeros((CYC, start + 384 - LON), F32)], 1
            )
        if off:
            v = pltpu.roll(v, 384 - off, 1)
        v = jnp.where(inside, v[:, :256], 0.0)
        for lane in range(2):
            xs.at[lane][pl.ds(a, CYC, stride=192), :] = v[:, lane * 128 : lane * 128 + 128]

    first = lax.broadcasted_iota(jnp.int32, (48, 128), 1) < 64

    def one_cycle(r, carry):
        rows = pl.ds(pl.multiple_of(r * 192, 192), 192)
        level = jnp.concatenate([xs[0, rows, :], xs[1, rows, :]], 1)
        value = level
        stack = []
        tc, tsin = twist_ref[0], twist_ref[1]
        for p in range(3):
            if p:
                value = value * level
            if p == 0:
                high = value.astype(BF16)
                y = dot(fh_ref[...], high) + dot(fl_ref[...], high)
            else:
                high, low = halves(value)
                y = dot(fh_ref[...], high) + dot(fl_ref[...], high) + dot(fh_ref[...], low)
            re, im = y[:HALF], y[HALF:]
            stack += list(halves(jnp.concatenate([re * tc + im * tsin, im * tc - re * tsin], 1)))
        o = dot(jnp.concatenate(stack, 0), second_ref[...])
        for p in range(3):
            both = o[p * 192 : p * 192 + HALF] + o[p * 192 + HALF : p * 192 + 192]
            for c in range(2):
                part = both[:, c * 128 : c * 128 + 128]
                part = part + pltpu.roll(part, 64, 1)
                qs[pl.ds(r * 8 + c * 3 + p, 48, stride=128), :] = jnp.where(first, part[:48], part[48:])
        return carry

    for i in range(4):
        table_copy(i).wait()
    loop(0, 16, lambda d: panel_copy(d).start())
    lax.fori_loop(0, CYC, one_cycle, 0, unroll=4)

    def one_k(k, carry):
        t = qs[pl.ds(k * 128 if isinstance(k, int) else pl.multiple_of(k * 128, 128), 128), :].T
        ts[pl.ds(k + FIRST - 1, 32, stride=SLOW), :] = t[0:32]
        ts[pl.ds(SLOW - k + FIRST - 1, 32, stride=SLOW), :] = t[32:64]
        return t

    def two_k(k, carry):
        t = one_k(k, carry)
        ts[pl.ds(k + 48 + FIRST - 1, 32, stride=SLOW), :] = t[64:96]
        ts[pl.ds(SLOW - 48 - k + FIRST - 1, 32, stride=SLOW), :] = t[96:128]
        return carry

    lax.fori_loop(0, 40, two_k, 0, unroll=4)
    for k in range(40, 43):
        two_k(k, 0)
    for k in range(43, 48):
        one_k(k, 0)

    pl.semaphore_wait(barrier, 22)

    sub = lax.broadcasted_iota(jnp.int32, (8, 128), 0)

    orders = ts.at[pl.ds(FIRST, ORDERS)]

    def chip_of(i):
        far = 7 - i // 2 - i % 2 * 4
        return far, (hy + far // 4) % 2 * 4 + (hz + far % 4) % 4

    def gathered(j, starts):
        for i in range(0, 128, 32):
            at = starts[i // 64] + i % 64
            rows = [orders[pl.ds(slot_ref[at + e], 1), :] for e in range(32)]
            for e in range(32):
                gs[j, i + e : i + e + 1, :] = rows[e]
        t = gs[j].T
        sides = [swap_chunks([t[(h * 8 + r) * 8 : (h * 8 + r + 1) * 8] for r in range(8)]) for h in range(2)]
        blocks = []
        for u in (0, 4):
            packed = [
                jnp.concatenate(
                    [jnp.where(sub < 6, side[u + v], pltpu.roll(side[u + 3], 6 - 2 * v, 0)) for v in range(3)], 1
                )
                for side in sides
            ]
            blocks.append(jnp.concatenate(packed, 0).astype(BF16))
        return blocks

    def send(T, far):
        @pl.when(far > 0)
        def _():
            in_copy(T, far * 2).start()

        in_copy(T, far * 2 + 1).start()

    for T in range(2):
        def two_chips(step, carry):
            for e in range(2):
                far, chip = chip_of(step * 2 + e)
                for j in range(2):
                    to = chip * 2 + j
                    start = to * 320 + T * 128
                    blocks = gathered(e * 2 + j, (start, start + 64))
                    msg_ref[pl.ds(pl.multiple_of(to * ROWS_IN + T * 32, 16), 32), :] = jnp.concatenate(blocks, 0)
                send(T, far)
            return carry

        lax.fori_loop(0, 4, two_chips, 0)

    def four_chips(step, carry):
        for e in range(4):
            far, chip = chip_of(step * 4 + e)
            start = chip * 640 + 256
            for j, block in enumerate(gathered(e, (start, start + 320))):
                msg_ref[pl.ds(pl.multiple_of((chip * 2 + j) * ROWS_IN + 64, 16), 16), :] = block
            send(2, far)
        return carry

    lax.fori_loop(0, 2, four_chips, 0)
    own_in = pl.ds(pl.multiple_of(me * ROWS_IN, 16), ROWS_IN)
    got[own_in, :] = msg_ref[own_in, :]
    loop(0, 16, lambda d: panel_copy(d).wait())
    def contract(q):
        sums = []
        for pair in range(2):
            accs = [None, None]
            for peer in range(16):
                rows = got[pl.ds(pl.multiple_of(q * 16 + peer * ROWS_IN, 16), 16), :].astype(F32)
                for e in range(2):
                    v = pair * 2 + e
                    sides = []
                    for h in (0, 8):
                        if v < 3:
                            sides.append(rows[h : h + 8, v * 128 : v * 128 + 128])
                        else:
                            x, y, z = (
                                pltpu.roll(rows[h : h + 8, w * 128 : w * 128 + 128], 2 + 2 * w, 0) for w in range(3)
                            )
                            sides.append(jnp.where(sub < 2, x, jnp.where(sub < 4, y, z)))
                    one = jnp.concatenate(sides, 1)
                    two = jnp.concatenate([one, one], 0).astype(BF16)
                    left = jnp.concatenate([two] * 8, 0) * diag_ref[...]
                    right = pan[
                        peer * 16 : peer * 16 + 16, pl.ds(pl.multiple_of(q * 64 + v * 16, 16), 16), :
                    ].reshape(256, DEG)
                    t = dot(left, right)
                    accs[e] = t if accs[e] is None else accs[e] + t
            sums += accs
        return sums

    def sum_slots(T, q):
        for v, t in enumerate(contract(q)):
            rows = t.reshape(16, 8, DEG)
            for c in range(2):
                row = base[T] + c * 4 * share[T] + (q - 2 * T) * 64 + v * 16
                mine[pl.ds(pl.multiple_of(row, 16), 16), :] = jnp.sum(rows * factor_ref[c][None], axis=1)

    def analyse_part(T):
        loop(1, 16, lambda d: in_copy(T, d).wait_recv())
        loop(2 * T, min(2 * T + 2, 5), lambda q: sum_slots(T, q))
        loop(1, 8, lambda d: slab_copy(T, d).start())

    def total_part(T):
        size = share[T]
        own = pl.ds(pl.multiple_of(base[T] + lat * size, 16), size)
        total = mine[own, :]
        for d in range(1, 8):
            slab_copy(T, d).wait_recv()
            total = total + parts[pl.ds(pl.multiple_of(base[T] + (lat + 8 - d) % 8 * size, 16), size), :]
        coeff[own, :] = (total * keeps[T * 32 : T * 32 + size, :]).astype(BF16)
        loop(1, 8, lambda d: coeff_copy(T, d).start())

    chunk = lax.broadcasted_iota(jnp.int32, (DEG, 128), 1) // 16

    def synthesis_part(T):
        groups = share[T] // 4
        loop(1, 8, lambda d: coeff_copy(T, d).wait_recv())
        for c in range(2):
            rows = coeff[base[T] + c * groups * 16 : base[T] + (c + 1) * groups * 16, :].astype(F32)
            if groups < 8:
                rows = jnp.concatenate([rows, jnp.zeros((128 - groups * 16, DEG), F32)], 0)
            turned = rows.T
            for g in range(groups):
                wide[g * DEG : g * DEG + DEG, c * 128 : c * 128 + 128] = jnp.where(
                    chunk == g, turned, 0.0
                ).astype(BF16)

        def two_peers(d, refs):
            left = jnp.concatenate(
                [
                    jnp.concatenate(
                        [
                            pan[
                                pl.ds(pl.multiple_of(ahead(d + e) * 16, 16), 16),
                                T * 128 + g * 16 : T * 128 + g * 16 + 16, :
                            ].reshape(256, DEG)
                            for g in range(groups)
                        ],
                        1,
                    )
                    for e in range(2)
                ],
                0,
            )
            o = dot(left, wide[: groups * DEG, :]).reshape(32, 16, 256)
            o = jnp.sum(o * pick_ref[...][None], axis=1)
            for e in range(2):
                place = pl.ds(pl.multiple_of(ahead(d + e) * ROWS_OUT + T * 16, 16), 16)
                refs[e][place, :] = o[e * 16 : e * 16 + 16].astype(BF16)

        def leaving(i):
            d = 16 - 2 * i
            two_peers(d, (syn, syn))
            out_copy(T, d).start()
            out_copy(T, d + 1).start()

        loop(1, 8, leaving)
        two_peers(0, (out_ref, syn))
        out_copy(T, 1).start()

    analyse_part(0)
    analyse_part(1)
    total_part(0)
    analyse_part(2)
    total_part(1)
    synthesis_part(0)
    total_part(2)
    synthesis_part(1)
    synthesis_part(2)
    for T in range(3):
        loop(1, 16, lambda d: in_copy(T, d).wait_send())
        loop(1, 16, lambda d: out_copy(T, d).wait())

        def finish_lat(d):
            slab_copy(T, d).wait_send()
            coeff_copy(T, d).wait_send()

        loop(1, 8, finish_lat)


def main(heights, slots, cutoffs, panels, factors):
    t = tables()
    dma = pltpu.SemaphoreType.DMA
    vec = pltpu.VMEM
    hbm = pl.BlockSpec(memory_space=pl.ANY)
    return pl.pallas_call(
        main_kernel,
        out_shape=jax.ShapeDtypeStruct((16 * ROWS_OUT, 256), BF16),
        in_specs=[pl.BlockSpec(memory_space=pltpu.SMEM)] * 2 + [hbm] * 6 + [vmem()] * 3,
        out_specs=vmem(),
        scratch_shapes=[
            vec((CYC, LON), BF16),
            vec((192, 192), BF16),
            vec((192, 192), BF16),
            vec((2, HALF, 256), F32),
            vec((512, 256), BF16),
            vec((2, CYC * 192, 128), F32),
            vec((48 * 128, 128), F32),
            vec((TROWS, 128), F32),
            vec((4, 128, 128), F32),
            vec((16 * ROWS_IN, 384), BF16),
            vec((256, 320, DEG), BF16),
            vec((16 * ROWS_IN, 384), BF16),
            vec((640, DEG), F32),
            vec((640, DEG), F32),
            vec((640, DEG), BF16),
            vec((80, DEG), F32),
            vec((8 * DEG, 256), BF16),
            vec((16 * ROWS_OUT, 256), BF16),
            dma((4,)), dma((4,)), dma((16,)), dma((3, 16)), dma((3, 16)), dma((3, 8)), dma((3, 8)), dma((3, 8)), dma((3, 8)),
            dma((3, 16)), dma((3, 16)),
        ],
        compiler_params=pltpu.CompilerParams(
            vmem_limit_bytes=56 * MIB, collective_id=0, has_side_effects=True
        ),
        cost_estimate=pl.CostEstimate(flops=2 * 10**10, bytes_accessed=24 * 10**6, transcendentals=0),
        name="main",
    )(slots, cutoffs, heights, *t["first"], t["twist"], t["second"], panels, t["diag"], factors, t["pick"])


def inverse_kernel(slot_ref, msg_hbm, back_hbm, twist_hbm, lh_hbm, ll_hbm, out_hbm,
                   msg_ref, back_ref, twist_ref, lh_ref, ll_ref, out_ref, ts, ls, ys, tsem, osem, msem):
    held = ((back_hbm, back_ref), (twist_hbm, twist_ref), (lh_hbm, lh_ref), (ll_hbm, ll_ref))
    copies = [pltpu.make_async_copy(held[i][0], held[i][1], tsem.at[i]) for i in range(4)]
    pieces = [
        pltpu.make_async_copy(msg_hbm.at[i * 192 : i * 192 + 192], msg_ref.at[i * 192 : i * 192 + 192], msem.at[i])
        for i in range(4)
    ]
    for copy in pieces + copies:
        copy.start()
    ts[0:FIRST, :] = jnp.zeros((FIRST, 128), F32)
    ts[FIRST + ORDERS : TROWS, :] = jnp.zeros((TROWS - ORDERS - FIRST, 128), F32)
    orders = ts.at[pl.ds(FIRST, ORDERS)]

    def one_peer(o, carry):
        for part in range(3):
            rows = msg_ref[pl.ds(pl.multiple_of(o * 48 + part * 16, 16), 16), :].astype(F32)
            count = 128 if part < 2 else 64
            t = jnp.concatenate([rows[:, :128], rows[:, 128:]], 0).T
            base = o * 320 + part * 128
            for i in range(count):
                orders[pl.ds(slot_ref[base + i], 1), 0:32] = t[i : i + 1]
        return carry

    for i in range(4):
        pieces[i].wait()
        lax.fori_loop(4 * i, 4 * i + 4, one_peer, 0, unroll=2)

    def one_k(k, carry):
        stack = []
        for base in (0, 48):
            plus = ts[pl.ds(k + base + FIRST - 1, 32, stride=SLOW), :]
            minus = ts[pl.ds(SLOW - base - k + FIRST - 1, 32, stride=SLOW), :]
            lone = k == 0 if base == 0 else k == 90 - base
            stack += [plus, jnp.where(lone, 0.0, minus)]
        ls[pl.ds(k, 32, stride=48), :] = jnp.concatenate(stack, 0)[:, :32].T
        return carry

    lax.fori_loop(0, 48, one_k, 0, unroll=4)
    first = lax.broadcasted_iota(jnp.int32, (48, 128), 1) < 64

    def four_cycles(step, carry):
        lefts = []
        for i in range(4):
            r = step * 4 + i
            l0 = ls[pl.ds(pl.multiple_of(r * 48, 48), 48), :]
            l1 = ls[pl.ds(pl.multiple_of((r + CYC) * 48, 48), 48), :]
            lefts += [jnp.where(first, l0, pltpu.roll(l1, 64, 1)), jnp.where(first, pltpu.roll(l0, 64, 1), l1)]
        left = jnp.concatenate(lefts, 0).astype(BF16)
        w = dot(jnp.concatenate([left, left], 1), back_ref[...])
        c, s = twist_ref[0], twist_ref[1]
        for i in range(4):
            re, im = w[i * HALF : i * HALF + HALF, :256], w[i * HALF : i * HALF + HALF, 256:]
            v = jnp.concatenate([re * c - im * s, im * c + re * s], 0).astype(BF16)
            field = dot(lh_ref[...], v) + dot(ll_ref[...], v)
            for lane in range(2):
                ys[lane, pl.ds(pl.multiple_of((step * 4 + i) * 192, 192), 192), :] = field[
                    :, lane * 128 : lane * 128 + 128
                ]
        return carry

    for copy in copies:
        copy.wait()
    lax.fori_loop(0, 4, four_cycles, 0, unroll=2)
    leaving = []
    for a in range(SLOW):
        v = jnp.concatenate([ys.at[lane][pl.ds(a, CYC, stride=192), :] for lane in range(2)], 1)
        out_ref[:, FAST * a : FAST * a + FAST] = v[:, :FAST]
        if a % 48 == 47 or a == SLOW - 1:
            place = slice(FAST * (a // 48 * 48), FAST * a + FAST)
            leaving.append(pltpu.make_async_copy(out_ref.at[:, place], out_hbm.at[:, place], osem.at[a // 48]))
            leaving[-1].start()
    for copy in leaving:
        copy.wait()


def inverse(msg, slots):
    t = tables()
    return pl.pallas_call(
        inverse_kernel,
        out_shape=jax.ShapeDtypeStruct((CYC, LON), F32),
        in_specs=[pl.BlockSpec(memory_space=pltpu.SMEM)] + [pl.BlockSpec(memory_space=pl.ANY)] * 5,
        out_specs=pl.BlockSpec(memory_space=pl.ANY),
        scratch_shapes=[
            pltpu.VMEM((16 * ROWS_OUT, 256), BF16),
            pltpu.VMEM((256, 512), BF16),
            pltpu.VMEM((2, HALF, 256), F32),
            pltpu.VMEM((192, 192), BF16),
            pltpu.VMEM((192, 192), BF16),
            pltpu.VMEM((CYC, LON), F32),
            pltpu.VMEM((TROWS, 128), F32),
            pltpu.VMEM((32 * 48, 128), F32),
            pltpu.VMEM((2, CYC * 192, 128), F32),
            pltpu.SemaphoreType.DMA((4,)),
            pltpu.SemaphoreType.DMA((4,)),
            pltpu.SemaphoreType.DMA((4,)),
        ],
        compiler_params=pltpu.CompilerParams(vmem_limit_bytes=62 * MIB),
        name="inverse",
    )(slots, msg, t["back"], t["twist"], *t["last"])


def degrees():
    stride = (NMAX - ORDERS) // DEG
    return ORDERS + np.arange(DEG, dtype=np.int32) * stride


def factor_rows():
    degree = degrees().astype(np.float64)
    rows = np.zeros((2, 8, DEG), np.float32)
    for c in range(2):
        rows[c, 3 * c] = 1.0
        rows[c, 3 * c + 1] = (degree + 2.0) / (2.0 * NMAX)
        rows[c, 3 * c + 2] = (degree + 2.0) * (degree + 1.0) / (6.0 * NMAX * NMAX)
    return rows


def local(heights, panels, ord_slot, cutoffs):
    back = main(heights, ord_slot, cutoffs, panels, factor_rows())
    return inverse(back, ord_slot)


def solution(mesh):
    return jax.shard_map(
        local,
        mesh=mesh,
        in_specs=(P(("lat", "ord"), None), P("lat", "ord", None), P(), P("ord")),
        out_specs=P(("lat", "ord"), None),
        check_vma=False,
    )
```
